32 devices in a mesh: tm: 4 (over y, x), line: 8 (over z, core).
Axes of the slice: x: 2, y: 2, z: 4, core: 2. Of those that a mesh axis runs over, the one named last changes fastest.
Arguments:
- station_traces: bfloat16 [256, 16384], P('line', 'tm'), may hold values from -6 to 6
- shot_onset_ticks: int32 [64], P('line'), may hold values from 0 to 16383, as said below
- span_place_index: int32 [64], P('line'), may hold values from 0 to 31, as said below
- spectral_keep_flags: int32 [64, 512], replicated, may hold values 0 or 1
Outputs:
- deblended: bfloat16 [128, 256, 1024], P('tm', 'line')
The draws below stay inside these ranges and needn't reach their ends.
Inputs may be any that keep to these rules, and one draw needn't show every extreme that they name: The block of 4096 samples holding shot_onset_ticks[s] owns shot s; each block owns at most 32 shots and one owns exactly 32. `span_place_index`: shots owned by the same block have distinct slots.
All inputs are finite; a program needn't handle non-finite values.
Results may differ from the reference program's by a relative error of at most 0.0078.
Values may be sent and summed in bfloat16 or wider, within the bound.
No kernel may reach another device: no remote copies, remote signals or barrier semaphores. Data moves between devices by JAX's collectives and lax.ppermute only.
A program may use at most 64 MiB of HBM per device.

```python
import math
import jax
import jax.numpy as jnp
from jax import lax

SPAN_TICKS = 1024
FREQ = 512
BATCH_TICKS = 4096
REC_DEV = 32
SLOTS = 32
NSHOT = 64
NREC = 256
SAMPLES = 16384
N_TM = 4
N_LINE = 8


def shot_plan(key):
    base = jax.random.fold_in(key, 11)
    key_busy, key_order, key_offset = jax.random.split(base, 3)
    busiest = jax.random.randint(key_busy, (), 0, N_TM)
    ranks = jax.random.permutation(key_order, NSHOT).astype(jnp.int32)
    others = jnp.maximum(ranks - SLOTS, 0)
    heavy = ranks < SLOTS
    span_holders = jnp.where(heavy, busiest, (busiest + 1 + others % (N_TM - 1)) % N_TM)
    slots = jnp.where(heavy, ranks, others // (N_TM - 1))
    offsets = jax.random.randint(key_offset, (NSHOT,), 0, BATCH_TICKS)
    return ((span_holders * BATCH_TICKS + offsets).astype(jnp.int32), slots.astype(jnp.int32))


def draw_shot_onset_ticks(key, part):
    return shot_plan(key)[0]


def draw_span_place_index(key, part):
    return shot_plan(key)[1]


def touch_ends(entries, rng, least, largest):
    longest = entries.shape.index(max(entries.shape))
    spots = []
    for shift in (0, 1):
        where = [jax.random.randint(jax.random.fold_in(rng, axis), (), 0, length) for axis, length in enumerate(entries.shape)]
        where[longest] = (where[longest] + shift) % entries.shape[longest]
        spots.append(tuple(where))
    return entries.at[spots[0]].set(least).at[spots[1]].set(largest)


def block_levels(rng, shape, cuts, smallest, high):
    gain, own = 1.0, jax.random.fold_in(rng, 6)
    for position, shards_of in cuts:
        heights = jnp.exp(jax.random.uniform(jax.random.fold_in(own, position), (shards_of,), jnp.float32, smallest / len(cuts), high / len(cuts)))
        gain = gain * jnp.repeat(heights, shape[position] // shards_of).reshape([-1 if axis == position else 1 for axis in range(len(shape))])
    return gain


def scatter_about(rng, extent, deviation, most, pieces=(), kind=jnp.bfloat16):
    values = deviation * jax.random.normal(rng, extent, jnp.float32)
    if pieces:
        values = values * block_levels(rng, extent, pieces, -0.22, 0.18)
    return jnp.clip(values, -most, most).astype(kind)


def setup_inputs(seed: int = 0) -> dict:
    keys = jax.random.split(jax.random.key(seed), 5)
    return {
        "station_traces": scatter_about(keys[0], (NREC, SAMPLES), 1.0, 6.0, ((0, 8), (1, 4))),
        "shot_onset_ticks": draw_shot_onset_ticks(jax.random.fold_in(keys[4], 71), 0),
        "span_place_index": draw_span_place_index(jax.random.fold_in(keys[4], 71), 0),
        "spectral_keep_flags": touch_ends((jax.random.randint(keys[3], (NSHOT, FREQ), 0, 4) < 3).astype(jnp.int32), jax.random.fold_in(keys[3], 1), 0, 1),
    }


def make_tables(window, shots):
    times = jnp.arange(window, dtype=jnp.int32)
    freqs = jnp.arange(window // 2, dtype=jnp.int32)
    phase = ((times[:, None] * freqs[None, :]) % window).astype(jnp.float32) * (2.0 * math.pi / window)
    cosine = jnp.cos(phase)
    sine = jnp.sin(phase)
    forward = jnp.concatenate([cosine, -sine], axis=1).astype(jnp.bfloat16)
    halves = jnp.where(freqs == 0, 0.5, 1.0).astype(jnp.float32)[:, None]
    inverse = jnp.concatenate([halves * cosine.T, -halves * sine.T], axis=0).astype(jnp.bfloat16)
    order = jnp.arange(shots, dtype=jnp.int32)
    turn = ((order[:, None] * order[None, :]) % shots).astype(jnp.float32) * (2.0 * math.pi / shots)
    return forward, inverse, jnp.cos(turn).astype(jnp.bfloat16), jnp.sin(turn).astype(jnp.bfloat16)


def filter_gathers(station_panels, keep_mask, tables):
    forward, inverse, shot_cos, shot_sin = tables
    shots, count_here, window = station_panels.shape
    freqs = window // 2
    spectrum = jnp.dot(station_panels.reshape(shots * count_here, window), forward, preferred_element_type=jnp.float32)
    spectrum = spectrum.astype(jnp.bfloat16).reshape(shots, count_here * window)
    cos_part = jnp.dot(shot_cos, spectrum, preferred_element_type=jnp.float32).reshape(shots, count_here, 2, freqs)
    sin_part = jnp.dot(shot_sin, spectrum, preferred_element_type=jnp.float32).reshape(shots, count_here, 2, freqs)
    sign_pair = jnp.array([1.0, -1.0], dtype=jnp.float32)[:, None]
    masked = (cos_part + sin_part[:, :, ::-1, :] * sign_pair) * keep_mask[:, None, None, :]
    masked = masked.astype(jnp.bfloat16).reshape(shots, count_here * window)
    cos_back = jnp.dot(shot_cos, masked, preferred_element_type=jnp.float32).reshape(shots, count_here, 2, freqs)
    sin_back = jnp.dot(shot_sin, masked, preferred_element_type=jnp.float32).reshape(shots, count_here, 2, freqs)
    mixed = (cos_back - sin_back[:, :, ::-1, :] * sign_pair).astype(jnp.bfloat16).reshape(shots * count_here, window)
    filtered = jnp.dot(mixed, inverse, preferred_element_type=jnp.float32) * (2.0 / (window * shots))
    return filtered.astype(jnp.bfloat16).reshape(shots, count_here, window)


def reference(station_traces, shot_onset_ticks, span_place_index, spectral_keep_flags):
    tables = make_tables(SPAN_TICKS, NSHOT)
    keep_mask = spectral_keep_flags.astype(jnp.float32)
    span_holders = shot_onset_ticks // BATCH_TICKS
    slot_code = span_holders * SLOTS + span_place_index
    all_codes = jnp.arange(N_TM * SLOTS, dtype=jnp.int32)
    matched = slot_code[:, None] == all_codes[None, :]
    sources = jnp.arange(NSHOT, dtype=jnp.int32)
    summed = jnp.sum(jnp.where(matched, sources[:, None], 0), axis=0)
    slot_source = jnp.where(jnp.any(matched, axis=0), summed, NSHOT).astype(jnp.int32)
    padded = jnp.pad(station_traces, ((0, 0), (0, SPAN_TICKS)))

    def one_block(block_index, result):
        trace_batch = lax.dynamic_slice_in_dim(padded, block_index * REC_DEV, REC_DEV, 0)
        station_panels = jax.vmap(lambda first_tick_shift: lax.dynamic_slice_in_dim(trace_batch, first_tick_shift, SPAN_TICKS, 1))(shot_onset_ticks)
        filtered = filter_gathers(station_panels, keep_mask, tables)
        slotted = jnp.take(filtered, slot_source, axis=0, mode="fill", fill_value=0)
        return lax.dynamic_update_slice_in_dim(result, slotted, block_index * REC_DEV, 1)

    empty_out = jnp.zeros((N_TM * SLOTS, NREC, SPAN_TICKS), jnp.bfloat16)
    return lax.fori_loop(0, N_LINE, one_block, empty_out)
```

```python
import functools
import math

import jax
import jax.numpy as jnp
import ml_dtypes
import numpy as np
from jax import lax
from jax.experimental import pallas as pl
from jax.experimental.pallas import tpu as pltpu
from jax.sharding import PartitionSpec as P

LANES = 128
RECS = 16


def make_tables(window, shots):
    half = window // 2
    quarter = half // 2
    times = np.arange(half)
    freqs = np.concatenate([np.arange(0, half, 2), np.arange(1, half, 2)])

    def waves(rows, columns, period):
        phase = (rows[:, None] * columns[None, :] % period) * (2.0 * math.pi / period)
        return np.cos(phase), np.sin(phase)

    bf16 = ml_dtypes.bfloat16
    cosine, sine = waves(times, freqs, window)
    forward = np.stack(
        [
            np.concatenate([cosine[:, cut], -sine[:, cut]], axis=1)
            for cut in (slice(0, quarter), slice(quarter, half))
        ]
    ).astype(bf16)
    gain = np.where(freqs == 0, 0.5, 1.0)[:, None] * (2.0 / (window * shots))
    inverse = np.stack(
        [
            np.concatenate([gain[cut] * cosine.T[cut], -gain[cut] * sine.T[cut]], axis=0)
            for cut in (slice(0, quarter), slice(quarter, half))
        ]
    ).astype(bf16)
    turn_cos, turn_sin = waves(np.arange(shots), np.arange(shots), shots)
    over_shots = np.block([[turn_cos, turn_sin], [-turn_sin, turn_cos]]).astype(bf16)
    back_rows = np.stack(
        [
            np.concatenate([turn_cos, -turn_sin], axis=1),
            np.concatenate([turn_sin, turn_cos], axis=1),
        ]
    ).astype(bf16)
    shift_cos, shift_sin = waves(np.arange(LANES), freqs, window)
    shifts = np.concatenate([shift_cos, shift_sin], axis=1)
    high = shifts.astype(bf16)
    low = (shifts - high.astype(np.float64)).astype(bf16)
    order = np.zeros((half, half), bf16)
    order[freqs, np.arange(half)] = 1
    return forward, inverse, over_shots, back_rows, np.stack([high, low]), order


def gather_kernel(
    ticks,
    places,
    here,
    traces,
    keep,
    forward,
    inverse,
    over_shots,
    back_rows,
    shifts,
    out,
    tiles,
    folds,
    spectra,
    turns,
    back,
    mixed,
):
    peers, recs, block_len = traces.shape
    shots, half = keep.shape
    window = 2 * half
    quarter = half // 2
    slots = out.shape[0]
    wide = window // LANES
    mid = wide // 2
    per_block = block_len // LANES
    f32, bf16 = jnp.float32, jnp.bfloat16

    for peer in range(peers):
        for tile in range(per_block):
            tiles[peer * per_block + tile] = traces[peer, :, tile * LANES : (tile + 1) * LANES]
    for tile in range(wide):
        tiles[peers * per_block + tile] = jnp.zeros((recs, LANES), bf16)

    lane = lax.broadcasted_iota(jnp.int32, (recs, LANES), 1)

    def cut(shot, carry):
        tick = ticks[shot]
        first = tick // LANES
        within = tick % LANES
        piece = [tiles[first + tile] for tile in range(wide)]
        last = tiles[first + wide]
        piece[0] = jnp.where(lane < within, last.astype(f32), piece[0].astype(f32)).astype(bf16)
        row = pl.multiple_of(shot * recs, recs)
        for tile in range(mid):
            at = slice(tile * LANES, (tile + 1) * LANES)
            folds[0, pl.ds(row, recs), at] = piece[tile] + piece[tile + mid]
            folds[1, pl.ds(row, recs), at] = piece[tile] - piece[tile + mid]
        return carry

    lax.fori_loop(0, shots, cut, 0, unroll=8)

    shot_row = lax.broadcasted_iota(jnp.int32, (shots, LANES), 0)
    shot_lane = lax.broadcasted_iota(jnp.int32, (1, shots), 1)
    within_all = jnp.zeros((shots, LANES), jnp.int32)
    place_all = jnp.full((1, shots), -1, jnp.int32)
    for shot in range(shots):
        tick = ticks[shot]
        within_all = jnp.where(shot_row == shot, tick % LANES, within_all)
        place = jnp.where(tick // block_len == here[0], places[shot], -1)
        place_all = jnp.where(shot_lane == shot, place, place_all)
    shift_lane = lax.broadcasted_iota(jnp.int32, (shots, LANES), 1)
    picks = (within_all == shift_lane).astype(f32).astype(bf16)
    turns[...] = jnp.dot(picks, shifts[0], preferred_element_type=f32) + jnp.dot(
        picks, shifts[1], preferred_element_type=f32
    )
    slot_row = lax.broadcasted_iota(jnp.int32, (slots, shots), 0)
    owned = (slot_row == place_all).astype(f32).astype(bf16)
    for part in range(2):
        back[part * slots : (part + 1) * slots] = jnp.dot(
            owned, back_rows[part], preferred_element_type=f32
        ).astype(bf16)

    rows = shots * recs
    step = min(rows, 256)
    for part in range(2):
        for row in range(0, rows, step):
            found = jnp.dot(
                folds[part, row : row + step], forward[part], preferred_element_type=f32
            )
            for tile in range(mid):
                spectra[part * mid + tile, row : row + step] = found[
                    :, tile * LANES : (tile + 1) * LANES
                ]

    arms = mid // 2
    for rec in range(recs):
        real, imag = [], []
        for tile in range(mid):
            part, arm = tile // arms, tile % arms
            at = slice(tile * LANES, (tile + 1) * LANES)
            cos_turn = turns[:, at]
            sin_turn = turns[:, half + tile * LANES : half + (tile + 1) * LANES]
            cos_part = spectra[part * mid + arm, pl.ds(rec, shots, stride=recs), :]
            sin_part = spectra[part * mid + arms + arm, pl.ds(rec, shots, stride=recs), :]
            real.append((cos_part * cos_turn - sin_part * sin_turn).astype(bf16))
            imag.append((cos_part * sin_turn + sin_part * cos_turn).astype(bf16))
        stacked = jnp.concatenate(
            [jnp.concatenate(real, axis=1), jnp.concatenate(imag, axis=1)], axis=0
        )
        waves = jnp.dot(over_shots[...], stacked, preferred_element_type=f32)
        masked = jnp.concatenate(
            [waves[:shots] * keep[...], waves[shots:] * keep[...]], axis=0
        ).astype(bf16)
        again = jnp.dot(back[...], masked, preferred_element_type=f32)
        for tile in range(mid):
            part, arm = tile // arms, tile % arms
            at = slice(tile * LANES, (tile + 1) * LANES)
            to = pl.ds(rec, slots, stride=recs)
            mixed[part * mid + arm, to, :] = again[:slots, at]
            mixed[part * mid + arms + arm, to, :] = again[slots:, at]

    group = max(1, min(slots, 256 // recs))
    for slot in range(0, slots, group):
        at = slice(slot * recs, (slot + group) * recs)
        even, odd = [
            jnp.dot(
                jnp.concatenate(
                    [mixed[part * mid + tile, at].astype(bf16) for tile in range(mid)], axis=1
                ),
                inverse[part],
                preferred_element_type=f32,
            )
            for part in range(2)
        ]
        out[slot : slot + group, :, :half] = (even + odd).reshape(group, recs, half).astype(bf16)
        out[slot : slot + group, :, half:] = (even - odd).reshape(group, recs, half).astype(bf16)


def filter_gathers(ticks, places, here, traces, keep, tables):
    forward, inverse, over_shots, back_rows, shifts = tables
    peers, rec_rows, block_len = traces.shape
    shots, half = keep.shape
    window = 2 * half
    slots = 2 * shots // peers
    recs = RECS
    total = peers * block_len
    smem = pl.BlockSpec(memory_space=pltpu.SMEM)

    def whole(array):
        return pl.BlockSpec(array.shape, lambda step: (0,) * array.ndim)

    sizes = (
        8 * peers * recs * block_len
        + 4 * 2 * 2 * shots * recs * half
        + 12 * shots * recs * half
        + 8 * slots * recs * window
        + 4 * slots * recs * window
        + 8 * (forward.size + inverse.size + over_shots.size + back_rows.size + shifts.size)
    )
    flops = 2 * rec_rows * (
        shots * window * half
        + slots * window * half
        + 4 * shots * shots * half
        + 4 * slots * shots * half
    )
    return pl.pallas_call(
        gather_kernel,
        grid=(rec_rows // recs,),
        out_shape=jax.ShapeDtypeStruct((slots, rec_rows, window), jnp.bfloat16),
        in_specs=[
            smem,
            smem,
            smem,
            pl.BlockSpec((peers, recs, block_len), lambda step: (0, step, 0)),
            whole(keep),
            whole(forward),
            whole(inverse),
            whole(over_shots),
            whole(back_rows),
            whole(shifts),
        ],
        out_specs=pl.BlockSpec((slots, recs, window), lambda step: (0, step, 0)),
        scratch_shapes=[
            pltpu.VMEM(((total + window) // LANES, recs, LANES), jnp.bfloat16),
            pltpu.VMEM((2, shots * recs, half), jnp.bfloat16),
            pltpu.VMEM((window // LANES, shots * recs, LANES), jnp.float32),
            pltpu.VMEM((shots, window), jnp.float32),
            pltpu.VMEM((2 * slots, 2 * shots), jnp.bfloat16),
            pltpu.VMEM((window // LANES, slots * recs, LANES), jnp.float32),
        ],
        compiler_params=pltpu.CompilerParams(vmem_limit_bytes=min(sizes + (12 << 20), 60 << 20)),
        cost_estimate=pl.CostEstimate(
            flops=flops, bytes_accessed=2 * (traces.size + slots * rec_rows * window), transcendentals=0
        ),
    )(ticks, places, here, traces, keep, forward, inverse, over_shots, back_rows, shifts)


def on_device(station_traces, shot_onset_ticks, span_place_index, spectral_keep_flags):
    shots, half = spectral_keep_flags.shape
    *tables, order = make_tables(2 * half, shots)
    traces = lax.all_gather(station_traces, "tm", axis=0)
    ticks = lax.all_gather(shot_onset_ticks, "line", axis=0, tiled=True)
    places = lax.all_gather(span_place_index, "line", axis=0, tiled=True)
    here = lax.axis_index("tm").astype(jnp.int32).reshape(1)
    keep = jnp.dot(
        spectral_keep_flags.astype(jnp.bfloat16), order, preferred_element_type=jnp.float32
    )
    return filter_gathers(ticks, places, here, traces, keep, tables)


def solution(mesh):
    in_specs = (P("line", "tm"), P("line"), P("line"), P())
    out_specs = P("tm", "line", None)
    return jax.shard_map(
        on_device, mesh=mesh, in_specs=in_specs, out_specs=out_specs, check_vma=False
    )
```

```python
import functools
import math

import jax
import jax.numpy as jnp
import ml_dtypes
import numpy as np
from jax import lax
from jax.experimental import pallas as pl
from jax.experimental.pallas import tpu as pltpu
from jax.sharding import PartitionSpec as P

LANES = 128
RECS = 16


def make_tables(window, shots):
    half = window // 2
    quarter = half // 2
    times = np.arange(half)
    freqs = np.concatenate([np.arange(0, half, 2), np.arange(1, half, 2)])

    def waves(rows, columns, period):
        phase = (rows[:, None] * columns[None, :] % period) * (2.0 * math.pi / period)
        return np.cos(phase), np.sin(phase)

    bf16 = ml_dtypes.bfloat16
    cosine, sine = waves(times, freqs, window)
    forward = np.stack(
        [
            np.concatenate([cosine[:, cut], -sine[:, cut]], axis=1)
            for cut in (slice(0, quarter), slice(quarter, half))
        ]
    ).astype(bf16)
    gain = np.where(freqs == 0, 0.5, 1.0)[:, None] * (2.0 / (window * shots))
    inverse = np.stack(
        [
            np.concatenate([gain[cut] * cosine.T[cut], -gain[cut] * sine.T[cut]], axis=0)
            for cut in (slice(0, quarter), slice(quarter, half))
        ]
    ).astype(bf16)
    turn_cos, turn_sin = waves(np.arange(shots), np.arange(shots), shots)
    over_shots = np.block([[turn_cos, turn_sin], [-turn_sin, turn_cos]]).astype(bf16)
    back_rows = np.stack(
        [
            np.concatenate([turn_cos, -turn_sin], axis=1),
            np.concatenate([turn_sin, turn_cos], axis=1),
        ]
    ).astype(bf16)
    shift_cos, shift_sin = waves(np.arange(LANES), freqs, window)
    shifts = np.concatenate([shift_cos, shift_sin], axis=1)
    high = shifts.astype(bf16)
    low = (shifts - high.astype(np.float64)).astype(bf16)
    order = np.zeros((half, half), bf16)
    order[freqs, np.arange(half)] = 1
    return forward, inverse, over_shots, back_rows, np.stack([high, low]), order


def gather_kernel(peers, chunk, *refs):
    ticks, places, here, *refs = refs
    traces, refs = refs[:peers], refs[peers:]
    keep, forward, inverse, over_shots, back_rows, shifts, *refs = refs
    out, tiles, folds, spectra, turns, back, mixed = refs[chunk > 0 :]
    recs, block_len = traces[-1].shape
    shots, half = keep.shape
    window = 2 * half
    quarter = half // 2
    slots = out.shape[0]
    wide = window // LANES
    mid = wide // 2
    per_block = block_len // LANES
    f32, bf16 = jnp.float32, jnp.bfloat16

    for away, block in enumerate(traces):
        base = partner(here[0], away, peers) * per_block
        for tile in range(per_block):
            tiles[base + tile] = block[:, tile * LANES : (tile + 1) * LANES]
    for tile in range(wide):
        tiles[peers * per_block + tile] = jnp.zeros((recs, LANES), bf16)

    lane = lax.broadcasted_iota(jnp.int32, (recs, LANES), 1)

    def cut(shot, carry):
        tick = ticks[shot]
        first = tick // LANES
        within = tick % LANES
        piece = [tiles[first + tile] for tile in range(wide)]
        last = tiles[first + wide]
        piece[0] = jnp.where(lane < within, last.astype(f32), piece[0].astype(f32)).astype(bf16)
        row = pl.multiple_of(shot * recs, recs)
        for tile in range(mid):
            at = slice(tile * LANES, (tile + 1) * LANES)
            folds[0, pl.ds(row, recs), at] = piece[tile] + piece[tile + mid]
            folds[1, pl.ds(row, recs), at] = piece[tile] - piece[tile + mid]
        return carry

    lax.fori_loop(0, shots, cut, 0, unroll=8)

    shot_row = lax.broadcasted_iota(jnp.int32, (shots, LANES), 0)
    shot_lane = lax.broadcasted_iota(jnp.int32, (1, shots), 1)
    within_all = jnp.zeros((shots, LANES), jnp.int32)
    place_all = jnp.full((1, shots), -1, jnp.int32)
    for shot in range(shots):
        tick = ticks[shot]
        within_all = jnp.where(shot_row == shot, tick % LANES, within_all)
        place = jnp.where(tick // block_len == here[0], places[shot], -1)
        place_all = jnp.where(shot_lane == shot, place, place_all)
    shift_lane = lax.broadcasted_iota(jnp.int32, (shots, LANES), 1)
    picks = (within_all == shift_lane).astype(f32).astype(bf16)
    turns[...] = jnp.dot(picks, shifts[0], preferred_element_type=f32) + jnp.dot(
        picks, shifts[1], preferred_element_type=f32
    )
    slot_row = lax.broadcasted_iota(jnp.int32, (slots, shots), 0)
    owned = (slot_row == place_all).astype(f32).astype(bf16)
    for part in range(2):
        back[part * slots : (part + 1) * slots] = jnp.dot(
            owned, back_rows[part], preferred_element_type=f32
        ).astype(bf16)

    rows = shots * recs
    step = min(rows, 256)
    for part in range(2):
        for row in range(0, rows, step):
            found = jnp.dot(
                folds[part, row : row + step], forward[part], preferred_element_type=f32
            )
            for tile in range(mid):
                spectra[part * mid + tile, row : row + step] = found[
                    :, tile * LANES : (tile + 1) * LANES
                ]

    arms = mid // 2
    for rec in range(recs):
        real, imag = [], []
        for tile in range(mid):
            part, arm = tile // arms, tile % arms
            at = slice(tile * LANES, (tile + 1) * LANES)
            cos_turn = turns[:, at]
            sin_turn = turns[:, half + tile * LANES : half + (tile + 1) * LANES]
            cos_part = spectra[part * mid + arm, pl.ds(rec, shots, stride=recs), :]
            sin_part = spectra[part * mid + arms + arm, pl.ds(rec, shots, stride=recs), :]
            real.append((cos_part * cos_turn - sin_part * sin_turn).astype(bf16))
            imag.append((cos_part * sin_turn + sin_part * cos_turn).astype(bf16))
        stacked = jnp.concatenate(
            [jnp.concatenate(real, axis=1), jnp.concatenate(imag, axis=1)], axis=0
        )
        waves = jnp.dot(over_shots[...], stacked, preferred_element_type=f32)
        masked = jnp.concatenate(
            [waves[:shots] * keep[...], waves[shots:] * keep[...]], axis=0
        ).astype(bf16)
        again = jnp.dot(back[...], masked, preferred_element_type=f32)
        for tile in range(mid):
            part, arm = tile // arms, tile % arms
            at = slice(tile * LANES, (tile + 1) * LANES)
            to = pl.ds(rec, slots, stride=recs)
            mixed[part * mid + arm, to, :] = again[:slots, at]
            mixed[part * mid + arms + arm, to, :] = again[slots:, at]

    group = max(1, min(slots, 256 // recs))
    for slot in range(0, slots, group):
        at = slice(slot * recs, (slot + group) * recs)
        even, odd = [
            jnp.dot(
                jnp.concatenate(
                    [mixed[part * mid + tile, at].astype(bf16) for tile in range(mid)], axis=1
                ),
                inverse[part],
                preferred_element_type=f32,
            )
            for part in range(2)
        ]
        out[slot : slot + group, :, :half] = (even + odd).reshape(group, recs, half).astype(bf16)
        out[slot : slot + group, :, half:] = (even - odd).reshape(group, recs, half).astype(bf16)


def partner(index, away, count):
    if count & (count - 1) == 0:
        return index ^ away
    return (index + away) % count


def filter_gathers(ticks, places, here, traces, keep, tables, chunk, chunks, filled):
    forward, inverse, over_shots, back_rows, shifts = tables
    peers = len(traces)
    recs, block_len = traces[-1].shape
    rec_rows = recs * chunks
    shots, half = keep.shape
    window = 2 * half
    slots = 2 * shots // peers
    total = peers * block_len
    smem = pl.BlockSpec(memory_space=pltpu.SMEM)
    shared = [keep, forward, inverse, over_shots, back_rows, shifts]

    def whole(array):
        return pl.BlockSpec(array.shape, lambda step: (0,) * array.ndim)

    flops = 2 * recs * (
        shots * window * half
        + slots * window * half
        + 4 * shots * shots * half
        + 4 * slots * shots * half
    )
    operands = [ticks, places, here, *traces, *shared]
    in_specs = [
        smem,
        smem,
        smem,
        pl.BlockSpec((recs, block_len), lambda step: (chunk, 0)),
        *[whole(block) for block in traces[1:]],
        *[whole(array) for array in shared],
    ]
    aliases = {}
    if chunk:
        aliases = {len(operands): 0}
        operands.append(filled)
        in_specs.append(pl.BlockSpec(memory_space=pl.ANY))
    return pl.pallas_call(
        functools.partial(gather_kernel, peers, chunk),
        grid=(1,),
        out_shape=jax.ShapeDtypeStruct((slots, rec_rows, window), jnp.bfloat16),
        in_specs=in_specs,
        out_specs=pl.BlockSpec((slots, recs, window), lambda step: (0, chunk, 0)),
        scratch_shapes=[
            pltpu.VMEM(((total + window) // LANES, recs, LANES), jnp.bfloat16),
            pltpu.VMEM((2, shots * recs, half), jnp.bfloat16),
            pltpu.VMEM((window // LANES, shots * recs, LANES), jnp.float32),
            pltpu.VMEM((shots, window), jnp.float32),
            pltpu.VMEM((2 * slots, 2 * shots), jnp.bfloat16),
            pltpu.VMEM((window // LANES, slots * recs, LANES), jnp.float32),
        ],
        input_output_aliases=aliases,
        compiler_params=pltpu.CompilerParams(vmem_limit_bytes=60 << 20),
        cost_estimate=pl.CostEstimate(
            flops=flops, bytes_accessed=2 * recs * (total + slots * window), transcendentals=0
        ),
    )(*operands)


def on_device(station_traces, shot_onset_ticks, span_place_index, spectral_keep_flags):
    shots, half = spectral_keep_flags.shape
    *tables, order = make_tables(2 * half, shots)
    peers = lax.axis_size("tm")
    chunks = station_traces.shape[0] // RECS
    gathered = []
    for chunk in range(chunks):
        part = station_traces[chunk * RECS : (chunk + 1) * RECS]
        gathered.append(
            [station_traces]
            + [
                lax.ppermute(
                    part, "tm", [(partner(index, away, peers), index) for index in range(peers)]
                )
                for away in range(1, peers)
            ]
        )
    ticks = lax.all_gather(shot_onset_ticks, "line", axis=0, tiled=True)
    places = lax.all_gather(span_place_index, "line", axis=0, tiled=True)
    here = lax.axis_index("tm").astype(jnp.int32).reshape(1)
    keep = jnp.dot(
        spectral_keep_flags.astype(jnp.bfloat16), order, preferred_element_type=jnp.float32
    )
    filled = None
    for chunk in range(chunks):
        filled = filter_gathers(
            ticks, places, here, gathered[chunk], keep, tables, chunk, chunks, filled
        )
    return filled


def solution(mesh):
    in_specs = (P("line", "tm"), P("line"), P("line"), P())
    out_specs = P("tm", "line", None)
    return jax.shard_map(
        on_device, mesh=mesh, in_specs=in_specs, out_specs=out_specs, check_vma=False
    )
```

```python
import functools
import math

import jax
import jax.numpy as jnp
import ml_dtypes
import numpy as np
from jax import lax
from jax.experimental import pallas as pl
from jax.experimental.pallas import tpu as pltpu
from jax.sharding import PartitionSpec as P

LANES = 128
RECS = 16


def make_tables(window, shots):
    half = window // 2
    quarter = half // 2
    times = np.arange(half)
    freqs = np.concatenate([np.arange(0, half, 2), np.arange(1, half, 2)])

    def waves(rows, columns, period):
        phase = (rows[:, None] * columns[None, :] % period) * (2.0 * math.pi / period)
        return np.cos(phase), np.sin(phase)

    bf16 = ml_dtypes.bfloat16
    cosine, sine = waves(times, freqs, window)
    forward = np.stack(
        [
            np.concatenate([cosine[:, cut], -sine[:, cut]], axis=1)
            for cut in (slice(0, quarter), slice(quarter, half))
        ]
    ).astype(bf16)
    gain = np.where(freqs == 0, 0.5, 1.0)[:, None] * (2.0 / (window * shots))
    inverse = np.stack(
        [
            np.concatenate([gain[cut] * cosine.T[cut], -gain[cut] * sine.T[cut]], axis=0)
            for cut in (slice(0, quarter), slice(quarter, half))
        ]
    ).astype(bf16)
    turn_cos, turn_sin = waves(np.arange(shots), np.arange(shots), shots)
    over_shots = np.block([[turn_cos, turn_sin], [-turn_sin, turn_cos]]).astype(bf16)
    back_rows = np.stack(
        [
            np.concatenate([turn_cos, -turn_sin], axis=1),
            np.concatenate([turn_sin, turn_cos], axis=1),
        ]
    ).astype(bf16)
    shift_cos, shift_sin = waves(np.arange(LANES), freqs, window)
    shifts = np.concatenate([shift_cos, shift_sin], axis=1)
    high = shifts.astype(bf16)
    low = (shifts - high.astype(np.float64)).astype(bf16)
    order = np.zeros((half, half), bf16)
    order[freqs, np.arange(half)] = 1
    return forward, inverse, over_shots, back_rows, np.stack([high, low]), order


def plan_kernel(peers, *refs):
    codes, refs = refs[:peers], refs[peers:]
    here, flags, order, back_rows, shifts, ticks, keep, turns, back = refs
    shots, half = flags.shape
    slots = back.shape[0] // 2
    share = shots // peers
    block_len = here[2]
    f32, bf16 = jnp.float32, jnp.bfloat16

    keep[...] = jnp.dot(flags[...].astype(f32).astype(bf16), order[...], preferred_element_type=f32)
    shot_row = lax.broadcasted_iota(jnp.int32, (shots, LANES), 0)
    shot_lane = lax.broadcasted_iota(jnp.int32, (1, shots), 1)
    within_all = jnp.zeros((shots, LANES), jnp.int32)
    place_all = jnp.full((1, shots), -1, jnp.int32)
    for away, block in enumerate(codes):
        base = partner(here[1], away, peers) * share
        for item in range(share):
            shot = base + item
            tick = block[item]
            ticks[shot] = tick
            within_all = jnp.where(shot_row == shot, tick % LANES, within_all)
            place = jnp.where(tick // block_len == here[0], block[share + item], -1)
            place_all = jnp.where(shot_lane == shot, place, place_all)
    shift_lane = lax.broadcasted_iota(jnp.int32, (shots, LANES), 1)
    picks = (within_all == shift_lane).astype(f32).astype(bf16)
    turns[...] = jnp.dot(picks, shifts[0], preferred_element_type=f32) + jnp.dot(
        picks, shifts[1], preferred_element_type=f32
    )
    slot_row = lax.broadcasted_iota(jnp.int32, (slots, shots), 0)
    owned = (slot_row == place_all).astype(f32).astype(bf16)
    for part in range(2):
        back[part * slots : (part + 1) * slots] = jnp.dot(
            owned, back_rows[part], preferred_element_type=f32
        ).astype(bf16)


def plan_shots(codes, here, flags, order, back_rows, shifts, slots):
    shots, half = flags.shape
    smem = pl.BlockSpec(memory_space=pltpu.SMEM)
    vmem = pl.BlockSpec(memory_space=pltpu.VMEM)
    return pl.pallas_call(
        functools.partial(plan_kernel, len(codes)),
        out_shape=[
            jax.ShapeDtypeStruct((shots,), jnp.int32),
            jax.ShapeDtypeStruct((shots, half), jnp.float32),
            jax.ShapeDtypeStruct((shots, 2 * half), jnp.float32),
            jax.ShapeDtypeStruct((2 * slots, 2 * shots), jnp.bfloat16),
        ],
        in_specs=[smem] * (len(codes) + 1) + [vmem] * 4,
        out_specs=[smem, vmem, vmem, vmem],
        compiler_params=pltpu.CompilerParams(vmem_limit_bytes=16 << 20),
        cost_estimate=pl.CostEstimate(
            flops=2 * shots * half * (half + 4 * LANES), bytes_accessed=2 << 20, transcendentals=0
        ),
    )(*codes, here, flags, order, back_rows, shifts)


def gather_kernel(peers, chunk, *refs):
    ticks, here, *refs = refs
    traces, refs = refs[:peers], refs[peers:]
    tables, refs = refs[:6], refs[6 + (chunk > 0) :]
    out, records, *refs = refs
    loaded, refs = refs[:6], refs[6:]
    tiles, folds, spectra, mixed, ready, record_sem, table_sem, out_sem = refs
    recs, block_len = records.shape[1:]
    keep, turns, back, over_shots, forward, inverse = loaded
    shots, half = keep.shape
    window = 2 * half
    slots = ready.shape[0]
    wide = window // LANES
    mid = wide // 2
    arms = mid // 2
    per_block = block_len // LANES
    f32, bf16 = jnp.float32, jnp.bfloat16
    rows_here = pl.ds(chunk * recs, recs)

    record_copies = [
        pltpu.make_async_copy(
            block.at[rows_here] if away == 0 else block, records.at[away], record_sem.at[away]
        )
        for away, block in enumerate(traces)
    ]
    table_copies = [
        pltpu.make_async_copy(table, place, table_sem.at[index])
        for index, (table, place) in enumerate(zip(tables, loaded))
    ]
    for copy in record_copies:
        copy.start()
    for index in (4, 1, 0, 2, 3, 5):
        table_copies[index].start()

    for away in range(peers):
        record_copies[away].wait()
        base = partner(here[0], away, peers) * per_block
        for tile in range(per_block):
            tiles[base + tile] = records[away, :, tile * LANES : (tile + 1) * LANES]
    for tile in range(wide):
        tiles[peers * per_block + tile] = jnp.zeros((recs, LANES), bf16)

    lane = lax.broadcasted_iota(jnp.int32, (recs, LANES), 1)

    def cut(shot, carry):
        tick = ticks[shot]
        first = tick // LANES
        within = tick % LANES
        piece = [tiles[first + tile] for tile in range(wide)]
        last = tiles[first + wide]
        piece[0] = jnp.where(lane < within, last.astype(f32), piece[0].astype(f32)).astype(bf16)
        row = pl.multiple_of(shot * recs, recs)
        for tile in range(mid):
            at = slice(tile * LANES, (tile + 1) * LANES)
            folds[0, pl.ds(row, recs), at] = piece[tile] + piece[tile + mid]
            folds[1, pl.ds(row, recs), at] = piece[tile] - piece[tile + mid]
        return carry

    lax.fori_loop(0, shots, cut, 0, unroll=8)

    table_copies[4].wait()
    rows = shots * recs
    step = min(rows, 256)
    for part in range(2):
        for row in range(0, rows, step):
            found = jnp.dot(
                folds[part, row : row + step], forward[part], preferred_element_type=f32
            )
            for tile in range(mid):
                spectra[part * mid + tile, row : row + step] = found[
                    :, tile * LANES : (tile + 1) * LANES
                ]

    for index in range(4):
        table_copies[index].wait()
    batch = 4
    for first in range(0, recs, batch):
        real, imag = [], []
        for rec in range(first, first + batch):
            for tile in range(mid):
                part, arm = tile // arms, tile % arms
                at = slice(tile * LANES, (tile + 1) * LANES)
                cos_turn = turns[:, at]
                sin_turn = turns[:, half + tile * LANES : half + (tile + 1) * LANES]
                cos_part = spectra[part * mid + arm, pl.ds(rec, shots, stride=recs), :]
                sin_part = spectra[part * mid + arms + arm, pl.ds(rec, shots, stride=recs), :]
                real.append((cos_part * cos_turn - sin_part * sin_turn).astype(bf16))
                imag.append((cos_part * sin_turn + sin_part * cos_turn).astype(bf16))
        stacked = jnp.concatenate(
            [jnp.concatenate(real, axis=1), jnp.concatenate(imag, axis=1)], axis=0
        )
        waves = jnp.dot(over_shots[...], stacked, preferred_element_type=f32)
        kept = jnp.concatenate([keep[...]] * batch, axis=1)
        masked = jnp.concatenate([waves[:shots] * kept, waves[shots:] * kept], axis=0).astype(bf16)
        again = jnp.dot(back[...], masked, preferred_element_type=f32)
        for rec in range(batch):
            to = pl.ds(first + rec, slots, stride=recs)
            for tile in range(mid):
                part, arm = tile // arms, tile % arms
                at = slice(rec * half + tile * LANES, rec * half + (tile + 1) * LANES)
                mixed[part * mid + arm, to, :] = again[:slots, at]
                mixed[part * mid + arms + arm, to, :] = again[slots:, at]

    table_copies[5].wait()
    group = max(1, min(slots, 256 // recs))
    out_copies = []
    for slot in range(0, slots, group):
        at = slice(slot * recs, (slot + group) * recs)
        even, odd = [
            jnp.dot(
                jnp.concatenate(
                    [mixed[part * mid + tile, at].astype(bf16) for tile in range(mid)], axis=1
                ),
                inverse[part],
                preferred_element_type=f32,
            )
            for part in range(2)
        ]
        ready[slot : slot + group, :, :half] = (even + odd).reshape(group, recs, half).astype(bf16)
        ready[slot : slot + group, :, half:] = (even - odd).reshape(group, recs, half).astype(bf16)
        copy = pltpu.make_async_copy(
            ready.at[pl.ds(slot, group)],
            out.at[pl.ds(slot, group), rows_here],
            out_sem.at[slot // group],
        )
        copy.start()
        out_copies.append(copy)
    for copy in out_copies:
        copy.wait()


def partner(index, away, count):
    if count & (count - 1) == 0:
        return index ^ away
    return (index + away) % count


def filter_gathers(ticks, here, traces, tables, chunk, chunks, filled):
    keep, turns, back, over_shots, forward, inverse = tables
    peers = len(traces)
    recs, block_len = traces[-1].shape
    rec_rows = recs * chunks
    shots, half = keep.shape
    window = 2 * half
    slots = 2 * shots // peers
    total = peers * block_len
    smem = pl.BlockSpec(memory_space=pltpu.SMEM)
    anywhere = pl.BlockSpec(memory_space=pl.ANY)
    flops = 2 * recs * (
        shots * window * half
        + slots * window * half
        + 4 * shots * shots * half
        + 4 * slots * shots * half
    )
    operands = [ticks, here, *traces, *tables]
    aliases = {}
    if chunk:
        aliases = {len(operands): 0}
        operands.append(filled)
    scratch = [
        pltpu.VMEM((peers, recs, block_len), jnp.bfloat16),
        *[pltpu.VMEM(table.shape, table.dtype) for table in tables],
        pltpu.VMEM(((total + window) // LANES, recs, LANES), jnp.bfloat16),
        pltpu.VMEM((2, shots * recs, half), jnp.bfloat16),
        pltpu.VMEM((window // LANES, shots * recs, LANES), jnp.float32),
        pltpu.VMEM((window // LANES, slots * recs, LANES), jnp.float32),
        pltpu.VMEM((slots, recs, window), jnp.bfloat16),
    ]
    size = sum(math.prod(ref.shape) * jnp.dtype(ref.dtype).itemsize for ref in scratch)
    return pl.pallas_call(
        functools.partial(gather_kernel, peers, chunk),
        out_shape=jax.ShapeDtypeStruct((slots, rec_rows, window), jnp.bfloat16),
        in_specs=[smem, smem] + [anywhere] * (len(operands) - 2),
        out_specs=anywhere,
        scratch_shapes=[
            *scratch,
            pltpu.SemaphoreType.DMA((peers,)),
            pltpu.SemaphoreType.DMA((len(tables),)),
            pltpu.SemaphoreType.DMA((slots,)),
        ],
        input_output_aliases=aliases,
        compiler_params=pltpu.CompilerParams(vmem_limit_bytes=min(size + (8 << 20), 60 << 20)),
        cost_estimate=pl.CostEstimate(
            flops=flops, bytes_accessed=2 * recs * (total + slots * window), transcendentals=0
        ),
    )(*operands)


def on_device(station_traces, shot_onset_ticks, span_place_index, spectral_keep_flags):
    shots, half = spectral_keep_flags.shape
    forward, inverse, over_shots, back_rows, shifts, order = make_tables(2 * half, shots)
    peers = lax.axis_size("tm")
    lines = lax.axis_size("line")
    chunks = station_traces.shape[0] // RECS
    slots = 2 * shots // peers

    def fetch(block, axis, count):
        return [
            lax.ppermute(
                block, axis, [(partner(index, away, count), index) for index in range(count)]
            )
            for away in range(1, count)
        ]

    gathered = [
        [station_traces, *fetch(station_traces[chunk * RECS : (chunk + 1) * RECS], "tm", peers)]
        for chunk in range(chunks)
    ]
    codes = jnp.concatenate([shot_onset_ticks, span_place_index])
    codes = [codes, *fetch(codes, "line", lines)]
    block_len = station_traces.shape[1]
    here = jnp.stack([lax.axis_index("tm"), lax.axis_index("line"), block_len]).astype(jnp.int32)
    ticks, keep, turns, back = plan_shots(
        codes, here, spectral_keep_flags, order, back_rows, shifts, slots
    )
    tables = [keep, turns, back, over_shots, forward, inverse]
    filled = None
    for chunk in range(chunks):
        filled = filter_gathers(ticks, here, gathered[chunk], tables, chunk, chunks, filled)
    return filled


def solution(mesh):
    in_specs = (P("line", "tm"), P("line"), P("line"), P())
    out_specs = P("tm", "line", None)
    return jax.shard_map(
        on_device, mesh=mesh, in_specs=in_specs, out_specs=out_specs, check_vma=False
    )
```

```python
import functools
import math

import jax
import jax.numpy as jnp
import ml_dtypes
import numpy as np
from jax import lax
from jax.experimental import pallas as pl
from jax.experimental.pallas import tpu as pltpu
from jax.sharding import PartitionSpec as P

LANES = 128
RECS = 16


def make_tables(window, shots):
    half = window // 2
    quarter = half // 2
    times = np.arange(half)
    freqs = np.concatenate([np.arange(0, half, 2), np.arange(1, half, 2)])

    def waves(rows, columns, period):
        phase = (rows[:, None] * columns[None, :] % period) * (2.0 * math.pi / period)
        return np.cos(phase), np.sin(phase)

    bf16 = ml_dtypes.bfloat16
    cosine, sine = waves(times, freqs, window)
    forward = np.stack(
        [
            np.concatenate([cosine[:, cut], -sine[:, cut]], axis=1)
            for cut in (slice(0, quarter), slice(quarter, half))
        ]
    ).astype(bf16)
    gain = np.where(freqs == 0, 0.5, 1.0)[:, None] * (2.0 / (window * shots))
    inverse = np.stack(
        [
            np.concatenate([gain[cut] * cosine.T[cut], -gain[cut] * sine.T[cut]], axis=0)
            for cut in (slice(0, quarter), slice(quarter, half))
        ]
    ).astype(bf16)
    turn_cos, turn_sin = waves(np.arange(shots), np.arange(shots), shots)
    over_shots = np.block([[turn_cos, turn_sin], [-turn_sin, turn_cos]]).astype(bf16)
    back_rows = np.stack(
        [
            np.concatenate([turn_cos, -turn_sin], axis=1),
            np.concatenate([turn_sin, turn_cos], axis=1),
        ]
    ).astype(bf16)
    shift_cos, shift_sin = waves(np.arange(LANES), freqs, window)
    shifts = np.concatenate([shift_cos, shift_sin], axis=1)
    high = shifts.astype(bf16)
    low = (shifts - high.astype(np.float64)).astype(bf16)
    order = np.zeros((half, half), bf16)
    order[freqs, np.arange(half)] = 1
    return forward, inverse, over_shots, back_rows, np.stack([high, low]), order


def plan_kernel(codes, here, flags, order, back_rows, shifts, ticks, keep, turns, back):
    shots, half = flags.shape
    slots = back.shape[0] // 2
    lines, share = codes.shape[0], codes.shape[1] // 2
    start = here[0] * here[1]
    f32, bf16 = jnp.float32, jnp.bfloat16

    keep[...] = jnp.dot(flags[...].astype(f32).astype(bf16), order[...], preferred_element_type=f32)
    shot_row = lax.broadcasted_iota(jnp.int32, (shots, LANES), 0)
    shot_lane = lax.broadcasted_iota(jnp.int32, (1, shots), 1)
    within_all = jnp.zeros((shots, LANES), jnp.int32)
    place_all = jnp.full((1, shots), -1, jnp.int32)
    for shot in range(shots):
        line, item = divmod(shot, share)
        tick = codes[line, item]
        ticks[shot] = tick
        within_all = jnp.where(shot_row == shot, tick & (LANES - 1), within_all)
        mine = (tick >= start) & (tick < start + here[1])
        place = jnp.where(mine, codes[line, share + item], -1)
        place_all = jnp.where(shot_lane == shot, place, place_all)
    shift_lane = lax.broadcasted_iota(jnp.int32, (shots, LANES), 1)
    picks = (within_all == shift_lane).astype(f32).astype(bf16)
    turns[...] = jnp.dot(picks, shifts[0], preferred_element_type=f32) + jnp.dot(
        picks, shifts[1], preferred_element_type=f32
    )
    slot_row = lax.broadcasted_iota(jnp.int32, (slots, shots), 0)
    owned = (slot_row == place_all).astype(f32).astype(bf16)
    for part in range(2):
        back[part * slots : (part + 1) * slots] = jnp.dot(
            owned, back_rows[part], preferred_element_type=f32
        ).astype(bf16)


def plan_shots(codes, here, flags, order, back_rows, shifts, slots):
    shots, half = flags.shape
    smem = pl.BlockSpec(memory_space=pltpu.SMEM)
    vmem = pl.BlockSpec(memory_space=pltpu.VMEM)
    return pl.pallas_call(
        plan_kernel,
        out_shape=[
            jax.ShapeDtypeStruct((shots,), jnp.int32),
            jax.ShapeDtypeStruct((shots, half), jnp.float32),
            jax.ShapeDtypeStruct((shots, 2 * half), jnp.float32),
            jax.ShapeDtypeStruct((2 * slots, 2 * shots), jnp.bfloat16),
        ],
        in_specs=[smem, smem] + [vmem] * 4,
        out_specs=[smem, vmem, vmem, vmem],
        compiler_params=pltpu.CompilerParams(vmem_limit_bytes=60 << 20),
        cost_estimate=pl.CostEstimate(
            flops=2 * shots * half * (half + 4 * LANES), bytes_accessed=2 << 20, transcendentals=0
        ),
    )(codes, here, flags, order, back_rows, shifts)


def gather_kernel(peers, chunk, *refs):
    ticks, here, *refs = refs
    traces, refs = refs[:peers], refs[peers:]
    tables, refs = refs[:6], refs[6 + (chunk > 0) :]
    out, records, *refs = refs
    loaded, refs = refs[:6], refs[6:]
    tiles, folds, spectra, mixed, ready, record_sem, table_sem, out_sem = refs
    recs, block_len = records.shape[1:]
    keep, turns, back, over_shots, forward, inverse = loaded
    shots, half = keep.shape
    window = 2 * half
    slots = ready.shape[0]
    wide = window // LANES
    mid = wide // 2
    arms = mid // 2
    per_block = block_len // LANES
    f32, bf16 = jnp.float32, jnp.bfloat16
    rows_here = pl.ds(chunk * recs, recs)

    record_copies = [
        pltpu.make_async_copy(
            block.at[rows_here] if away == 0 else block, records.at[away], record_sem.at[away]
        )
        for away, block in enumerate(traces)
    ]
    table_copies = [
        pltpu.make_async_copy(table, place, table_sem.at[index])
        for index, (table, place) in enumerate(zip(tables, loaded))
    ]
    for copy in record_copies:
        copy.start()
    for index in (4, 1, 0, 2, 3, 5):
        table_copies[index].start()

    for away in range(peers):
        record_copies[away].wait()
        base = partner(here[0], away, peers) * per_block
        for tile in range(per_block):
            tiles[base + tile] = records[away, :, tile * LANES : (tile + 1) * LANES]
    for tile in range(wide):
        tiles[peers * per_block + tile] = jnp.zeros((recs, LANES), bf16)

    lane = lax.broadcasted_iota(jnp.int32, (recs, LANES), 1)

    def cut(shot):
        tick = ticks[shot]
        first = lax.shift_right_logical(tick, LANES.bit_length() - 1)
        within = tick & (LANES - 1)
        piece = [tiles[first + tile] for tile in range(wide)]
        last = tiles[first + wide]
        piece[0] = jnp.where(lane < within, last.astype(f32), piece[0].astype(f32)).astype(bf16)
        rows = slice(shot * recs, (shot + 1) * recs)
        for tile in range(mid):
            at = slice(tile * LANES, (tile + 1) * LANES)
            folds[0, rows, at] = piece[tile] + piece[tile + mid]
            folds[1, rows, at] = piece[tile] - piece[tile + mid]

    table_copies[4].wait()
    rows = shots * recs
    step = min(rows, 512)
    for row in range(0, rows, step):
        for shot in range(row // recs, (row + step) // recs):
            cut(shot)
        for part in range(2):
            found = jnp.dot(
                folds[part, row : row + step], forward[part], preferred_element_type=f32
            )
            for tile in range(mid):
                spectra[part * mid + tile, row : row + step] = found[
                    :, tile * LANES : (tile + 1) * LANES
                ]

    for index in range(4):
        table_copies[index].wait()
    batch = 4
    for first in range(0, recs, batch):
        real, imag = [], []
        for rec in range(first, first + batch):
            for tile in range(mid):
                part, arm = tile // arms, tile % arms
                at = slice(tile * LANES, (tile + 1) * LANES)
                cos_turn = turns[:, at]
                sin_turn = turns[:, half + tile * LANES : half + (tile + 1) * LANES]
                cos_part = spectra[part * mid + arm, pl.ds(rec, shots, stride=recs), :]
                sin_part = spectra[part * mid + arms + arm, pl.ds(rec, shots, stride=recs), :]
                real.append((cos_part * cos_turn - sin_part * sin_turn).astype(bf16))
                imag.append((cos_part * sin_turn + sin_part * cos_turn).astype(bf16))
        stacked = jnp.concatenate(
            [jnp.concatenate(real, axis=1), jnp.concatenate(imag, axis=1)], axis=0
        )
        waves = jnp.dot(over_shots[...], stacked, preferred_element_type=f32)
        kept = jnp.concatenate([keep[...]] * batch, axis=1)
        masked = jnp.concatenate([waves[:shots] * kept, waves[shots:] * kept], axis=0).astype(bf16)
        again = jnp.dot(back[...], masked, preferred_element_type=f32)
        for rec in range(batch):
            to = pl.ds(first + rec, slots, stride=recs)
            for tile in range(mid):
                part, arm = tile // arms, tile % arms
                at = slice(rec * half + tile * LANES, rec * half + (tile + 1) * LANES)
                mixed[part * mid + arm, to, :] = again[:slots, at]
                mixed[part * mid + arms + arm, to, :] = again[slots:, at]

    table_copies[5].wait()
    group = max(1, min(slots, 256 // recs))
    out_copies = []
    for slot in range(0, slots, group):
        at = slice(slot * recs, (slot + group) * recs)
        even, odd = [
            jnp.dot(
                jnp.concatenate(
                    [mixed[part * mid + tile, at].astype(bf16) for tile in range(mid)], axis=1
                ),
                inverse[part],
                preferred_element_type=f32,
            )
            for part in range(2)
        ]
        ready[slot : slot + group, :, :half] = (even + odd).reshape(group, recs, half).astype(bf16)
        ready[slot : slot + group, :, half:] = (even - odd).reshape(group, recs, half).astype(bf16)
        copy = pltpu.make_async_copy(
            ready.at[pl.ds(slot, group)],
            out.at[pl.ds(slot, group), rows_here],
            out_sem.at[slot // group],
        )
        copy.start()
        out_copies.append(copy)
    for copy in out_copies:
        copy.wait()


def partner(index, away, count):
    if count & (count - 1) == 0:
        return index ^ away
    return (index + away) % count


def filter_gathers(ticks, here, traces, tables, chunk, chunks, filled):
    keep, turns, back, over_shots, forward, inverse = tables
    peers = len(traces)
    recs, block_len = traces[-1].shape
    rec_rows = recs * chunks
    shots, half = keep.shape
    window = 2 * half
    slots = 2 * shots // peers
    total = peers * block_len
    smem = pl.BlockSpec(memory_space=pltpu.SMEM)
    anywhere = pl.BlockSpec(memory_space=pl.ANY)
    flops = 2 * recs * (
        shots * window * half
        + slots * window * half
        + 4 * shots * shots * half
        + 4 * slots * shots * half
    )
    operands = [ticks, here, *traces, *tables]
    aliases = {}
    if chunk:
        aliases = {len(operands): 0}
        operands.append(filled)
    scratch = [
        pltpu.VMEM((peers, recs, block_len), jnp.bfloat16),
        *[pltpu.VMEM(table.shape, table.dtype) for table in tables],
        pltpu.VMEM(((total + window) // LANES, recs, LANES), jnp.bfloat16),
        pltpu.VMEM((2, shots * recs, half), jnp.bfloat16),
        pltpu.VMEM((window // LANES, shots * recs, LANES), jnp.float32),
        pltpu.VMEM((window // LANES, slots * recs, LANES), jnp.float32),
        pltpu.VMEM((slots, recs, window), jnp.bfloat16),
    ]
    return pl.pallas_call(
        functools.partial(gather_kernel, peers, chunk),
        out_shape=jax.ShapeDtypeStruct((slots, rec_rows, window), jnp.bfloat16),
        in_specs=[smem, smem] + [anywhere] * (len(operands) - 2),
        out_specs=anywhere,
        scratch_shapes=[
            *scratch,
            pltpu.SemaphoreType.DMA((peers,)),
            pltpu.SemaphoreType.DMA((len(tables),)),
            pltpu.SemaphoreType.DMA((slots,)),
        ],
        input_output_aliases=aliases,
        compiler_params=pltpu.CompilerParams(vmem_limit_bytes=60 << 20),
        cost_estimate=pl.CostEstimate(
            flops=flops, bytes_accessed=2 * recs * (total + slots * window), transcendentals=0
        ),
    )(*operands)


def on_device(station_traces, shot_onset_ticks, span_place_index, spectral_keep_flags):
    shots, half = spectral_keep_flags.shape
    forward, inverse, over_shots, back_rows, shifts, order = make_tables(2 * half, shots)
    peers = lax.axis_size("tm")
    lines = lax.axis_size("line")
    chunks = station_traces.shape[0] // RECS
    slots = 2 * shots // peers

    def fetch(block, axis, count):
        return [
            lax.ppermute(
                block, axis, [(partner(index, away, count), index) for index in range(count)]
            )
            for away in range(1, count)
        ]

    gathered = [
        [station_traces, *fetch(station_traces[chunk * RECS : (chunk + 1) * RECS], "tm", peers)]
        for chunk in range(chunks)
    ]
    codes = jnp.concatenate([shot_onset_ticks, span_place_index])
    codes = jnp.broadcast_to(codes[None], (lines, codes.shape[0]))
    codes = lax.all_to_all(codes, "line", split_axis=0, concat_axis=0, tiled=True)
    here = jnp.stack([lax.axis_index("tm"), station_traces.shape[1]]).astype(jnp.int32)
    ticks, keep, turns, back = plan_shots(
        codes, here, spectral_keep_flags, order, back_rows, shifts, slots
    )
    tables = [keep, turns, back, over_shots, forward, inverse]
    filled = None
    for chunk in range(chunks):
        filled = filter_gathers(ticks, here, gathered[chunk], tables, chunk, chunks, filled)
    return filled


def solution(mesh):
    in_specs = (P("line", "tm"), P("line"), P("line"), P())
    out_specs = P("tm", "line", None)
    return jax.shard_map(
        on_device, mesh=mesh, in_specs=in_specs, out_specs=out_specs, check_vma=False
    )
```

```python
import functools
import math

import jax
import jax.numpy as jnp
import ml_dtypes
import numpy as np
from jax import lax
from jax.experimental import pallas as pl
from jax.experimental.pallas import tpu as pltpu
from jax.sharding import PartitionSpec as P

LANES = 128
RECS = 16


def make_tables(window, shots):
    half = window // 2
    quarter = half // 2
    times = np.arange(half)
    freqs = np.concatenate([np.arange(0, half, 2), np.arange(1, half, 2)])

    def waves(rows, columns, period):
        phase = (rows[:, None] * columns[None, :] % period) * (2.0 * math.pi / period)
        return np.cos(phase), np.sin(phase)

    bf16 = ml_dtypes.bfloat16
    cosine, sine = waves(times, freqs, window)
    forward = np.stack(
        [
            np.concatenate([cosine[:, cut], -sine[:, cut]], axis=1)
            for cut in (slice(0, quarter), slice(quarter, half))
        ]
    ).astype(bf16)
    gain = np.where(freqs == 0, 0.5, 1.0)[:, None] * (2.0 / (window * shots))
    inverse = np.stack(
        [
            np.concatenate([gain[cut] * cosine.T[cut], -gain[cut] * sine.T[cut]], axis=0)
            for cut in (slice(0, quarter), slice(quarter, half))
        ]
    ).astype(bf16)
    turn_cos, turn_sin = waves(np.arange(shots), np.arange(shots), shots)
    over_shots = np.block([[turn_cos, turn_sin], [-turn_sin, turn_cos]]).astype(bf16)
    back_rows = np.stack(
        [
            np.concatenate([turn_cos, -turn_sin], axis=1),
            np.concatenate([turn_sin, turn_cos], axis=1),
        ]
    ).astype(bf16)
    order = np.zeros((half, half), bf16)
    order[freqs, np.arange(half)] = 1
    return forward, inverse, over_shots, back_rows, order


def partner(index, away, count):
    if count & (count - 1) == 0:
        return index ^ away
    return (index + away) % count


def gather_kernel(peers, *refs):
    codes, here, *refs = refs
    traces, refs = refs[:peers], refs[peers:]
    keep, over_shots, back_rows = refs[:3]
    table_refs, out = refs[3:5], refs[5]
    forward, inverse, tiles, folds, spectra, mixed, swapped, ready, table_sem, out_sem = refs[6:]
    rec_rows, block_len = traces[0].shape
    shots, half = keep.shape
    window = 2 * half
    quarter = half // 2
    slots = ready.shape[1]
    share = codes.shape[1] // 2
    recs = RECS
    wide = window // LANES
    mid = wide // 2
    per_block = block_len // LANES
    f32, bf16 = jnp.float32, jnp.bfloat16

    table_copies = [
        pltpu.make_async_copy(table, place, table_sem.at[index])
        for index, (table, place) in enumerate(zip(table_refs, (forward, inverse)))
    ]
    for copy in table_copies:
        copy.start()

    for away, block in enumerate(traces):
        base = partner(here[0], away, peers) * per_block
        for tile in range(per_block):
            tiles[base + tile] = block[:, tile * LANES : (tile + 1) * LANES]
    for tile in range(wide):
        tiles[peers * per_block + tile] = jnp.zeros((rec_rows, LANES), bf16)

    start = here[0] * here[1]
    shot_lane = lax.broadcasted_iota(jnp.int32, (1, shots), 1)
    place_all = jnp.full((1, shots), -1, jnp.int32)
    for shot in range(shots):
        line, item = divmod(shot, share)
        tick = codes[line, item]
        mine = (tick >= start) & (tick < start + here[1])
        place = jnp.where(mine, codes[line, share + item], -1)
        place_all = jnp.where(shot_lane == shot, place, place_all)
    slot_row = lax.broadcasted_iota(jnp.int32, (slots, shots), 0)
    owned = (slot_row == place_all).astype(f32).astype(bf16)
    back = jnp.concatenate(
        [jnp.dot(owned, back_rows[part], preferred_element_type=f32) for part in range(2)], axis=0
    ).astype(bf16)

    lane = lax.broadcasted_iota(jnp.int16, (recs, LANES), 1)

    def cut(shot, rows):
        tick = codes[shot // share, shot % share]
        first = lax.shift_right_logical(tick, LANES.bit_length() - 1)
        within = tick & (LANES - 1)
        piece = [tiles[first + tile, rows] for tile in range(wide + 1)]
        early = lane < within.astype(jnp.int16)
        piece = [jnp.where(early, piece[tile + 1], piece[tile]) for tile in range(wide)]
        turn = (LANES - within) & (LANES - 1)
        sums = [pltpu.roll(piece[tile] + piece[tile + mid], turn, 1) for tile in range(mid)]
        gaps = [pltpu.roll(piece[tile] - piece[tile + mid], turn, 1) for tile in range(mid)]
        return sums, gaps

    out_copies = []
    for chunk in range(rec_rows // recs):
        rows = slice(chunk * recs, (chunk + 1) * recs)
        for first in range(0, shots, 16):
            cuts = [cut(shot, rows) for shot in range(first, first + 16)]
            for part in range(2):
                for tile in range(mid):
                    panel = jnp.stack([cuts[item][part][tile] for item in range(16)])
                    folds[part, :, first : first + 16, tile * LANES : (tile + 1) * LANES] = (
                        jnp.swapaxes(panel, 0, 1)
                    )
        if chunk == 0:
            table_copies[0].wait()
        group = 8
        for rec in range(0, recs, group):
            for part in range(2):
                found = jnp.dot(
                    folds[part, rec : rec + group].reshape(group * shots, half),
                    forward[part],
                    preferred_element_type=f32,
                )
                spectra[part, rec * shots : (rec + group) * shots] = found.astype(bf16)
        for rec in range(recs):
            at = slice(rec * shots, (rec + 1) * shots)
            even, odd = spectra[0, at], spectra[1, at]
            stacked = jnp.concatenate(
                [
                    jnp.concatenate([even[:, :quarter], odd[:, :quarter]], axis=1),
                    jnp.concatenate([even[:, quarter:], odd[:, quarter:]], axis=1),
                ],
                axis=0,
            )
            waves = jnp.dot(over_shots[...], stacked, preferred_element_type=f32)
            masked = jnp.concatenate(
                [waves[:shots] * keep[...], waves[shots:] * keep[...]], axis=0
            ).astype(bf16)
            again = jnp.dot(back, masked, preferred_element_type=f32).astype(bf16)
            at = slice(rec * slots, (rec + 1) * slots)
            for part in range(2):
                columns = slice(part * quarter, (part + 1) * quarter)
                mixed[part, at, :quarter] = again[:slots, columns]
                mixed[part, at, quarter:] = again[slots:, columns]
        if chunk == 0:
            table_copies[1].wait()
        for rec in range(0, recs, group):
            at = slice(rec * slots, (rec + group) * slots)
            even, odd = [
                jnp.dot(mixed[part, at], inverse[part], preferred_element_type=f32)
                for part in range(2)
            ]
            swapped[rec : rec + group, :, :half] = (
                (even + odd).astype(bf16).reshape(group, slots, half)
            )
            swapped[rec : rec + group, :, half:] = (
                (even - odd).astype(bf16).reshape(group, slots, half)
            )
        for slot in range(0, slots, 16):
            for tile in range(wide):
                at = slice(tile * LANES, (tile + 1) * LANES)
                ready[chunk, slot : slot + 16, :, at] = jnp.swapaxes(
                    swapped[:, slot : slot + 16, at], 0, 1
                )
        copy = pltpu.make_async_copy(
            ready.at[chunk], out.at[:, pl.ds(chunk * recs, recs)], out_sem.at[chunk]
        )
        copy.start()
        out_copies.append(copy)
    for copy in out_copies:
        copy.wait()


def filter_gathers(codes, here, traces, keep, tables):
    forward, inverse, over_shots, back_rows = tables
    peers = len(traces)
    rec_rows, block_len = traces[0].shape
    shots, half = keep.shape
    window = 2 * half
    slots = 2 * shots // peers
    total = peers * block_len
    chunks = rec_rows // RECS
    smem = pl.BlockSpec(memory_space=pltpu.SMEM)
    vmem = pl.BlockSpec(memory_space=pltpu.VMEM)
    anywhere = pl.BlockSpec(memory_space=pl.ANY)
    flops = 2 * rec_rows * (
        shots * window * half
        + slots * window * half
        + 4 * shots * shots * half
        + 4 * slots * shots * half
    )
    bf16 = jnp.bfloat16
    return pl.pallas_call(
        functools.partial(gather_kernel, peers),
        out_shape=jax.ShapeDtypeStruct((slots, rec_rows, window), bf16),
        in_specs=[smem, smem] + [vmem] * (peers + 3) + [anywhere] * 2,
        out_specs=anywhere,
        scratch_shapes=[
            pltpu.VMEM(forward.shape, bf16),
            pltpu.VMEM(inverse.shape, bf16),
            pltpu.VMEM(((total + window) // LANES, rec_rows, LANES), bf16),
            pltpu.VMEM((2, RECS, shots, half), bf16),
            pltpu.VMEM((2, RECS * shots, half), bf16),
            pltpu.VMEM((2, RECS * slots, half), bf16),
            pltpu.VMEM((RECS, slots, window), bf16),
            pltpu.VMEM((chunks, slots, RECS, window), bf16),
            pltpu.SemaphoreType.DMA((2,)),
            pltpu.SemaphoreType.DMA((chunks,)),
        ],
        compiler_params=pltpu.CompilerParams(vmem_limit_bytes=60 << 20),
        cost_estimate=pl.CostEstimate(
            flops=flops,
            bytes_accessed=2 * rec_rows * (total + slots * window),
            transcendentals=0,
        ),
    )(codes, here, *traces, keep, over_shots, back_rows, forward, inverse)


def on_device(station_traces, shot_onset_ticks, span_place_index, spectral_keep_flags):
    shots, half = spectral_keep_flags.shape
    *tables, order = make_tables(2 * half, shots)
    peers = lax.axis_size("tm")
    lines = lax.axis_size("line")
    traces = [station_traces] + [
        lax.ppermute(
            station_traces,
            "tm",
            [(partner(index, away, peers), index) for index in range(peers)],
        )
        for away in range(1, peers)
    ]
    codes = jnp.concatenate([shot_onset_ticks, span_place_index])
    codes = jnp.broadcast_to(codes[None], (lines, codes.shape[0]))
    codes = lax.all_to_all(codes, "line", split_axis=0, concat_axis=0, tiled=True)
    here = jnp.stack([lax.axis_index("tm"), station_traces.shape[1]]).astype(jnp.int32)
    keep = jnp.dot(
        spectral_keep_flags.astype(jnp.bfloat16), order, preferred_element_type=jnp.float32
    )
    return filter_gathers(codes, here, traces, keep, tables)


def solution(mesh):
    in_specs = (P("line", "tm"), P("line"), P("line"), P())
    out_specs = P("tm", "line", None)
    return jax.shard_map(
        on_device, mesh=mesh, in_specs=in_specs, out_specs=out_specs, check_vma=False
    )
```

```python
import functools
import math

import jax
import jax.numpy as jnp
import ml_dtypes
import numpy as np
from jax import lax
from jax.experimental import pallas as pl
from jax.experimental.pallas import tpu as pltpu
from jax.sharding import PartitionSpec as P

LANES = 128
RECS = 16


def make_tables(window, shots):
    half = window // 2
    quarter = half // 2
    times = np.arange(half)
    freqs = np.concatenate([np.arange(0, half, 2), np.arange(1, half, 2)])

    def waves(rows, columns, period):
        phase = (rows[:, None] * columns[None, :] % period) * (2.0 * math.pi / period)
        return np.cos(phase), np.sin(phase)

    bf16 = ml_dtypes.bfloat16
    cosine, sine = waves(times, freqs, window)
    forward = np.stack(
        [
            np.concatenate([cosine[:, cut], -sine[:, cut]], axis=1)
            for cut in (slice(0, quarter), slice(quarter, half))
        ]
    ).astype(bf16)
    gain = np.where(freqs == 0, 0.5, 1.0)[:, None] * (2.0 / (window * shots))
    inverse = np.stack(
        [
            np.concatenate([gain[cut] * cosine.T[cut], -gain[cut] * sine.T[cut]], axis=0)
            for cut in (slice(0, quarter), slice(quarter, half))
        ]
    ).astype(bf16)
    turn_cos, turn_sin = waves(np.arange(shots), np.arange(shots), shots)
    forward, inverse = [
        table.reshape(2, half, half // LANES, LANES).swapaxes(1, 2) for table in (forward, inverse)
    ]
    over_shots = np.block([[turn_cos, turn_sin], [-turn_sin, turn_cos]]).astype(bf16)
    back_rows = np.stack(
        [
            np.concatenate([turn_cos, -turn_sin], axis=1),
            np.concatenate([turn_sin, turn_cos], axis=1),
        ]
    ).astype(bf16)
    order = np.zeros((half, half), bf16)
    order[freqs, np.arange(half)] = 1
    return forward, inverse, over_shots, back_rows, order


def partner(index, away, count):
    if count & (count - 1) == 0:
        return index ^ away
    return (index + away) % count


def gather_kernel(peers, *refs):
    codes, here, *refs = refs
    traces, refs = refs[:peers], refs[peers:]
    keep, over_shots, back_rows = refs[:3]
    table_refs, out = refs[3:5], refs[5]
    forward, inverse, tiles, folds, spectra, mixed, swapped, ready, table_sem, out_sem = refs[6:]
    rec_rows, block_len = traces[0].shape
    shots, half = keep.shape
    window = 2 * half
    slots = ready.shape[2]
    share = codes.shape[1] // 2
    recs = RECS
    wide = window // LANES
    mid = wide // 2
    arms = mid // 2
    per_block = block_len // LANES
    f32, bf16 = jnp.float32, jnp.bfloat16

    table_copies = [
        pltpu.make_async_copy(table, place, table_sem.at[index])
        for index, (table, place) in enumerate(zip(table_refs, (forward, inverse)))
    ]
    for copy in table_copies:
        copy.start()

    for away, block in enumerate(traces):
        base = partner(here[0], away, peers) * per_block
        for tile in range(per_block):
            tiles[base + tile] = block[:, tile * LANES : (tile + 1) * LANES]
    for tile in range(wide):
        tiles[peers * per_block + tile] = jnp.zeros((rec_rows, LANES), bf16)

    start = here[0] * here[1]
    shot_lane = lax.broadcasted_iota(jnp.int32, (1, shots), 1)
    place_all = jnp.full((1, shots), -1, jnp.int32)
    for shot in range(shots):
        line, item = divmod(shot, share)
        tick = codes[line, item]
        mine = (tick >= start) & (tick < start + here[1])
        place = jnp.where(mine, codes[line, share + item], -1)
        place_all = jnp.where(shot_lane == shot, place, place_all)
    slot_row = lax.broadcasted_iota(jnp.int32, (slots, shots), 0)
    owned = (slot_row == place_all).astype(f32).astype(bf16)
    back = jnp.concatenate(
        [jnp.dot(owned, back_rows[part], preferred_element_type=f32) for part in range(2)], axis=0
    ).astype(bf16)

    lane = lax.broadcasted_iota(jnp.int16, (recs, LANES), 1)

    def cut(shot, rows):
        tick = codes[shot // share, shot % share]
        first = lax.shift_right_logical(tick, LANES.bit_length() - 1)
        within = tick & (LANES - 1)
        piece = [tiles[first + tile, rows] for tile in range(wide + 1)]
        early = lane < within.astype(jnp.int16)
        piece = [jnp.where(early, piece[tile + 1], piece[tile]) for tile in range(wide)]
        turn = (LANES - within) & (LANES - 1)
        sums = [pltpu.roll(piece[tile] + piece[tile + mid], turn, 1) for tile in range(mid)]
        gaps = [pltpu.roll(piece[tile] - piece[tile + mid], turn, 1) for tile in range(mid)]
        return sums, gaps

    def product(left, right, part):
        return jnp.dot(
            left,
            jnp.concatenate([right[part, tile] for tile in range(mid)], axis=1),
            preferred_element_type=f32,
        )

    out_copies = []
    for chunk in range(rec_rows // recs):
        rows = slice(chunk * recs, (chunk + 1) * recs)
        for first in range(0, shots, 16):
            cuts = [cut(shot, rows) for shot in range(first, first + 16)]
            for part in range(2):
                for tile in range(mid):
                    panel = jnp.stack([cuts[item][part][tile] for item in range(16)])
                    folds[part, tile, :, first : first + 16] = jnp.swapaxes(panel, 0, 1)
        if chunk == 0:
            table_copies[0].wait()
        group = 8
        for rec in range(0, recs, group):
            for part in range(2):
                panel = [
                    folds[part, tile, rec : rec + group].reshape(group * shots, LANES)
                    for tile in range(mid)
                ]
                found = product(jnp.concatenate(panel, axis=1), forward, part).astype(bf16)
                for tile in range(mid):
                    spectra[part, tile, rec * shots : (rec + group) * shots] = found[
                        :, tile * LANES : (tile + 1) * LANES
                    ]
        for rec in range(recs):
            at = slice(rec * shots, (rec + 1) * shots)
            real, imag = [
                jnp.concatenate(
                    [spectra[part, tile, at] for part in range(2) for tile in tiles_of], axis=1
                )
                for tiles_of in (range(arms), range(arms, mid))
            ]
            stacked = jnp.concatenate([real, imag], axis=0)
            waves = jnp.dot(over_shots[...], stacked, preferred_element_type=f32)
            masked = jnp.concatenate(
                [waves[:shots] * keep[...], waves[shots:] * keep[...]], axis=0
            ).astype(bf16)
            again = jnp.dot(back, masked, preferred_element_type=f32).astype(bf16)
            at = slice(rec * slots, (rec + 1) * slots)
            for part in range(2):
                for arm in range(arms):
                    tile = part * arms + arm
                    columns = slice(tile * LANES, (tile + 1) * LANES)
                    mixed[part, arm, at] = again[:slots, columns]
                    mixed[part, arms + arm, at] = again[slots:, columns]
        if chunk == 0:
            table_copies[1].wait()
        for rec in range(0, recs, group):
            at = slice(rec * slots, (rec + group) * slots)
            even, odd = [
                product(
                    jnp.concatenate([mixed[part, tile, at] for tile in range(mid)], axis=1),
                    inverse,
                    part,
                )
                for part in range(2)
            ]
            early, late = (even + odd).astype(bf16), (even - odd).astype(bf16)
            for tile in range(mid):
                columns = slice(tile * LANES, (tile + 1) * LANES)
                for half_at, found in ((tile, early), (tile + mid, late)):
                    swapped[half_at, rec : rec + group] = found[:, columns].reshape(
                        group, slots, LANES
                    )
        for tile in range(wide):
            for slot in range(0, slots, 16):
                ready[chunk, tile, slot : slot + 16] = jnp.swapaxes(
                    swapped[tile, :, slot : slot + 16], 0, 1
                )
            copy = pltpu.make_async_copy(
                ready.at[chunk, tile],
                out.at[:, pl.ds(chunk * recs, recs), pl.ds(tile * LANES, LANES)],
                out_sem.at[chunk, tile],
            )
            copy.start()
            out_copies.append(copy)
    for copy in out_copies:
        copy.wait()


def filter_gathers(codes, here, traces, keep, tables):
    forward, inverse, over_shots, back_rows = tables
    peers = len(traces)
    rec_rows, block_len = traces[0].shape
    shots, half = keep.shape
    window = 2 * half
    slots = 2 * shots // peers
    total = peers * block_len
    chunks = rec_rows // RECS
    smem = pl.BlockSpec(memory_space=pltpu.SMEM)
    vmem = pl.BlockSpec(memory_space=pltpu.VMEM)
    anywhere = pl.BlockSpec(memory_space=pl.ANY)
    flops = 2 * rec_rows * (
        shots * window * half
        + slots * window * half
        + 4 * shots * shots * half
        + 4 * slots * shots * half
    )
    bf16 = jnp.bfloat16
    return pl.pallas_call(
        functools.partial(gather_kernel, peers),
        out_shape=jax.ShapeDtypeStruct((slots, rec_rows, window), bf16),
        in_specs=[smem, smem] + [vmem] * (peers + 3) + [anywhere] * 2,
        out_specs=anywhere,
        scratch_shapes=[
            pltpu.VMEM(forward.shape, bf16),
            pltpu.VMEM(inverse.shape, bf16),
            pltpu.VMEM(((total + window) // LANES, rec_rows, LANES), bf16),
            pltpu.VMEM((2, half // LANES, RECS, shots, LANES), bf16),
            pltpu.VMEM((2, half // LANES, RECS * shots, LANES), bf16),
            pltpu.VMEM((2, half // LANES, RECS * slots, LANES), bf16),
            pltpu.VMEM((window // LANES, RECS, slots, LANES), bf16),
            pltpu.VMEM((chunks, window // LANES, slots, RECS, LANES), bf16),
            pltpu.SemaphoreType.DMA((2,)),
            pltpu.SemaphoreType.DMA((chunks, window // LANES)),
        ],
        compiler_params=pltpu.CompilerParams(vmem_limit_bytes=60 << 20),
        cost_estimate=pl.CostEstimate(
            flops=flops,
            bytes_accessed=2 * rec_rows * (total + slots * window),
            transcendentals=0,
        ),
    )(codes, here, *traces, keep, over_shots, back_rows, forward, inverse)


def on_device(station_traces, shot_onset_ticks, span_place_index, spectral_keep_flags):
    shots, half = spectral_keep_flags.shape
    *tables, order = make_tables(2 * half, shots)
    peers = lax.axis_size("tm")
    lines = lax.axis_size("line")
    traces = [station_traces] + [
        lax.ppermute(
            station_traces,
            "tm",
            [(partner(index, away, peers), index) for index in range(peers)],
        )
        for away in range(1, peers)
    ]
    codes = jnp.concatenate([shot_onset_ticks, span_place_index])
    codes = jnp.broadcast_to(codes[None], (lines, codes.shape[0]))
    codes = lax.all_to_all(codes, "line", split_axis=0, concat_axis=0, tiled=True)
    here = jnp.stack([lax.axis_index("tm"), station_traces.shape[1]]).astype(jnp.int32)
    keep = jnp.dot(
        spectral_keep_flags.astype(jnp.bfloat16), order, preferred_element_type=jnp.float32
    )
    return filter_gathers(codes, here, traces, keep, tables)


def solution(mesh):
    in_specs = (P("line", "tm"), P("line"), P("line"), P())
    out_specs = P("tm", "line", None)
    return jax.shard_map(
        on_device, mesh=mesh, in_specs=in_specs, out_specs=out_specs, check_vma=False
    )
```

```python
import functools
import math

import jax
import jax.numpy as jnp
import ml_dtypes
import numpy as np
from jax import lax
from jax.experimental import pallas as pl
from jax.experimental.pallas import tpu as pltpu
from jax.sharding import PartitionSpec as P

LANES = 128
RECS = 16


def make_tables(window, shots):
    half = window // 2
    quarter = half // 2
    times = np.arange(half)
    freqs = np.concatenate([np.arange(0, half, 2), np.arange(1, half, 2)])

    def waves(rows, columns, period):
        phase = (rows[:, None] * columns[None, :] % period) * (2.0 * math.pi / period)
        return np.cos(phase), np.sin(phase)

    bf16 = ml_dtypes.bfloat16
    cosine, sine = waves(times, freqs, window)
    forward = np.stack(
        [
            np.concatenate([cosine[:, cut], -sine[:, cut]], axis=1)
            for cut in (slice(0, quarter), slice(quarter, half))
        ]
    ).astype(bf16)
    gain = np.where(freqs == 0, 0.5, 1.0)[:, None] * (2.0 / (window * shots))
    inverse = np.stack(
        [
            np.concatenate([gain[cut] * cosine.T[cut], -gain[cut] * sine.T[cut]], axis=0)
            for cut in (slice(0, quarter), slice(quarter, half))
        ]
    ).astype(bf16)
    turn_cos, turn_sin = waves(np.arange(shots), np.arange(shots), shots)
    forward, inverse = [
        table.reshape(2, half, half // LANES, LANES).swapaxes(1, 2) for table in (forward, inverse)
    ]
    over_shots = np.block([[turn_cos, turn_sin], [-turn_sin, turn_cos]]).astype(bf16)
    back_rows = np.stack(
        [
            np.concatenate([turn_cos, -turn_sin], axis=1),
            np.concatenate([turn_sin, turn_cos], axis=1),
        ]
    ).astype(bf16)
    order = np.zeros((half, half), bf16)
    order[freqs, np.arange(half)] = 1
    return forward, inverse, over_shots, back_rows, order


def partner(index, away, count):
    if count & (count - 1) == 0:
        return index ^ away
    return (index + away) % count


def gather_kernel(peers, *refs):
    codes, here, *refs = refs
    traces, refs = refs[:peers], refs[peers:]
    keep, over_shots, back_rows = refs[:3]
    table_refs, out = refs[3:5], refs[5]
    forward, inverse, tiles, folds, spectra, waved, mixed, swapped, ready, table_sem, out_sem = refs[6:]
    rec_rows, block_len = traces[0].shape
    shots, half = keep.shape
    window = 2 * half
    slots = ready.shape[2]
    share = codes.shape[1] // 2
    recs = RECS
    wide = window // LANES
    mid = wide // 2
    arms = mid // 2
    per_block = block_len // LANES
    f32, bf16 = jnp.float32, jnp.bfloat16

    table_copies = [
        pltpu.make_async_copy(table, place, table_sem.at[index])
        for index, (table, place) in enumerate(zip(table_refs, (forward, inverse)))
    ]
    for copy in table_copies:
        copy.start()

    for away, block in enumerate(traces):
        base = partner(here[0], away, peers) * per_block
        for tile in range(per_block):
            tiles[base + tile] = block[:, tile * LANES : (tile + 1) * LANES]
    for tile in range(wide):
        tiles[peers * per_block + tile] = jnp.zeros((rec_rows, LANES), bf16)

    start = here[0] * here[1]
    shot_lane = lax.broadcasted_iota(jnp.int32, (1, shots), 1)
    place_all = jnp.full((1, shots), -1, jnp.int32)
    for shot in range(shots):
        line, item = divmod(shot, share)
        tick = codes[line, item]
        mine = (tick >= start) & (tick < start + here[1])
        place = jnp.where(mine, codes[line, share + item], -1)
        place_all = jnp.where(shot_lane == shot, place, place_all)
    slot_row = lax.broadcasted_iota(jnp.int32, (slots, shots), 0)
    owned = (slot_row == place_all).astype(f32).astype(bf16)
    back = jnp.concatenate(
        [jnp.dot(owned, back_rows[part], preferred_element_type=f32) for part in range(2)], axis=0
    ).astype(bf16)

    lane = lax.broadcasted_iota(jnp.int16, (recs, LANES), 1)

    def cut(shot, rows):
        tick = codes[shot // share, shot % share]
        first = lax.shift_right_logical(tick, LANES.bit_length() - 1)
        within = tick & (LANES - 1)
        piece = [tiles[first + tile, rows] for tile in range(wide + 1)]
        early = lane < within.astype(jnp.int16)
        piece = [jnp.where(early, piece[tile + 1], piece[tile]) for tile in range(wide)]
        turn = (LANES - within) & (LANES - 1)
        sums = [pltpu.roll(piece[tile] + piece[tile + mid], turn, 1) for tile in range(mid)]
        gaps = [pltpu.roll(piece[tile] - piece[tile + mid], turn, 1) for tile in range(mid)]
        return sums, gaps

    def product(left, right, part):
        return jnp.dot(
            left,
            jnp.concatenate([right[part, tile] for tile in range(mid)], axis=1),
            preferred_element_type=f32,
        )

    out_copies = []
    for chunk in range(rec_rows // recs):
        rows = slice(chunk * recs, (chunk + 1) * recs)
        for first in range(0, shots, 16):
            cuts = [cut(shot, rows) for shot in range(first, first + 16)]
            for part in range(2):
                for tile in range(mid):
                    panel = jnp.stack([cuts[item][part][tile] for item in range(16)])
                    folds[part, tile, :, first : first + 16] = jnp.swapaxes(panel, 0, 1)
        if chunk == 0:
            table_copies[0].wait()
        group = 8
        for rec in range(0, recs, group):
            for part in range(2):
                panel = [
                    folds[part, tile, rec : rec + group].reshape(group * shots, LANES)
                    for tile in range(mid)
                ]
                found = product(jnp.concatenate(panel, axis=1), forward, part).astype(bf16)
                for tile in range(mid):
                    spectra[part, tile, rec * shots : (rec + group) * shots] = found[
                        :, tile * LANES : (tile + 1) * LANES
                    ]
        for rec in range(recs):
            at = slice(rec * shots, (rec + 1) * shots)
            real, imag = [
                jnp.concatenate(
                    [spectra[part, tile, at] for part in range(2) for tile in tiles_of], axis=1
                )
                for tiles_of in (range(arms), range(arms, mid))
            ]
            stacked = jnp.concatenate([real, imag], axis=0)
            waves = jnp.dot(over_shots[...], stacked, preferred_element_type=f32)
            masked = jnp.concatenate(
                [waves[:shots] * keep[...], waves[shots:] * keep[...]], axis=0
            ).astype(bf16)
            at = slice(2 * rec * shots, 2 * (rec + 1) * shots)
            for tile in range(mid):
                waved[tile, at] = masked[:, tile * LANES : (tile + 1) * LANES]
        for rec in range(recs):
            at = slice(2 * rec * shots, 2 * (rec + 1) * shots)
            masked = jnp.concatenate([waved[tile, at] for tile in range(mid)], axis=1)
            again = jnp.dot(back, masked, preferred_element_type=f32).astype(bf16)
            at = slice(rec * slots, (rec + 1) * slots)
            for part in range(2):
                for arm in range(arms):
                    tile = part * arms + arm
                    columns = slice(tile * LANES, (tile + 1) * LANES)
                    mixed[part, arm, at] = again[:slots, columns]
                    mixed[part, arms + arm, at] = again[slots:, columns]
        if chunk == 0:
            table_copies[1].wait()
        for rec in range(0, recs, group):
            at = slice(rec * slots, (rec + group) * slots)
            even, odd = [
                product(
                    jnp.concatenate([mixed[part, tile, at] for tile in range(mid)], axis=1),
                    inverse,
                    part,
                )
                for part in range(2)
            ]
            early, late = (even + odd).astype(bf16), (even - odd).astype(bf16)
            for tile in range(mid):
                columns = slice(tile * LANES, (tile + 1) * LANES)
                for half_at, found in ((tile, early), (tile + mid, late)):
                    swapped[half_at, rec : rec + group] = found[:, columns].reshape(
                        group, slots, LANES
                    )
        for tile in range(wide):
            for slot in range(0, slots, 16):
                ready[chunk, tile, slot : slot + 16] = jnp.swapaxes(
                    swapped[tile, :, slot : slot + 16], 0, 1
                )
            copy = pltpu.make_async_copy(
                ready.at[chunk, tile],
                out.at[:, pl.ds(chunk * recs, recs), pl.ds(tile * LANES, LANES)],
                out_sem.at[chunk, tile],
            )
            copy.start()
            out_copies.append(copy)
    for copy in out_copies:
        copy.wait()


def filter_gathers(codes, here, traces, keep, tables):
    forward, inverse, over_shots, back_rows = tables
    peers = len(traces)
    rec_rows, block_len = traces[0].shape
    shots, half = keep.shape
    window = 2 * half
    slots = 2 * shots // peers
    total = peers * block_len
    chunks = rec_rows // RECS
    smem = pl.BlockSpec(memory_space=pltpu.SMEM)
    vmem = pl.BlockSpec(memory_space=pltpu.VMEM)
    anywhere = pl.BlockSpec(memory_space=pl.ANY)
    flops = 2 * rec_rows * (
        shots * window * half
        + slots * window * half
        + 4 * shots * shots * half
        + 4 * slots * shots * half
    )
    bf16 = jnp.bfloat16
    return pl.pallas_call(
        functools.partial(gather_kernel, peers),
        out_shape=jax.ShapeDtypeStruct((slots, rec_rows, window), bf16),
        in_specs=[smem, smem] + [vmem] * (peers + 3) + [anywhere] * 2,
        out_specs=anywhere,
        scratch_shapes=[
            pltpu.VMEM(forward.shape, bf16),
            pltpu.VMEM(inverse.shape, bf16),
            pltpu.VMEM(((total + window) // LANES, rec_rows, LANES), bf16),
            pltpu.VMEM((2, half // LANES, RECS, shots, LANES), bf16),
            pltpu.VMEM((2, half // LANES, RECS * shots, LANES), bf16),
            pltpu.VMEM((half // LANES, 2 * RECS * shots, LANES), bf16),
            pltpu.VMEM((2, half // LANES, RECS * slots, LANES), bf16),
            pltpu.VMEM((window // LANES, RECS, slots, LANES), bf16),
            pltpu.VMEM((chunks, window // LANES, slots, RECS, LANES), bf16),
            pltpu.SemaphoreType.DMA((2,)),
            pltpu.SemaphoreType.DMA((chunks, window // LANES)),
        ],
        compiler_params=pltpu.CompilerParams(vmem_limit_bytes=60 << 20),
        cost_estimate=pl.CostEstimate(
            flops=flops,
            bytes_accessed=2 * rec_rows * (total + slots * window),
            transcendentals=0,
        ),
    )(codes, here, *traces, keep, over_shots, back_rows, forward, inverse)


def on_device(station_traces, shot_onset_ticks, span_place_index, spectral_keep_flags):
    shots, half = spectral_keep_flags.shape
    *tables, order = make_tables(2 * half, shots)
    peers = lax.axis_size("tm")
    lines = lax.axis_size("line")
    traces = [station_traces] + [
        lax.ppermute(
            station_traces,
            "tm",
            [(partner(index, away, peers), index) for index in range(peers)],
        )
        for away in range(1, peers)
    ]
    codes = jnp.concatenate([shot_onset_ticks, span_place_index])
    codes = jnp.broadcast_to(codes[None], (lines, codes.shape[0]))
    codes = lax.all_to_all(codes, "line", split_axis=0, concat_axis=0, tiled=True)
    here = jnp.stack([lax.axis_index("tm"), station_traces.shape[1]]).astype(jnp.int32)
    keep = jnp.dot(
        spectral_keep_flags.astype(jnp.bfloat16), order, preferred_element_type=jnp.float32
    )
    return filter_gathers(codes, here, traces, keep, tables)


def solution(mesh):
    in_specs = (P("line", "tm"), P("line"), P("line"), P())
    out_specs = P("tm", "line", None)
    return jax.shard_map(
        on_device, mesh=mesh, in_specs=in_specs, out_specs=out_specs, check_vma=False
    )
```

```python
import functools
import math

import jax
import jax.numpy as jnp
import ml_dtypes
import numpy as np
from jax import lax
from jax.experimental import pallas as pl
from jax.experimental.pallas import tpu as pltpu
from jax.sharding import PartitionSpec as P

LANES = 128
RECS = 16


def make_tables(window, shots):
    half = window // 2
    quarter = half // 2
    times = np.arange(half)
    freqs = np.concatenate([np.arange(0, half, 2), np.arange(1, half, 2)])

    def waves(rows, columns, period):
        phase = (rows[:, None] * columns[None, :] % period) * (2.0 * math.pi / period)
        return np.cos(phase), np.sin(phase)

    bf16 = ml_dtypes.bfloat16
    cosine, sine = waves(times, freqs, window)
    forward = np.stack(
        [
            np.concatenate([cosine[:, cut], -sine[:, cut]], axis=1)
            for cut in (slice(0, quarter), slice(quarter, half))
        ]
    ).astype(bf16)
    gain = np.where(freqs == 0, 0.5, 1.0)[:, None] * (2.0 / (window * shots))
    inverse = np.stack(
        [
            np.concatenate([gain[cut] * cosine.T[cut], -gain[cut] * sine.T[cut]], axis=0)
            for cut in (slice(0, quarter), slice(quarter, half))
        ]
    ).astype(bf16)
    turn_cos, turn_sin = waves(np.arange(shots), np.arange(shots), shots)
    forward, inverse = [
        table.reshape(2, half, half // LANES, LANES).swapaxes(1, 2) for table in (forward, inverse)
    ]
    over_shots = np.block([[turn_cos, turn_sin], [-turn_sin, turn_cos]]).astype(bf16)
    back_rows = np.stack(
        [
            np.concatenate([turn_cos, -turn_sin], axis=1),
            np.concatenate([turn_sin, turn_cos], axis=1),
        ]
    ).astype(bf16)
    order = np.zeros((half, half), bf16)
    order[freqs, np.arange(half)] = 1
    return forward, inverse, over_shots, back_rows, order


def partner(index, away, count):
    if count & (count - 1) == 0:
        return index ^ away
    return (index + away) % count


def plan_kernel(codes, here, flags, order, back_rows, keep, back):
    shots = flags.shape[0]
    slots = back.shape[0] // 2
    share = codes.shape[1] // 2
    f32, bf16 = jnp.float32, jnp.bfloat16
    keep[...] = jnp.dot(flags[...].astype(f32).astype(bf16), order[...], preferred_element_type=f32)
    start = here[0] * here[1]
    shot_lane = lax.broadcasted_iota(jnp.int32, (1, shots), 1)
    place_all = jnp.full((1, shots), -1, jnp.int32)
    for shot in range(shots):
        line, item = divmod(shot, share)
        tick = codes[line, item]
        mine = (tick >= start) & (tick < start + here[1])
        place = jnp.where(mine, codes[line, share + item], -1)
        place_all = jnp.where(shot_lane == shot, place, place_all)
    slot_row = lax.broadcasted_iota(jnp.int32, (slots, shots), 0)
    owned = (slot_row == place_all).astype(f32).astype(bf16)
    for part in range(2):
        back[part * slots : (part + 1) * slots] = jnp.dot(
            owned, back_rows[part], preferred_element_type=f32
        ).astype(bf16)


def plan_shots(codes, here, flags, order, back_rows, slots):
    shots, half = flags.shape
    smem = pl.BlockSpec(memory_space=pltpu.SMEM)
    vmem = pl.BlockSpec(memory_space=pltpu.VMEM)
    return pl.pallas_call(
        plan_kernel,
        out_shape=[
            jax.ShapeDtypeStruct((shots, half), jnp.float32),
            jax.ShapeDtypeStruct((2 * slots, 2 * shots), jnp.bfloat16),
        ],
        in_specs=[smem, smem, vmem, vmem, vmem],
        out_specs=[vmem, vmem],
        compiler_params=pltpu.CompilerParams(vmem_limit_bytes=60 << 20),
        cost_estimate=pl.CostEstimate(flops=0, bytes_accessed=8 << 20, transcendentals=0),
    )(codes, here, flags, order, back_rows)


def gather_kernel(peers, chunk, *refs):
    codes, here, *refs = refs
    traces, refs = refs[:peers], refs[peers:]
    keep, over_shots, back = refs[:3]
    table_refs, refs = refs[3:5], refs[5 + (chunk > 0) :]
    out, forward, inverse, tiles, folds, spectra, waved, mixed, swapped, ready = refs[:10]
    table_sem, out_sem = refs[10:]
    recs, block_len = traces[0].shape
    shots, half = keep.shape
    window = 2 * half
    slots = ready.shape[1]
    share = codes.shape[1] // 2
    wide = window // LANES
    mid = wide // 2
    arms = mid // 2
    per_block = block_len // LANES
    f32, bf16 = jnp.float32, jnp.bfloat16

    table_copies = [
        pltpu.make_async_copy(table, place, table_sem.at[index])
        for index, (table, place) in enumerate(zip(table_refs, (forward, inverse)))
    ]
    for copy in table_copies:
        copy.start()

    for away, block in enumerate(traces):
        base = partner(here[0], away, peers) * per_block
        for tile in range(per_block):
            tiles[base + tile] = block[:, tile * LANES : (tile + 1) * LANES]
    for tile in range(wide):
        tiles[peers * per_block + tile] = jnp.zeros((recs, LANES), bf16)

    lane = lax.broadcasted_iota(jnp.int16, (recs, LANES), 1)

    def cut(shot):
        tick = codes[shot // share, shot % share]
        first = lax.shift_right_logical(tick, LANES.bit_length() - 1)
        within = tick & (LANES - 1)
        piece = [tiles[first + tile] for tile in range(wide + 1)]
        early = lane < within.astype(jnp.int16)
        piece = [jnp.where(early, piece[tile + 1], piece[tile]) for tile in range(wide)]
        turn = (LANES - within) & (LANES - 1)
        sums = [pltpu.roll(piece[tile] + piece[tile + mid], turn, 1) for tile in range(mid)]
        gaps = [pltpu.roll(piece[tile] - piece[tile + mid], turn, 1) for tile in range(mid)]
        return sums, gaps

    def product(left, right, part):
        return jnp.dot(
            left,
            jnp.concatenate([right[part, tile] for tile in range(mid)], axis=1),
            preferred_element_type=f32,
        )

    out_copies = []
    for first in range(0, shots, 16):
        cuts = [cut(shot) for shot in range(first, first + 16)]
        for part in range(2):
            for tile in range(mid):
                panel = jnp.stack([cuts[item][part][tile] for item in range(16)])
                folds[part, tile, :, first : first + 16] = jnp.swapaxes(panel, 0, 1)
    table_copies[0].wait()
    group = 8
    for rec in range(0, recs, group):
        for part in range(2):
            panel = [
                folds[part, tile, rec : rec + group].reshape(group * shots, LANES)
                for tile in range(mid)
            ]
            found = product(jnp.concatenate(panel, axis=1), forward, part).astype(bf16)
            for tile in range(mid):
                spectra[part, tile, rec * shots : (rec + group) * shots] = found[
                    :, tile * LANES : (tile + 1) * LANES
                ]
    for rec in range(recs):
        at = slice(rec * shots, (rec + 1) * shots)
        real, imag = [
            jnp.concatenate(
                [spectra[part, tile, at] for part in range(2) for tile in tiles_of], axis=1
            )
            for tiles_of in (range(arms), range(arms, mid))
        ]
        stacked = jnp.concatenate([real, imag], axis=0)
        waves = jnp.dot(over_shots[...], stacked, preferred_element_type=f32)
        masked = jnp.concatenate(
            [waves[:shots] * keep[...], waves[shots:] * keep[...]], axis=0
        ).astype(bf16)
        at = slice(2 * rec * shots, 2 * (rec + 1) * shots)
        for tile in range(mid):
            waved[tile, at] = masked[:, tile * LANES : (tile + 1) * LANES]
    for rec in range(recs):
        at = slice(2 * rec * shots, 2 * (rec + 1) * shots)
        masked = jnp.concatenate([waved[tile, at] for tile in range(mid)], axis=1)
        again = jnp.dot(back[...], masked, preferred_element_type=f32).astype(bf16)
        at = slice(rec * slots, (rec + 1) * slots)
        for part in range(2):
            for arm in range(arms):
                tile = part * arms + arm
                columns = slice(tile * LANES, (tile + 1) * LANES)
                mixed[part, arm, at] = again[:slots, columns]
                mixed[part, arms + arm, at] = again[slots:, columns]
    table_copies[1].wait()
    for rec in range(0, recs, group):
        at = slice(rec * slots, (rec + group) * slots)
        even, odd = [
            product(
                jnp.concatenate([mixed[part, tile, at] for tile in range(mid)], axis=1),
                inverse,
                part,
            )
            for part in range(2)
        ]
        early, late = (even + odd).astype(bf16), (even - odd).astype(bf16)
        for tile in range(mid):
            columns = slice(tile * LANES, (tile + 1) * LANES)
            for half_at, found in ((tile, early), (tile + mid, late)):
                swapped[half_at, rec : rec + group] = found[:, columns].reshape(
                    group, slots, LANES
                )
    for tile in range(wide):
        for slot in range(0, slots, 16):
            ready[tile, slot : slot + 16] = jnp.swapaxes(
                swapped[tile, :, slot : slot + 16], 0, 1
            )
        copy = pltpu.make_async_copy(
            ready.at[tile],
            out.at[:, pl.ds(chunk * recs, recs), pl.ds(tile * LANES, LANES)],
            out_sem.at[tile],
        )
        copy.start()
        out_copies.append(copy)
    for copy in out_copies:
        copy.wait()


def filter_gathers(codes, here, traces, tables, chunk, chunks, filled):
    keep, over_shots, back, forward, inverse = tables
    peers = len(traces)
    recs, block_len = traces[0].shape
    rec_rows = recs * chunks
    shots, half = keep.shape
    window = 2 * half
    slots = 2 * shots // peers
    total = peers * block_len
    smem = pl.BlockSpec(memory_space=pltpu.SMEM)
    vmem = pl.BlockSpec(memory_space=pltpu.VMEM)
    anywhere = pl.BlockSpec(memory_space=pl.ANY)
    bf16 = jnp.bfloat16
    operands = [codes, here, *traces, keep, over_shots, back, forward, inverse]
    aliases = {}
    if chunk:
        aliases = {len(operands): 0}
        operands.append(filled)
    return pl.pallas_call(
        functools.partial(gather_kernel, peers, chunk),
        out_shape=jax.ShapeDtypeStruct((slots, rec_rows, window), bf16),
        in_specs=[smem, smem] + [vmem] * (peers + 3) + [anywhere] * (2 + (chunk > 0)),
        out_specs=anywhere,
        scratch_shapes=[
            pltpu.VMEM(forward.shape, bf16),
            pltpu.VMEM(inverse.shape, bf16),
            pltpu.VMEM(((total + window) // LANES, recs, LANES), bf16),
            pltpu.VMEM((2, half // LANES, recs, shots, LANES), bf16),
            pltpu.VMEM((2, half // LANES, recs * shots, LANES), bf16),
            pltpu.VMEM((half // LANES, 2 * recs * shots, LANES), bf16),
            pltpu.VMEM((2, half // LANES, recs * slots, LANES), bf16),
            pltpu.VMEM((window // LANES, recs, slots, LANES), bf16),
            pltpu.VMEM((window // LANES, slots, recs, LANES), bf16),
            pltpu.SemaphoreType.DMA((2,)),
            pltpu.SemaphoreType.DMA((window // LANES,)),
        ],
        input_output_aliases=aliases,
        compiler_params=pltpu.CompilerParams(vmem_limit_bytes=60 << 20),
        cost_estimate=pl.CostEstimate(flops=0, bytes_accessed=20 << 20, transcendentals=0),
    )(*operands)


def on_device(station_traces, shot_onset_ticks, span_place_index, spectral_keep_flags):
    shots, half = spectral_keep_flags.shape
    forward, inverse, over_shots, back_rows, order = make_tables(2 * half, shots)
    peers = lax.axis_size("tm")
    lines = lax.axis_size("line")
    chunks = station_traces.shape[0] // RECS
    gathered = []
    for chunk in range(chunks):
        part = station_traces[chunk * RECS : (chunk + 1) * RECS]
        gathered.append(
            [part]
            + [
                lax.ppermute(
                    part, "tm", [(partner(index, away, peers), index) for index in range(peers)]
                )
                for away in range(1, peers)
            ]
        )
    codes = jnp.concatenate([shot_onset_ticks, span_place_index])
    codes = jnp.broadcast_to(codes[None], (lines, codes.shape[0]))
    codes = lax.all_to_all(codes, "line", split_axis=0, concat_axis=0, tiled=True)
    here = jnp.stack([lax.axis_index("tm"), station_traces.shape[1]]).astype(jnp.int32)
    keep, back = plan_shots(
        codes, here, spectral_keep_flags, order, back_rows, 2 * shots // peers
    )
    tables = [keep, over_shots, back, forward, inverse]
    filled = None
    for chunk in range(chunks):
        filled = filter_gathers(codes, here, gathered[chunk], tables, chunk, chunks, filled)
    return filled


def solution(mesh):
    in_specs = (P("line", "tm"), P("line"), P("line"), P())
    out_specs = P("tm", "line", None)
    return jax.shard_map(
        on_device, mesh=mesh, in_specs=in_specs, out_specs=out_specs, check_vma=False
    )
```

```python
import functools
import math

import jax
import jax.numpy as jnp
import ml_dtypes
import numpy as np
from jax import lax
from jax.experimental import pallas as pl
from jax.experimental.pallas import tpu as pltpu
from jax.sharding import PartitionSpec as P

LANES = 128
BLOCK = 16


def make_tables(window, shots):
    half = window // 2
    quarter = half // 2
    times = np.arange(half)
    freqs = np.concatenate([np.arange(0, half, 2), np.arange(1, half, 2)])

    def waves(rows, columns, period):
        phase = (rows[:, None] * columns[None, :] % period) * (2.0 * math.pi / period)
        return np.cos(phase), np.sin(phase)

    bf16 = ml_dtypes.bfloat16
    cosine, sine = waves(times, freqs, window)
    forward = np.stack(
        [
            np.concatenate([cosine[:, cut], -sine[:, cut]], axis=1)
            for cut in (slice(0, quarter), slice(quarter, half))
        ]
    ).astype(bf16)
    gain = np.where(freqs == 0, 0.5, 1.0)[:, None] * (2.0 / (window * shots))
    inverse = np.stack(
        [
            np.concatenate([gain[cut] * cosine.T[cut], -gain[cut] * sine.T[cut]], axis=0)
            for cut in (slice(0, quarter), slice(quarter, half))
        ]
    ).astype(bf16)
    turn_cos, turn_sin = waves(np.arange(shots), np.arange(shots), shots)
    forward, inverse = [
        table.reshape(2, half, half // LANES, LANES).swapaxes(1, 2) for table in (forward, inverse)
    ]
    over_shots = np.block([[turn_cos, turn_sin], [-turn_sin, turn_cos]]).astype(bf16)
    back_rows = np.stack(
        [
            np.concatenate([turn_cos, -turn_sin], axis=1),
            np.concatenate([turn_sin, turn_cos], axis=1),
        ]
    ).astype(bf16)
    order = np.zeros((half, half), bf16)
    order[freqs, np.arange(half)] = 1
    return forward, inverse, over_shots, back_rows, order


def partner(index, away, count):
    if count & (count - 1) == 0:
        return index ^ away
    return (index + away) % count


def gather_kernel(peers, recs, *refs):
    ticks, places, *refs = refs
    share = ticks.shape[1]
    traces, refs = refs[:peers], refs[peers:]
    flags, over_shots, back_rows = refs[:3]
    table_refs, out = refs[3:6], refs[6]
    forward, inverse, order, tiles, folds, spectra, waved, mixed, swapped, ready = refs[7:17]
    table_sem, out_sem = refs[17:]
    rec_rows, block_len = traces[0].shape
    shots, half = flags.shape
    window = 2 * half
    slots = ready.shape[1]
    wide = window // LANES
    mid = wide // 2
    arms = mid // 2
    per_block = block_len // LANES
    f32, bf16 = jnp.float32, jnp.bfloat16
    here = lax.axis_index("tm")

    table_copies = [
        pltpu.make_async_copy(table, place, table_sem.at[index])
        for index, (table, place) in enumerate(zip(table_refs, (forward, inverse, order)))
    ]
    for index in (0, 2, 1):
        table_copies[index].start()

    for away, block in enumerate(traces):
        base = partner(here, away, peers) * per_block
        for tile in range(per_block):
            tiles[base + tile] = block[:, tile * LANES : (tile + 1) * LANES]
    for tile in range(wide):
        tiles[peers * per_block + tile] = jnp.zeros((rec_rows, LANES), bf16)

    lane = lax.broadcasted_iota(jnp.int16, (recs, LANES), 1)

    def cut(shot, rows):
        tick = ticks[shot // share, shot % share]
        first = lax.shift_right_logical(tick, LANES.bit_length() - 1)
        within = tick & (LANES - 1)
        piece = [tiles[first + tile, rows] for tile in range(wide + 1)]
        early = lane < within.astype(jnp.int16)
        piece = [jnp.where(early, piece[tile + 1], piece[tile]) for tile in range(wide)]
        turn = (LANES - within) & (LANES - 1)
        sums = [pltpu.roll(piece[tile] + piece[tile + mid], turn, 1) for tile in range(mid)]
        gaps = [pltpu.roll(piece[tile] - piece[tile + mid], turn, 1) for tile in range(mid)]
        return sums, gaps

    def cut_block(block, rows):
        cuts = [cut(shot, rows) for shot in range(block * BLOCK, (block + 1) * BLOCK)]
        for part in range(2):
            for tile in range(mid):
                panel = jnp.stack([cuts[item][part][tile] for item in range(BLOCK)])
                folds[block % 2, part, tile] = jnp.swapaxes(panel, 0, 1)

    def product(left, right, part):
        return jnp.dot(
            jnp.concatenate(left, axis=1),
            jnp.concatenate([right[part, tile] for tile in range(mid)], axis=1),
            preferred_element_type=f32,
        )

    def columns(tile):
        return slice(tile * LANES, (tile + 1) * LANES)

    def transform_block(block):
        for part in range(2):
            panel = [folds[block % 2, part, tile].reshape(recs * BLOCK, LANES) for tile in range(mid)]
            found = product(panel, forward, part).astype(bf16)
            for tile in range(mid):
                spectra[part, tile, :, block * BLOCK : (block + 1) * BLOCK] = found[
                    :, columns(tile)
                ].reshape(recs, BLOCK, LANES)

    def over(rec, keep):
        stacked = jnp.concatenate(
            [
                jnp.concatenate(
                    [spectra[part, tile, rec] for part in range(2) for tile in which], axis=1
                )
                for which in (range(arms), range(arms, mid))
            ],
            axis=0,
        )
        waves = jnp.dot(over_shots[...], stacked, preferred_element_type=f32)
        masked = jnp.concatenate([waves[:shots] * keep, waves[shots:] * keep], axis=0).astype(bf16)
        for tile in range(mid):
            waved[rec % 4, tile] = masked[:, columns(tile)]

    def under(rec, back):
        masked = jnp.concatenate([waved[rec % 4, tile] for tile in range(mid)], axis=1)
        again = jnp.dot(back, masked, preferred_element_type=f32).astype(bf16)
        for part in range(2):
            for arm in range(arms):
                at = columns(part * arms + arm)
                mixed[part, arm, rec] = again[:slots, at]
                mixed[part, arms + arm, rec] = again[slots:, at]

    group = 8

    def restore(first):
        even, odd = [
            product(
                [
                    mixed[part, tile, first : first + group].reshape(group * slots, LANES)
                    for tile in range(mid)
                ],
                inverse,
                part,
            )
            for part in range(2)
        ]
        early, late = (even + odd).astype(bf16), (even - odd).astype(bf16)
        for tile in range(mid):
            for to, found in ((tile, early), (tile + mid, late)):
                swapped[to, first : first + group] = found[:, columns(tile)].reshape(
                    group, slots, LANES
                )

    out_copies = []

    def send(chunk, first):
        base = chunk * recs + first
        for tile in range(wide):
            for slot in range(0, slots, BLOCK):
                ready[tile, slot : slot + BLOCK, base : base + BLOCK] = jnp.swapaxes(
                    swapped[tile, first : first + BLOCK, slot : slot + BLOCK], 0, 1
                )
        copies = [
            pltpu.make_async_copy(
                ready.at[tile, :, pl.ds(base, BLOCK)],
                out.at[:, pl.ds(base, BLOCK), pl.ds(tile * LANES, LANES)],
                out_sem.at[base // BLOCK, tile],
            )
            for tile in range(wide)
        ]
        for copy in copies:
            copy.start()
        out_copies.extend(copies)

    shot_lane = lax.broadcasted_iota(jnp.int32, (1, shots), 1)
    place_all = jnp.full((1, shots), -1, jnp.int32)
    for shot in range(shots):
        tick = ticks[shot // share, shot % share]
        mine = (tick >= here * block_len) & (tick < (here + 1) * block_len)
        place = jnp.where(mine, places[shot // share, shot % share], -1)
        place_all = jnp.where(shot_lane == shot, place, place_all)
    slot_row = lax.broadcasted_iota(jnp.int32, (slots, shots), 0)
    owned = (slot_row == place_all).astype(f32).astype(bf16)

    blocks = shots // BLOCK
    for chunk in range(rec_rows // recs):
        rows = slice(chunk * recs, (chunk + 1) * recs)
        cut_block(0, rows)
        if chunk == 0:
            back = jnp.concatenate(
                [jnp.dot(owned, back_rows[part], preferred_element_type=f32) for part in range(2)],
                axis=0,
            ).astype(bf16)
            table_copies[0].wait()
        for block in range(blocks):
            if block + 1 < blocks:
                cut_block(block + 1, rows)
            transform_block(block)
        if chunk == 0:
            table_copies[2].wait()
            keep = jnp.dot(
                flags[...].astype(f32).astype(bf16), order[...], preferred_element_type=f32
            )
        over(0, keep)
        for rec in range(recs):
            if rec + 1 < recs:
                over(rec + 1, keep)
            under(rec, back)
            if chunk == 0 and rec == group:
                table_copies[1].wait()
            if rec % group == 1 and rec > group:
                restore(rec - group - 1)
            if rec % BLOCK == 2 and rec > BLOCK:
                send(chunk, rec - BLOCK - 2)
        restore(recs - group)
        send(chunk, recs - BLOCK)
    for copy in out_copies:
        copy.wait()


def filter_gathers(codes, traces, flags, tables):
    forward, inverse, over_shots, back_rows, order = tables
    peers = len(traces)
    rec_rows, block_len = traces[0].shape
    shots, half = flags.shape
    window = 2 * half
    slots = 2 * shots // peers
    total = peers * block_len
    recs = rec_rows if shots * rec_rows * window <= 4 << 20 else BLOCK
    smem = pl.BlockSpec(memory_space=pltpu.SMEM)
    vmem = pl.BlockSpec(memory_space=pltpu.VMEM)
    anywhere = pl.BlockSpec(memory_space=pl.ANY)
    flops = 2 * rec_rows * (
        shots * window * half
        + slots * window * half
        + 4 * shots * shots * half
        + 4 * slots * shots * half
    )
    bf16 = jnp.bfloat16
    return pl.pallas_call(
        functools.partial(gather_kernel, peers, recs),
        out_shape=jax.ShapeDtypeStruct((slots, rec_rows, window), bf16),
        in_specs=[smem, smem] + [vmem] * (peers + 3) + [anywhere] * 3,
        out_specs=anywhere,
        scratch_shapes=[
            pltpu.VMEM(forward.shape, bf16),
            pltpu.VMEM(inverse.shape, bf16),
            pltpu.VMEM(order.shape, bf16),
            pltpu.VMEM(((total + window) // LANES, rec_rows, LANES), bf16),
            pltpu.VMEM((2, 2, half // LANES, recs, BLOCK, LANES), bf16),
            pltpu.VMEM((2, half // LANES, recs, shots, LANES), bf16),
            pltpu.VMEM((4, half // LANES, 2 * shots, LANES), bf16),
            pltpu.VMEM((2, half // LANES, recs, slots, LANES), bf16),
            pltpu.VMEM((window // LANES, recs, slots, LANES), bf16),
            pltpu.VMEM((window // LANES, slots, rec_rows, LANES), bf16),
            pltpu.SemaphoreType.DMA((3,)),
            pltpu.SemaphoreType.DMA((rec_rows // BLOCK, window // LANES)),
        ],
        compiler_params=pltpu.CompilerParams(vmem_limit_bytes=60 << 20),
        cost_estimate=pl.CostEstimate(
            flops=flops,
            bytes_accessed=2 * rec_rows * (total + slots * window),
            transcendentals=0,
        ),
    )(*codes, *traces, flags, over_shots, back_rows, forward, inverse, order)


def on_device(station_traces, shot_onset_ticks, span_place_index, spectral_keep_flags):
    shots, half = spectral_keep_flags.shape
    tables = make_tables(2 * half, shots)
    peers = lax.axis_size("tm")
    lines = lax.axis_size("line")
    traces = [station_traces] + [
        lax.ppermute(
            station_traces,
            "tm",
            [(partner(index, away, peers), index) for index in range(peers)],
        )
        for away in range(1, peers)
    ]
    share = shots // lines
    row = lax.broadcasted_iota(jnp.int32, (lines, share), 0)
    own = row == lax.axis_index("line")
    codes = lax.psum(
        [jnp.where(own, part[None], 0) for part in (shot_onset_ticks, span_place_index)], "line"
    )
    return filter_gathers(codes, traces, spectral_keep_flags, tables)


def solution(mesh):
    in_specs = (P("line", "tm"), P("line"), P("line"), P())
    out_specs = P("tm", "line", None)
    return jax.shard_map(
        on_device, mesh=mesh, in_specs=in_specs, out_specs=out_specs, check_vma=False
    )
```

```python
import functools
import math

import jax
import jax.numpy as jnp
import ml_dtypes
import numpy as np
from jax import lax
from jax.experimental import pallas as pl
from jax.experimental.pallas import tpu as pltpu
from jax.sharding import PartitionSpec as P

LANES = 128
BLOCK = 16


def make_tables(window, shots):
    half = window // 2
    quarter = half // 2
    times = np.arange(half)
    freqs = np.concatenate([np.arange(0, half, 2), np.arange(1, half, 2)])

    def waves(rows, columns, period):
        phase = (rows[:, None] * columns[None, :] % period) * (2.0 * math.pi / period)
        return np.cos(phase), np.sin(phase)

    bf16 = ml_dtypes.bfloat16
    cosine, sine = waves(times, freqs, window)
    forward = np.stack(
        [
            np.concatenate([cosine[:, cut], -sine[:, cut]], axis=1)
            for cut in (slice(0, quarter), slice(quarter, half))
        ]
    ).astype(bf16)
    gain = np.where(freqs == 0, 0.5, 1.0)[:, None] * (2.0 / (window * shots))
    inverse = np.stack(
        [
            np.concatenate([gain[cut] * cosine.T[cut], -gain[cut] * sine.T[cut]], axis=0)
            for cut in (slice(0, quarter), slice(quarter, half))
        ]
    ).astype(bf16)
    turn_cos, turn_sin = waves(np.arange(shots), np.arange(shots), shots)
    forward, inverse = [
        table.reshape(2, half, half // LANES, LANES).swapaxes(1, 2) for table in (forward, inverse)
    ]
    over_shots = np.block([[turn_cos, turn_sin], [-turn_sin, turn_cos]]).astype(bf16)
    back_rows = np.stack(
        [
            np.concatenate([turn_cos, -turn_sin], axis=1),
            np.concatenate([turn_sin, turn_cos], axis=1),
        ]
    ).astype(bf16)
    order = np.zeros((half, half), bf16)
    order[freqs, np.arange(half)] = 1
    return forward, inverse, over_shots, back_rows, order


def partner(index, away, count):
    if count & (count - 1) == 0:
        return index ^ away
    return (index + away) % count


def gather_kernel(peers, recs, *refs):
    ticks, places, *refs = refs
    share = ticks.shape[1]
    traces, refs = refs[:peers], refs[peers:]
    table_refs, out, loaded, refs = refs[:6], refs[6], refs[7:14], refs[14:]
    own, forward, inverse, order, flags, over_shots, back_rows = loaded
    tiles, folds, spectra, waved, mixed, swapped, ready, table_sem, out_sem = refs
    rec_rows, block_len = traces[0].shape
    shots, half = flags.shape
    window = 2 * half
    slots = ready.shape[1]
    wide = window // LANES
    mid = wide // 2
    arms = mid // 2
    per_block = block_len // LANES
    f32, bf16 = jnp.float32, jnp.bfloat16
    here = lax.axis_index("tm")

    table_copies = [
        pltpu.make_async_copy(table, place, table_sem.at[index])
        for index, (table, place) in enumerate(zip((traces[0], *table_refs), loaded))
    ]
    for index in (0, 6, 1, 4, 3, 5, 2):
        table_copies[index].start()

    table_copies[0].wait()
    for away, block in enumerate((own, *traces[1:])):
        base = partner(here, away, peers) * per_block
        for tile in range(per_block):
            tiles[base + tile] = block[:, tile * LANES : (tile + 1) * LANES]
    for tile in range(wide):
        tiles[peers * per_block + tile] = jnp.zeros((rec_rows, LANES), bf16)

    lane = lax.broadcasted_iota(jnp.int16, (recs, LANES), 1)

    def cut(shot, rows):
        tick = ticks[shot // share, shot % share]
        first = lax.shift_right_logical(tick, LANES.bit_length() - 1)
        within = tick & (LANES - 1)
        piece = [tiles[first + tile, rows] for tile in range(wide + 1)]
        early = lane < within.astype(jnp.int16)
        piece = [jnp.where(early, piece[tile + 1], piece[tile]) for tile in range(wide)]
        turn = (LANES - within) & (LANES - 1)
        sums = [pltpu.roll(piece[tile] + piece[tile + mid], turn, 1) for tile in range(mid)]
        gaps = [pltpu.roll(piece[tile] - piece[tile + mid], turn, 1) for tile in range(mid)]
        return sums, gaps

    def cut_block(block, rows):
        cuts = [cut(shot, rows) for shot in range(block * BLOCK, (block + 1) * BLOCK)]
        for part in range(2):
            for tile in range(mid):
                panel = jnp.stack([cuts[item][part][tile] for item in range(BLOCK)])
                folds[block % 2, part, tile] = jnp.swapaxes(panel, 0, 1)

    def product(left, right, part):
        return jnp.dot(
            jnp.concatenate(left, axis=1),
            jnp.concatenate([right[part, tile] for tile in range(mid)], axis=1),
            preferred_element_type=f32,
        )

    def columns(tile):
        return slice(tile * LANES, (tile + 1) * LANES)

    def transform_block(block):
        for part in range(2):
            panel = [folds[block % 2, part, tile].reshape(recs * BLOCK, LANES) for tile in range(mid)]
            found = product(panel, forward, part).astype(bf16)
            for tile in range(mid):
                spectra[part, tile, :, block * BLOCK : (block + 1) * BLOCK] = found[
                    :, columns(tile)
                ].reshape(recs, BLOCK, LANES)

    def over(rec, keep):
        stacked = jnp.concatenate(
            [
                jnp.concatenate(
                    [spectra[part, tile, rec] for part in range(2) for tile in which], axis=1
                )
                for which in (range(arms), range(arms, mid))
            ],
            axis=0,
        )
        waves = jnp.dot(over_shots[...], stacked, preferred_element_type=f32)
        masked = jnp.concatenate([waves[:shots] * keep, waves[shots:] * keep], axis=0).astype(bf16)
        for tile in range(mid):
            waved[tile, rec] = masked[:, columns(tile)]

    def under(rec, back):
        masked = jnp.concatenate([waved[tile, rec] for tile in range(mid)], axis=1)
        again = jnp.dot(back, masked, preferred_element_type=f32).astype(bf16)
        for part in range(2):
            for arm in range(arms):
                at = columns(part * arms + arm)
                mixed[part, arm, rec] = again[:slots, at]
                mixed[part, arms + arm, rec] = again[slots:, at]

    group = 8

    def restore(first):
        even, odd = [
            product(
                [
                    mixed[part, tile, first : first + group].reshape(group * slots, LANES)
                    for tile in range(mid)
                ],
                inverse,
                part,
            )
            for part in range(2)
        ]
        early, late = (even + odd).astype(bf16), (even - odd).astype(bf16)
        for tile in range(mid):
            for to, found in ((tile, early), (tile + mid, late)):
                swapped[to, first : first + group] = found[:, columns(tile)].reshape(
                    group, slots, LANES
                )

    out_copies = []

    def send(chunk, first):
        base = chunk * recs + first
        for tile in range(wide):
            for slot in range(0, slots, BLOCK):
                ready[tile, slot : slot + BLOCK, base : base + BLOCK] = jnp.swapaxes(
                    swapped[tile, first : first + BLOCK, slot : slot + BLOCK], 0, 1
                )
        copies = [
            pltpu.make_async_copy(
                ready.at[tile, :, pl.ds(base, BLOCK)],
                out.at[:, pl.ds(base, BLOCK), pl.ds(tile * LANES, LANES)],
                out_sem.at[base // BLOCK, tile],
            )
            for tile in range(wide)
        ]
        for copy in copies:
            copy.start()
        out_copies.extend(copies)

    shot_lane = lax.broadcasted_iota(jnp.int32, (1, shots), 1)
    place_all = jnp.full((1, shots), -1, jnp.int32)
    for shot in range(shots):
        tick = ticks[shot // share, shot % share]
        mine = (tick >= here * block_len) & (tick < (here + 1) * block_len)
        place = jnp.where(mine, places[shot // share, shot % share], -1)
        place_all = jnp.where(shot_lane == shot, place, place_all)
    slot_row = lax.broadcasted_iota(jnp.int32, (slots, shots), 0)
    owned = (slot_row == place_all).astype(f32).astype(bf16)

    blocks = shots // BLOCK
    for chunk in range(rec_rows // recs):
        rows = slice(chunk * recs, (chunk + 1) * recs)
        cut_block(0, rows)
        if chunk == 0:
            table_copies[6].wait()
            back = jnp.concatenate(
                [jnp.dot(owned, back_rows[part], preferred_element_type=f32) for part in range(2)],
                axis=0,
            ).astype(bf16)
            table_copies[1].wait()
        for block in range(blocks):
            if block + 1 < blocks:
                cut_block(block + 1, rows)
            transform_block(block)
        if chunk == 0:
            for index in (3, 4, 5):
                table_copies[index].wait()
            keep = jnp.dot(
                flags[...].astype(f32).astype(bf16), order[...], preferred_element_type=f32
            )
        for rec in range(recs):
            over(rec, keep)
        for rec in range(recs):
            under(rec, back)
        if chunk == 0:
            table_copies[2].wait()
        for first in range(0, recs, group):
            restore(first)
        for first in range(0, recs, BLOCK):
            send(chunk, first)
    for copy in out_copies:
        copy.wait()


def filter_gathers(codes, traces, flags, tables):
    forward, inverse, over_shots, back_rows, order = tables
    peers = len(traces)
    rec_rows, block_len = traces[0].shape
    shots, half = flags.shape
    window = 2 * half
    slots = 2 * shots // peers
    total = peers * block_len
    recs = rec_rows if shots * rec_rows * window <= 4 << 20 else BLOCK
    smem = pl.BlockSpec(memory_space=pltpu.SMEM)
    vmem = pl.BlockSpec(memory_space=pltpu.VMEM)
    hbm = pl.BlockSpec(memory_space=pltpu.HBM)
    flops = 2 * rec_rows * (
        shots * window * half
        + slots * window * half
        + 4 * shots * shots * half
        + 4 * slots * shots * half
    )
    bf16 = jnp.bfloat16
    shared = [forward, inverse, order, flags, over_shots, back_rows]
    return pl.pallas_call(
        functools.partial(gather_kernel, peers, recs),
        out_shape=jax.ShapeDtypeStruct((slots, rec_rows, window), bf16),
        in_specs=[smem, smem, hbm] + [vmem] * (peers - 1) + [hbm] * 6,
        out_specs=hbm,
        scratch_shapes=[
            pltpu.VMEM((rec_rows, block_len), bf16),
            *[pltpu.VMEM(table.shape, table.dtype) for table in shared],
            pltpu.VMEM(((total + window) // LANES, rec_rows, LANES), bf16),
            pltpu.VMEM((2, 2, half // LANES, recs, BLOCK, LANES), bf16),
            pltpu.VMEM((2, half // LANES, recs, shots, LANES), bf16),
            pltpu.VMEM((half // LANES, recs, 2 * shots, LANES), bf16),
            pltpu.VMEM((2, half // LANES, recs, slots, LANES), bf16),
            pltpu.VMEM((window // LANES, recs, slots, LANES), bf16),
            pltpu.VMEM((window // LANES, slots, rec_rows, LANES), bf16),
            pltpu.SemaphoreType.DMA((7,)),
            pltpu.SemaphoreType.DMA((rec_rows // BLOCK, window // LANES)),
        ],
        compiler_params=pltpu.CompilerParams(vmem_limit_bytes=60 << 20),
        cost_estimate=pl.CostEstimate(
            flops=flops,
            bytes_accessed=2 * rec_rows * (total + slots * window),
            transcendentals=0,
        ),
    )(*codes, *traces, *shared)


def on_device(station_traces, shot_onset_ticks, span_place_index, spectral_keep_flags):
    shots, half = spectral_keep_flags.shape
    tables = make_tables(2 * half, shots)
    peers = lax.axis_size("tm")
    lines = lax.axis_size("line")
    traces = [station_traces] + [
        lax.ppermute(
            station_traces,
            "tm",
            [(partner(index, away, peers), index) for index in range(peers)],
        )
        for away in range(1, peers)
    ]
    share = shots // lines
    row = lax.broadcasted_iota(jnp.int32, (lines, share), 0)
    own = row == lax.axis_index("line")
    codes = lax.psum(
        [jnp.where(own, part[None], 0) for part in (shot_onset_ticks, span_place_index)], "line"
    )
    return filter_gathers(codes, traces, spectral_keep_flags, tables)


def solution(mesh):
    in_specs = (P("line", "tm"), P("line"), P("line"), P())
    out_specs = P("tm", "line", None)
    return jax.shard_map(
        on_device, mesh=mesh, in_specs=in_specs, out_specs=out_specs, check_vma=False
    )
```

```python
import functools
import math

import jax
import jax.numpy as jnp
import ml_dtypes
import numpy as np
from jax import lax
from jax.experimental import pallas as pl
from jax.experimental.pallas import tpu as pltpu
from jax.sharding import PartitionSpec as P

LANES = 128
BLOCK = 16


def make_tables(window, shots):
    half = window // 2
    quarter = half // 2
    times = np.arange(half)
    freqs = np.concatenate([np.arange(0, half, 2), np.arange(1, half, 2)])

    def waves(rows, columns, period):
        phase = (rows[:, None] * columns[None, :] % period) * (2.0 * math.pi / period)
        return np.cos(phase), np.sin(phase)

    bf16 = ml_dtypes.bfloat16
    cosine, sine = waves(times, freqs, window)
    forward = np.stack(
        [
            np.concatenate([cosine[:, cut], -sine[:, cut]], axis=1)
            for cut in (slice(0, quarter), slice(quarter, half))
        ]
    ).astype(bf16)
    gain = np.where(freqs == 0, 0.5, 1.0)[:, None] * (2.0 / (window * shots))
    inverse = np.stack(
        [
            np.concatenate([gain[cut] * cosine.T[cut], -gain[cut] * sine.T[cut]], axis=0)
            for cut in (slice(0, quarter), slice(quarter, half))
        ]
    ).astype(bf16)
    turn_cos, turn_sin = waves(np.arange(shots), np.arange(shots), shots)
    forward, inverse = [
        table.reshape(2, half, half // LANES, LANES).swapaxes(1, 2) for table in (forward, inverse)
    ]
    over_shots = np.block([[turn_cos, turn_sin], [-turn_sin, turn_cos]]).astype(bf16)
    back_rows = np.stack(
        [
            np.concatenate([turn_cos, -turn_sin], axis=1),
            np.concatenate([turn_sin, turn_cos], axis=1),
        ]
    ).astype(bf16)
    order = np.zeros((half, half), bf16)
    order[freqs, np.arange(half)] = 1
    return forward, inverse, over_shots, back_rows, order


def partner(index, away, count):
    if count & (count - 1) == 0:
        return index ^ away
    return (index + away) % count


def gather_kernel(peers, recs, *refs):
    ticks, places, *refs = refs
    share = ticks.shape[1]
    traces, refs = refs[:peers], refs[peers:]
    table_refs, out, loaded, refs = refs[:6], refs[6], refs[7:14], refs[14:]
    own, forward, inverse, order, flags, over_shots, back_rows = loaded
    tiles, folds, spectra, waved, mixed, ready, table_sem, out_sem = refs
    rec_rows, block_len = traces[0].shape
    shots, half = flags.shape
    window = 2 * half
    slots = ready.shape[0]
    pitch = recs + 1
    wide = window // LANES
    mid = wide // 2
    arms = mid // 2
    per_block = block_len // LANES
    f32, bf16 = jnp.float32, jnp.bfloat16
    here = lax.axis_index("tm")

    table_copies = [
        pltpu.make_async_copy(table, place, table_sem.at[index])
        for index, (table, place) in enumerate(zip((traces[0], *table_refs), loaded))
    ]
    for index in (0, 6, 1, 4, 3, 5, 2):
        table_copies[index].start()

    table_copies[0].wait()
    for away, block in enumerate((own, *traces[1:])):
        base = partner(here, away, peers) * per_block
        for tile in range(per_block):
            tiles[base + tile] = block[:, tile * LANES : (tile + 1) * LANES]
    for tile in range(wide):
        tiles[peers * per_block + tile] = jnp.zeros((rec_rows, LANES), bf16)

    lane = lax.broadcasted_iota(jnp.int16, (recs, LANES), 1)

    def cut(shot, rows):
        tick = ticks[shot // share, shot % share]
        first = lax.shift_right_logical(tick, LANES.bit_length() - 1)
        within = tick & (LANES - 1)
        piece = [tiles[first + tile, rows] for tile in range(wide + 1)]
        early = lane < within.astype(jnp.int16)
        piece = [jnp.where(early, piece[tile + 1], piece[tile]) for tile in range(wide)]
        turn = (LANES - within) & (LANES - 1)
        sums = [pltpu.roll(piece[tile] + piece[tile + mid], turn, 1) for tile in range(mid)]
        gaps = [pltpu.roll(piece[tile] - piece[tile + mid], turn, 1) for tile in range(mid)]
        return sums, gaps

    def cut_block(block, rows):
        for item in range(BLOCK):
            for part, tiles_of in enumerate(cut(block * BLOCK + item, rows)):
                for tile in range(mid):
                    folds[block % 2, part, tile, item * recs : (item + 1) * recs] = tiles_of[tile]

    def product(left, right, part):
        return jnp.dot(
            jnp.concatenate(left, axis=1),
            jnp.concatenate([right[part, tile] for tile in range(mid)], axis=1),
            preferred_element_type=f32,
        )

    def columns(tile):
        return slice(tile * LANES, (tile + 1) * LANES)

    def transform_block(block):
        for part in range(2):
            panel = [folds[block % 2, part, tile] for tile in range(mid)]
            found = product(panel, forward, part)
            for item in range(BLOCK):
                row = (block * BLOCK + item) * pitch
                for tile in range(mid):
                    spectra[part * mid + tile, row : row + recs] = found[
                        item * recs : (item + 1) * recs, columns(tile)
                    ]

    def over(rec, keep):
        at = pl.ds(rec, shots, stride=pitch)
        stacked = jnp.concatenate(
            [
                jnp.concatenate(
                    [
                        spectra[part * mid + tile, at].astype(bf16)
                        for part in range(2)
                        for tile in which
                    ],
                    axis=1,
                )
                for which in (range(arms), range(arms, mid))
            ],
            axis=0,
        )
        waves = jnp.dot(over_shots[...], stacked, preferred_element_type=f32)
        masked = jnp.concatenate([waves[:shots] * keep, waves[shots:] * keep], axis=0).astype(bf16)
        for tile in range(mid):
            waved[tile, rec] = masked[:, columns(tile)]

    def under(rec, back):
        masked = jnp.concatenate([waved[tile, rec] for tile in range(mid)], axis=1)
        again = jnp.dot(back, masked, preferred_element_type=f32)
        to = pl.ds(rec, slots, stride=pitch)
        for part in range(2):
            for arm in range(arms):
                at = columns(part * arms + arm)
                mixed[part * mid + arm, to] = again[:slots, at]
                mixed[part * mid + arms + arm, to] = again[slots:, at]

    group = min(slots, 256 // recs)
    out_copies = []

    def restore(chunk, first):
        even, odd = [
            product(
                [
                    jnp.concatenate(
                        [
                            mixed[part * mid + tile, slot * pitch : slot * pitch + recs].astype(bf16)
                            for slot in range(first, first + group)
                        ],
                        axis=0,
                    )
                    for tile in range(mid)
                ],
                inverse,
                part,
            )
            for part in range(2)
        ]
        rows = slice(chunk * recs, (chunk + 1) * recs)
        early, late = (even + odd).astype(bf16), (even - odd).astype(bf16)
        ready[first : first + group, rows, :half] = early.reshape(group, recs, half)
        ready[first : first + group, rows, half:] = late.reshape(group, recs, half)
        block = (pl.ds(first, group), pl.ds(chunk * recs, recs))
        copy = pltpu.make_async_copy(
            ready.at[block], out.at[block], out_sem.at[chunk, first // group]
        )
        copy.start()
        out_copies.append(copy)

    shot_lane = lax.broadcasted_iota(jnp.int32, (1, shots), 1)
    place_all = jnp.full((1, shots), -1, jnp.int32)
    for shot in range(shots):
        tick = ticks[shot // share, shot % share]
        mine = (tick >= here * block_len) & (tick < (here + 1) * block_len)
        place = jnp.where(mine, places[shot // share, shot % share], -1)
        place_all = jnp.where(shot_lane == shot, place, place_all)
    slot_row = lax.broadcasted_iota(jnp.int32, (slots, shots), 0)
    owned = (slot_row == place_all).astype(f32).astype(bf16)

    blocks = shots // BLOCK
    for chunk in range(rec_rows // recs):
        rows = slice(chunk * recs, (chunk + 1) * recs)
        cut_block(0, rows)
        if chunk == 0:
            table_copies[6].wait()
            back = jnp.concatenate(
                [jnp.dot(owned, back_rows[part], preferred_element_type=f32) for part in range(2)],
                axis=0,
            ).astype(bf16)
            table_copies[1].wait()
        for block in range(blocks):
            if block + 1 < blocks:
                cut_block(block + 1, rows)
            transform_block(block)
        if chunk == 0:
            for index in (3, 4, 5):
                table_copies[index].wait()
            keep = jnp.dot(
                flags[...].astype(f32).astype(bf16), order[...], preferred_element_type=f32
            )
        for rec in range(recs):
            over(rec, keep)
        for rec in range(recs):
            under(rec, back)
        if chunk == 0:
            table_copies[2].wait()
        for first in range(0, slots, group):
            restore(chunk, first)
    for copy in out_copies:
        copy.wait()


def filter_gathers(codes, traces, flags, tables):
    forward, inverse, over_shots, back_rows, order = tables
    peers = len(traces)
    rec_rows, block_len = traces[0].shape
    shots, half = flags.shape
    window = 2 * half
    slots = 2 * shots // peers
    total = peers * block_len
    recs = rec_rows if shots * rec_rows * window <= 4 << 20 else BLOCK
    smem = pl.BlockSpec(memory_space=pltpu.SMEM)
    vmem = pl.BlockSpec(memory_space=pltpu.VMEM)
    hbm = pl.BlockSpec(memory_space=pltpu.HBM)
    flops = 2 * rec_rows * (
        shots * window * half
        + slots * window * half
        + 4 * shots * shots * half
        + 4 * slots * shots * half
    )
    bf16 = jnp.bfloat16
    shared = [forward, inverse, order, flags, over_shots, back_rows]
    return pl.pallas_call(
        functools.partial(gather_kernel, peers, recs),
        out_shape=jax.ShapeDtypeStruct((slots, rec_rows, window), bf16),
        in_specs=[smem, smem, hbm] + [vmem] * (peers - 1) + [hbm] * 6,
        out_specs=hbm,
        scratch_shapes=[
            pltpu.VMEM((rec_rows, block_len), bf16),
            *[pltpu.VMEM(table.shape, table.dtype) for table in shared],
            pltpu.VMEM(((total + window) // LANES, rec_rows, LANES), bf16),
            pltpu.VMEM((2, 2, half // LANES, BLOCK * recs, LANES), bf16),
            pltpu.VMEM((window // LANES, shots * (recs + 1), LANES), jnp.float32),
            pltpu.VMEM((half // LANES, recs, 2 * shots, LANES), bf16),
            pltpu.VMEM((window // LANES, slots * (recs + 1), LANES), jnp.float32),
            pltpu.VMEM((slots, rec_rows, window), bf16),
            pltpu.SemaphoreType.DMA((7,)),
            pltpu.SemaphoreType.DMA((rec_rows // recs, slots)),
        ],
        compiler_params=pltpu.CompilerParams(vmem_limit_bytes=60 << 20),
        cost_estimate=pl.CostEstimate(
            flops=flops,
            bytes_accessed=2 * rec_rows * (total + slots * window),
            transcendentals=0,
        ),
    )(*codes, *traces, *shared)


def on_device(station_traces, shot_onset_ticks, span_place_index, spectral_keep_flags):
    shots, half = spectral_keep_flags.shape
    tables = make_tables(2 * half, shots)
    peers = lax.axis_size("tm")
    lines = lax.axis_size("line")
    traces = [station_traces] + [
        lax.ppermute(
            station_traces,
            "tm",
            [(partner(index, away, peers), index) for index in range(peers)],
        )
        for away in range(1, peers)
    ]
    share = shots // lines
    row = lax.broadcasted_iota(jnp.int32, (lines, share), 0)
    own = row == lax.axis_index("line")
    codes = lax.psum(
        [jnp.where(own, part[None], 0) for part in (shot_onset_ticks, span_place_index)], "line"
    )
    return filter_gathers(codes, traces, spectral_keep_flags, tables)


def solution(mesh):
    in_specs = (P("line", "tm"), P("line"), P("line"), P())
    out_specs = P("tm", "line", None)
    return jax.shard_map(
        on_device, mesh=mesh, in_specs=in_specs, out_specs=out_specs, check_vma=False
    )
```

```python
import functools
import math

import jax
import jax.numpy as jnp
import ml_dtypes
import numpy as np
from jax import lax
from jax.experimental import pallas as pl
from jax.experimental.pallas import tpu as pltpu
from jax.sharding import PartitionSpec as P

LANES = 128
BLOCK = 16


def make_tables(window, shots):
    half = window // 2
    quarter, eighth = window // 4, window // 8
    bf16 = ml_dtypes.bfloat16

    def waves(rows, columns, period):
        phase = (rows[:, None] * columns[None, :] % period) * (2.0 * math.pi / period)
        return np.cos(phase), np.sin(phase)

    classes = [np.arange(first, half, 4) for first in (0, 2)]
    classes += [
        np.concatenate([np.arange(first, half, 8) for first in pair]) for pair in ((1, 7), (3, 5))
    ]
    freqs = np.concatenate(classes)
    forward, inverse = [], []
    for part, found in enumerate(classes):
        gain = np.where(found == 0, 0.5, 1.0)[:, None] * (2.0 / (window * shots))
        if part < 2:
            cosine, sine = waves(np.arange(quarter), found, window)
            forward.append(np.concatenate([cosine, -sine], axis=1))
            inverse.append(np.concatenate([gain * cosine.T, -gain * sine.T], axis=0))
            continue
        cosine, sine = waves(np.arange(eighth), found, window)
        turn = np.where(found % 8 < 4, 1.0, -1.0)
        way = -turn if part == 2 else turn
        forward.append(np.block([[cosine, -sine], [way * sine, way * cosine]]))
        inverse.append(
            np.block(
                [
                    [gain * cosine.T, turn[:, None] * gain * sine.T],
                    [-gain * sine.T, turn[:, None] * gain * cosine.T],
                ]
            )
        )
    forward, inverse = np.stack(forward).astype(bf16), np.stack(inverse).astype(bf16)
    turn_cos, turn_sin = waves(np.arange(shots), np.arange(shots), shots)
    over_shots = np.block([[turn_cos, turn_sin], [-turn_sin, turn_cos]]).astype(bf16)
    back_rows = np.stack(
        [
            np.concatenate([turn_cos, -turn_sin], axis=1),
            np.concatenate([turn_sin, turn_cos], axis=1),
        ]
    ).astype(bf16)
    order = np.zeros((half, half), bf16)
    order[freqs, np.arange(half)] = 1
    return forward, inverse, over_shots, back_rows, order


def partner(index, away, count):
    if count & (count - 1) == 0:
        return index ^ away
    return (index + away) % count


def gather_kernel(aways, recs, *refs):
    ticks, places, *refs = refs
    share = ticks.shape[1]
    peers = len(aways)
    traces, refs = refs[:peers], refs[peers:]
    table_refs, out, loaded, refs = refs[:6], refs[6], refs[7:14], refs[14:]
    own, forward, inverse, order, flags, over_shots, back_rows = loaded
    tiles, folds, spectra, waved, mixed, ready, table_sem, out_sem = refs
    rec_rows, block_len = traces[0].shape
    shots, half = flags.shape
    window = 2 * half
    slots = ready.shape[0]
    pitch = recs + 1
    wide = window // LANES
    mid = wide // 2
    parts = range(mid)
    side = math.sqrt(0.5)
    per_block = block_len // LANES
    f32, bf16 = jnp.float32, jnp.bfloat16
    here = lax.axis_index("tm")

    table_copies = [
        pltpu.make_async_copy(table, place, table_sem.at[index])
        for index, (table, place) in enumerate(zip((traces[0], *table_refs), loaded))
    ]
    for index in (0, 6, 1, 4, 3, 5, 2):
        table_copies[index].start()

    table_copies[0].wait()
    for away, block in zip(aways, (own, *traces[1:])):
        base = partner(here, away, peers) * per_block
        for tile in range(per_block):
            tiles[base + tile] = block[:, tile * LANES : (tile + 1) * LANES]
    for tile in range(wide):
        tiles[peers * per_block + tile] = jnp.zeros((rec_rows, LANES), bf16)

    lane = lax.broadcasted_iota(jnp.int16, (recs, LANES), 1)

    def cut(shot, rows):
        tick = ticks[shot // share, shot % share]
        first = lax.shift_right_logical(tick, LANES.bit_length() - 1)
        within = tick & (LANES - 1)
        piece = [tiles[first + tile, rows] for tile in range(wide + 1)]
        early = lane < within.astype(jnp.int16)
        piece = [jnp.where(early, piece[tile + 1], piece[tile]) for tile in range(wide)]
        turn = (LANES - within) & (LANES - 1)
        sums = [piece[tile] + piece[tile + mid] for tile in range(mid)]
        gaps = [piece[tile] - piece[tile + mid] for tile in range(mid)]
        near = (gaps[1] - gaps[3]) * bf16(side)
        far = (gaps[1] + gaps[3]) * bf16(side)
        pairs = [
            (sums[0] + sums[2], sums[1] + sums[3]),
            (sums[0] - sums[2], sums[1] - sums[3]),
            (gaps[0] + near, gaps[2] + far),
            (gaps[0] - near, gaps[2] - far),
        ]
        return [[pltpu.roll(tile, turn, 1) for tile in pair] for pair in pairs]

    def cut_block(block, rows):
        for item in range(BLOCK):
            for part, pair in enumerate(cut(block * BLOCK + item, rows)):
                for side_of, tile in enumerate(pair):
                    folds[block % 2, part, side_of, item * recs : (item + 1) * recs] = tile

    def columns(tile):
        return slice(tile * LANES, (tile + 1) * LANES)

    def transform_block(block):
        for part in parts:
            panel = jnp.concatenate([folds[block % 2, part, side_of] for side_of in range(2)], axis=1)
            found = jnp.dot(panel, forward[part], preferred_element_type=f32)
            for item in range(BLOCK):
                row = (block * BLOCK + item) * pitch
                for side_of in range(2):
                    spectra[2 * part + side_of, row : row + recs] = found[
                        item * recs : (item + 1) * recs, columns(side_of)
                    ]

    def over(rec, keep):
        at = pl.ds(rec, shots, stride=pitch)
        stacked = jnp.concatenate(
            [
                jnp.concatenate([spectra[2 * part + side_of, at].astype(bf16) for part in parts], axis=1)
                for side_of in range(2)
            ],
            axis=0,
        )
        waves = jnp.dot(over_shots[...], stacked, preferred_element_type=f32)
        masked = jnp.concatenate([waves[:shots] * keep, waves[shots:] * keep], axis=0).astype(bf16)
        for part in parts:
            waved[part, rec] = masked[:, columns(part)]

    def under(rec, back):
        masked = jnp.concatenate([waved[part, rec] for part in parts], axis=1)
        again = jnp.dot(back, masked, preferred_element_type=f32)
        to = pl.ds(rec, slots, stride=pitch)
        for part in parts:
            mixed[2 * part, to] = again[:slots, columns(part)]
            mixed[2 * part + 1, to] = again[slots:, columns(part)]

    group = min(slots, 256 // recs)
    out_copies = []

    def restore(chunk, first):
        found = []
        for part in parts:
            panel = [
                jnp.concatenate(
                    [
                        mixed[2 * part + side_of, slot * pitch : slot * pitch + recs].astype(bf16)
                        for slot in range(first, first + group)
                    ],
                    axis=0,
                )
                for side_of in range(2)
            ]
            found.append(
                jnp.dot(
                    jnp.concatenate(panel, axis=1), inverse[part], preferred_element_type=f32
                )
            )
        plus, minus = found[0] + found[1], found[0] - found[1]
        even = [plus[:, :LANES], plus[:, LANES:], minus[:, :LANES], minus[:, LANES:]]
        total, gap = found[2] + found[3], found[2] - found[3]
        real_gap, imag_sum = gap[:, :LANES], total[:, LANES:]
        odd = [
            total[:, :LANES],
            (real_gap - imag_sum) * side,
            -gap[:, LANES:],
            (real_gap + imag_sum) * -side,
        ]
        rows = slice(chunk * recs, (chunk + 1) * recs)
        for tile in range(mid):
            for to, value in ((tile, even[tile] + odd[tile]), (tile + mid, even[tile] - odd[tile])):
                ready[first : first + group, rows, columns(to)] = value.astype(bf16).reshape(
                    group, recs, LANES
                )
        block = (pl.ds(first, group), pl.ds(chunk * recs, recs))
        copy = pltpu.make_async_copy(
            ready.at[block], out.at[block], out_sem.at[chunk, first // group]
        )
        copy.start()
        out_copies.append(copy)

    shot_lane = lax.broadcasted_iota(jnp.int32, (1, shots), 1)
    place_all = jnp.full((1, shots), -1, jnp.int32)
    for shot in range(shots):
        tick = ticks[shot // share, shot % share]
        mine = (tick >= here * block_len) & (tick < (here + 1) * block_len)
        place = jnp.where(mine, places[shot // share, shot % share], -1)
        place_all = jnp.where(shot_lane == shot, place, place_all)
    slot_row = lax.broadcasted_iota(jnp.int32, (slots, shots), 0)
    owned = (slot_row == place_all).astype(f32).astype(bf16)

    blocks = shots // BLOCK
    for chunk in range(rec_rows // recs):
        rows = slice(chunk * recs, (chunk + 1) * recs)
        cut_block(0, rows)
        if chunk == 0:
            table_copies[6].wait()
            back = jnp.concatenate(
                [jnp.dot(owned, back_rows[part], preferred_element_type=f32) for part in range(2)],
                axis=0,
            ).astype(bf16)
            table_copies[1].wait()
        for block in range(blocks):
            if block + 1 < blocks:
                cut_block(block + 1, rows)
            transform_block(block)
        if chunk == 0:
            for index in (3, 4, 5):
                table_copies[index].wait()
            keep = jnp.dot(
                flags[...].astype(f32).astype(bf16), order[...], preferred_element_type=f32
            )
        for rec in range(recs):
            over(rec, keep)
        for rec in range(recs):
            under(rec, back)
        if chunk == 0:
            table_copies[2].wait()
        for first in range(0, slots, group):
            restore(chunk, first)
    for copy in out_copies:
        copy.wait()


def filter_gathers(codes, traces, aways, flags, tables):
    forward, inverse, over_shots, back_rows, order = tables
    peers = len(traces)
    rec_rows, block_len = traces[0].shape
    shots, half = flags.shape
    window = 2 * half
    slots = 2 * shots // peers
    total = peers * block_len
    recs = rec_rows if shots * rec_rows * window <= 4 << 20 else BLOCK
    smem = pl.BlockSpec(memory_space=pltpu.SMEM)
    vmem = pl.BlockSpec(memory_space=pltpu.VMEM)
    hbm = pl.BlockSpec(memory_space=pltpu.HBM)
    flops = 2 * rec_rows * (
        shots * window * half
        + slots * window * half
        + 4 * shots * shots * half
        + 4 * slots * shots * half
    )
    bf16 = jnp.bfloat16
    shared = [forward, inverse, order, flags, over_shots, back_rows]
    return pl.pallas_call(
        functools.partial(gather_kernel, aways, recs),
        out_shape=jax.ShapeDtypeStruct((slots, rec_rows, window), bf16),
        in_specs=[smem, smem, hbm] + [vmem] * (peers - 1) + [hbm] * 6,
        out_specs=hbm,
        scratch_shapes=[
            pltpu.VMEM((rec_rows, block_len), bf16),
            *[pltpu.VMEM(table.shape, table.dtype) for table in shared],
            pltpu.VMEM(((total + window) // LANES, rec_rows, LANES), bf16),
            pltpu.VMEM((2, half // LANES, 2, BLOCK * recs, LANES), bf16),
            pltpu.VMEM((window // LANES, shots * (recs + 1), LANES), jnp.float32),
            pltpu.VMEM((half // LANES, recs, 2 * shots, LANES), bf16),
            pltpu.VMEM((window // LANES, slots * (recs + 1), LANES), jnp.float32),
            pltpu.VMEM((slots, rec_rows, window), bf16),
            pltpu.SemaphoreType.DMA((7,)),
            pltpu.SemaphoreType.DMA((rec_rows // recs, slots)),
        ],
        compiler_params=pltpu.CompilerParams(vmem_limit_bytes=60 << 20),
        cost_estimate=pl.CostEstimate(
            flops=flops,
            bytes_accessed=2 * rec_rows * (total + slots * window),
            transcendentals=0,
        ),
    )(*codes, *traces, *shared)


def on_device(station_traces, shot_onset_ticks, span_place_index, spectral_keep_flags):
    shots, half = spectral_keep_flags.shape
    tables = make_tables(2 * half, shots)
    peers = lax.axis_size("tm")
    lines = lax.axis_size("line")
    farthest = list(range(peers - 1, 0, -1))
    aways = [0, *farthest[1::-1], *farthest[2:]]
    traces = [station_traces] + [
        lax.ppermute(
            station_traces,
            "tm",
            [(partner(index, away, peers), index) for index in range(peers)],
        )
        for away in aways[1:]
    ]
    share = shots // lines
    row = lax.broadcasted_iota(jnp.int32, (lines, share), 0)
    own = row == lax.axis_index("line")
    codes = lax.psum(
        [jnp.where(own, part[None], 0) for part in (shot_onset_ticks, span_place_index)], "line"
    )
    return filter_gathers(codes, traces, aways, spectral_keep_flags, tables)


def solution(mesh):
    in_specs = (P("line", "tm"), P("line"), P("line"), P())
    out_specs = P("tm", "line", None)
    return jax.shard_map(
        on_device, mesh=mesh, in_specs=in_specs, out_specs=out_specs, check_vma=False
    )
```

```python
import functools
import math

import jax
import jax.numpy as jnp
import ml_dtypes
import numpy as np
from jax import lax
from jax.experimental import pallas as pl
from jax.experimental.pallas import tpu as pltpu
from jax.sharding import PartitionSpec as P

LANES = 128
BLOCK = 16


def make_tables(window, shots):
    half = window // 2
    quarter, eighth = window // 4, window // 8
    bf16 = ml_dtypes.bfloat16

    def waves(rows, columns, period):
        phase = (rows[:, None] * columns[None, :] % period) * (2.0 * math.pi / period)
        return np.cos(phase), np.sin(phase)

    classes = [np.arange(first, half, 4) for first in (0, 2)]
    classes += [
        np.concatenate([np.arange(first, half, 8) for first in pair]) for pair in ((1, 7), (3, 5))
    ]
    freqs = np.concatenate(classes)
    forward, inverse = [], []
    for part, found in enumerate(classes):
        gain = np.where(found == 0, 0.5, 1.0)[:, None] * (2.0 / (window * shots))
        if part < 2:
            cosine, sine = waves(np.arange(quarter), found, window)
            forward.append(np.concatenate([cosine, -sine], axis=1))
            inverse.append(np.concatenate([gain * cosine.T, -gain * sine.T], axis=0))
            continue
        cosine, sine = waves(np.arange(eighth), found, window)
        turn = np.where(found % 8 < 4, 1.0, -1.0)
        way = -turn if part == 2 else turn
        forward.append(np.block([[cosine, -sine], [way * sine, way * cosine]]))
        inverse.append(
            np.block(
                [
                    [gain * cosine.T, turn[:, None] * gain * sine.T],
                    [-gain * sine.T, turn[:, None] * gain * cosine.T],
                ]
            )
        )
    forward, inverse = np.stack(forward).astype(bf16), np.stack(inverse).astype(bf16)
    turn_cos, turn_sin = waves(np.arange(shots), np.arange(shots), shots)
    over_shots = np.block([[turn_cos, turn_sin], [-turn_sin, turn_cos]]).astype(bf16)
    back_rows = np.stack(
        [
            np.concatenate([turn_cos, -turn_sin], axis=1),
            np.concatenate([turn_sin, turn_cos], axis=1),
        ]
    ).astype(bf16)
    order = np.zeros((half, half), bf16)
    order[freqs, np.arange(half)] = 1
    return forward, inverse, over_shots, back_rows, order


def partner(index, away, count):
    if count & (count - 1) == 0:
        return index ^ away
    return (index + away) % count


def gather_kernel(aways, recs, *refs):
    codes, *refs = refs
    share = codes.shape[2]
    peers = len(aways)
    traces, refs = refs[:peers], refs[peers:]
    table_refs, out, loaded, refs = refs[:6], refs[6], refs[7:14], refs[14:]
    own, forward, inverse, order, flags, over_shots, back_rows = loaded
    tiles, folds, spectra, waved, mixed, ready, table_sem, out_sem = refs
    rec_rows, block_len = traces[0].shape
    shots, half = flags.shape
    window = 2 * half
    slots = ready.shape[0]
    pitch = recs + 1
    wide = window // LANES
    mid = wide // 2
    parts = range(mid)
    side = math.sqrt(0.5)
    per_block = block_len // LANES
    f32, bf16 = jnp.float32, jnp.bfloat16
    here = lax.axis_index("tm")

    table_copies = [
        pltpu.make_async_copy(table, place, table_sem.at[index])
        for index, (table, place) in enumerate(zip((traces[0], *table_refs), loaded))
    ]
    for index in (0, 6, 1, 4, 3, 5, 2):
        table_copies[index].start()

    for away, block in [*zip(aways[1:], traces[1:]), (0, own)]:
        if away == 0:
            table_copies[0].wait()
        base = partner(here, away, peers) * per_block
        for tile in range(per_block):
            tiles[base + tile] = block[:, tile * LANES : (tile + 1) * LANES]
    for tile in range(wide):
        tiles[peers * per_block + tile] = jnp.zeros((rec_rows, LANES), bf16)

    lane = lax.broadcasted_iota(jnp.int16, (recs, LANES), 1)

    def cut(shot, rows):
        tick = codes[0, shot // share, shot % share]
        first = lax.shift_right_logical(tick, LANES.bit_length() - 1)
        within = tick & (LANES - 1)
        piece = [tiles[first + tile, rows] for tile in range(wide + 1)]
        early = lane < within.astype(jnp.int16)
        piece = [jnp.where(early, piece[tile + 1], piece[tile]) for tile in range(wide)]
        turn = (LANES - within) & (LANES - 1)
        sums = [piece[tile] + piece[tile + mid] for tile in range(mid)]
        gaps = [piece[tile] - piece[tile + mid] for tile in range(mid)]
        near = (gaps[1] - gaps[3]) * bf16(side)
        far = (gaps[1] + gaps[3]) * bf16(side)
        pairs = [
            (sums[0] + sums[2], sums[1] + sums[3]),
            (sums[0] - sums[2], sums[1] - sums[3]),
            (gaps[0] + near, gaps[2] + far),
            (gaps[0] - near, gaps[2] - far),
        ]
        return [[pltpu.roll(tile, turn, 1) for tile in pair] for pair in pairs]

    def cut_block(block, rows):
        for item in range(BLOCK):
            for part, pair in enumerate(cut(block * BLOCK + item, rows)):
                for side_of, tile in enumerate(pair):
                    folds[block % 2, part, side_of, item * recs : (item + 1) * recs] = tile

    def columns(tile):
        return slice(tile * LANES, (tile + 1) * LANES)

    def transform_block(block):
        for part in parts:
            panel = jnp.concatenate([folds[block % 2, part, side_of] for side_of in range(2)], axis=1)
            found = jnp.dot(panel, forward[part], preferred_element_type=f32)
            for item in range(BLOCK):
                row = (block * BLOCK + item) * pitch
                for side_of in range(2):
                    spectra[2 * part + side_of, row : row + recs] = found[
                        item * recs : (item + 1) * recs, columns(side_of)
                    ]

    def over(rec, keep):
        at = pl.ds(rec, shots, stride=pitch)
        stacked = jnp.concatenate(
            [
                jnp.concatenate([spectra[2 * part + side_of, at].astype(bf16) for part in parts], axis=1)
                for side_of in range(2)
            ],
            axis=0,
        )
        waves = jnp.dot(over_shots[...], stacked, preferred_element_type=f32)
        masked = waves.astype(bf16) * keep
        for part in parts:
            waved[part, rec] = masked[:, columns(part)]

    def under(rec, back):
        masked = jnp.concatenate([waved[part, rec] for part in parts], axis=1)
        again = jnp.dot(back, masked, preferred_element_type=f32)
        to = pl.ds(rec, slots, stride=pitch)
        for part in parts:
            mixed[2 * part, to] = again[:slots, columns(part)]
            mixed[2 * part + 1, to] = again[slots:, columns(part)]

    group = min(slots, 256 // recs)
    out_copies = []

    def restore(chunk, first):
        found = []
        for part in parts:
            panel = [
                jnp.concatenate(
                    [
                        mixed[2 * part + side_of, slot * pitch : slot * pitch + recs].astype(bf16)
                        for slot in range(first, first + group)
                    ],
                    axis=0,
                )
                for side_of in range(2)
            ]
            found.append(
                jnp.dot(
                    jnp.concatenate(panel, axis=1), inverse[part], preferred_element_type=f32
                )
            )
        plus, minus = found[0] + found[1], found[0] - found[1]
        even = [plus[:, :LANES], plus[:, LANES:], minus[:, :LANES], minus[:, LANES:]]
        total, gap = found[2] + found[3], found[2] - found[3]
        real_gap, imag_sum = gap[:, :LANES], total[:, LANES:]
        odd = [
            total[:, :LANES],
            (real_gap - imag_sum) * side,
            -gap[:, LANES:],
            (real_gap + imag_sum) * -side,
        ]
        rows = slice(chunk * recs, (chunk + 1) * recs)
        for tile in range(mid):
            for to, value in ((tile, even[tile] + odd[tile]), (tile + mid, even[tile] - odd[tile])):
                ready[first : first + group, rows, columns(to)] = value.astype(bf16).reshape(
                    group, recs, LANES
                )
        block = (pl.ds(first, group), pl.ds(chunk * recs, recs))
        copy = pltpu.make_async_copy(
            ready.at[block], out.at[block], out_sem.at[chunk, first // group]
        )
        copy.start()
        out_copies.append(copy)

    shot_lane = lax.broadcasted_iota(jnp.int32, (1, shots), 1)
    place_all = jnp.full((1, shots), -1, jnp.int32)
    for shot in range(shots):
        tick = codes[0, shot // share, shot % share]
        mine = (tick >= here * block_len) & (tick < (here + 1) * block_len)
        place = jnp.where(mine, codes[1, shot // share, shot % share], -1)
        place_all = jnp.where(shot_lane == shot, place, place_all)
    slot_row = lax.broadcasted_iota(jnp.int32, (slots, shots), 0)
    owned = (slot_row == place_all).astype(f32).astype(bf16)

    blocks = shots // BLOCK
    for chunk in range(rec_rows // recs):
        rows = slice(chunk * recs, (chunk + 1) * recs)
        cut_block(0, rows)
        if chunk == 0:
            table_copies[6].wait()
            back = jnp.concatenate(
                [jnp.dot(owned, back_rows[part], preferred_element_type=f32) for part in range(2)],
                axis=0,
            ).astype(bf16)
            table_copies[1].wait()
        for block in range(blocks):
            if block + 1 < blocks:
                cut_block(block + 1, rows)
            transform_block(block)
            if chunk == 0 and block == 0:
                for index in (3, 4, 5):
                    table_copies[index].wait()
                kept = jnp.dot(
                    flags[...].astype(f32).astype(bf16), order[...], preferred_element_type=f32
                ).astype(bf16)
                keep = jnp.concatenate([kept, kept], axis=0)
        for rec in range(recs):
            over(rec, keep)
        for rec in range(recs):
            under(rec, back)
        if chunk == 0:
            table_copies[2].wait()
        for first in range(0, slots, group):
            restore(chunk, first)
    for copy in out_copies:
        copy.wait()


def filter_gathers(codes, traces, aways, flags, tables):
    forward, inverse, over_shots, back_rows, order = tables
    peers = len(traces)
    rec_rows, block_len = traces[0].shape
    shots, half = flags.shape
    window = 2 * half
    slots = 2 * shots // peers
    total = peers * block_len
    recs = rec_rows if shots * rec_rows * window <= 4 << 20 else BLOCK
    smem = pl.BlockSpec(memory_space=pltpu.SMEM)
    vmem = pl.BlockSpec(memory_space=pltpu.VMEM)
    hbm = pl.BlockSpec(memory_space=pltpu.HBM)
    flops = 2 * rec_rows * (
        shots * window * half
        + slots * window * half
        + 4 * shots * shots * half
        + 4 * slots * shots * half
    )
    bf16 = jnp.bfloat16
    shared = [forward, inverse, order, flags, over_shots, back_rows]
    return pl.pallas_call(
        functools.partial(gather_kernel, aways, recs),
        out_shape=jax.ShapeDtypeStruct((slots, rec_rows, window), bf16),
        in_specs=[smem, hbm] + [vmem] * (peers - 1) + [hbm] * 6,
        out_specs=hbm,
        scratch_shapes=[
            pltpu.VMEM((rec_rows, block_len), bf16),
            *[pltpu.VMEM(table.shape, table.dtype) for table in shared],
            pltpu.VMEM(((total + window) // LANES, rec_rows, LANES), bf16),
            pltpu.VMEM((2, half // LANES, 2, BLOCK * recs, LANES), bf16),
            pltpu.VMEM((window // LANES, shots * (recs + 1), LANES), jnp.float32),
            pltpu.VMEM((half // LANES, recs, 2 * shots, LANES), bf16),
            pltpu.VMEM((window // LANES, slots * (recs + 1), LANES), jnp.float32),
            pltpu.VMEM((slots, rec_rows, window), bf16),
            pltpu.SemaphoreType.DMA((7,)),
            pltpu.SemaphoreType.DMA((rec_rows // recs, slots)),
        ],
        compiler_params=pltpu.CompilerParams(vmem_limit_bytes=60 << 20),
        cost_estimate=pl.CostEstimate(
            flops=flops,
            bytes_accessed=2 * rec_rows * (total + slots * window),
            transcendentals=0,
        ),
    )(codes, *traces, *shared)


def on_device(station_traces, shot_onset_ticks, span_place_index, spectral_keep_flags):
    shots, half = spectral_keep_flags.shape
    tables = make_tables(2 * half, shots)
    peers = lax.axis_size("tm")
    lines = lax.axis_size("line")
    aways = list(range(peers))
    traces = [station_traces] + [
        lax.ppermute(
            station_traces,
            "tm",
            [(partner(index, away, peers), index) for index in range(peers)],
        )
        for away in aways[1:]
    ]
    shape = (2, lines, shots // lines)
    which = lax.broadcasted_iota(jnp.int32, shape, 0)
    line = lax.broadcasted_iota(jnp.int32, shape, 1)
    both = jnp.where(which == 0, shot_onset_ticks, span_place_index)
    codes = lax.psum(jnp.where(line == lax.axis_index("line"), both, 0), "line")
    return filter_gathers(codes, traces, aways, spectral_keep_flags, tables)


def solution(mesh):
    in_specs = (P("line", "tm"), P("line"), P("line"), P())
    out_specs = P("tm", "line", None)
    return jax.shard_map(
        on_device, mesh=mesh, in_specs=in_specs, out_specs=out_specs, check_vma=False
    )
```

```python
import functools
import math

import jax
import jax.numpy as jnp
import ml_dtypes
import numpy as np
from jax import lax
from jax.experimental import pallas as pl
from jax.experimental.pallas import tpu as pltpu
from jax.sharding import PartitionSpec as P

LANES = 128
BLOCK = 16


def make_tables(window, shots):
    half = window // 2
    quarter, eighth = window // 4, window // 8
    bf16 = ml_dtypes.bfloat16

    def waves(rows, columns, period):
        phase = (rows[:, None] * columns[None, :] % period) * (2.0 * math.pi / period)
        return np.cos(phase), np.sin(phase)

    classes = [np.arange(first, half, 4) for first in (0, 2)]
    classes += [
        np.concatenate([np.arange(first, half, 8) for first in pair]) for pair in ((1, 7), (3, 5))
    ]
    freqs = np.concatenate(classes)
    forward, inverse = [], []
    for part, found in enumerate(classes):
        gain = np.where(found == 0, 0.5, 1.0)[:, None] * (2.0 / (window * shots))
        if part < 2:
            cosine, sine = waves(np.arange(quarter), found, window)
            forward.append(np.concatenate([cosine, -sine], axis=1))
            inverse.append(np.concatenate([gain * cosine.T, -gain * sine.T], axis=0))
            continue
        cosine, sine = waves(np.arange(eighth), found, window)
        turn = np.where(found % 8 < 4, 1.0, -1.0)
        way = -turn if part == 2 else turn
        forward.append(np.block([[cosine, -sine], [way * sine, way * cosine]]))
        inverse.append(
            np.block(
                [
                    [gain * cosine.T, turn[:, None] * gain * sine.T],
                    [-gain * sine.T, turn[:, None] * gain * cosine.T],
                ]
            )
        )
    forward, inverse = np.stack(forward).astype(bf16), np.stack(inverse).astype(bf16)
    turn_cos, turn_sin = waves(np.arange(shots), np.arange(shots), shots)
    over_shots = np.block([[turn_cos, turn_sin], [-turn_sin, turn_cos]]).astype(bf16)
    back_rows = np.stack(
        [
            np.concatenate([turn_cos, -turn_sin], axis=1),
            np.concatenate([turn_sin, turn_cos], axis=1),
        ]
    ).astype(bf16)
    order = np.zeros((half, half), bf16)
    order[freqs, np.arange(half)] = 1
    return forward, inverse, over_shots, back_rows, order


def partner(index, away, count):
    if count & (count - 1) == 0:
        return index ^ away
    return (index + away) % count


def gather_kernel(aways, recs, *refs):
    codes_ref, *refs = refs
    peers = len(aways)
    traces, refs = refs[:peers], refs[peers:]
    table_refs, out, codes, records, loaded, refs = (
        refs[:6], refs[6], refs[7], refs[8], refs[9:15], refs[15:]
    )
    share = codes.shape[2]
    forward, inverse, order, flags, over_shots, back_rows = loaded
    tiles, folds, spectra, waved, mixed, ready, codes_sem, record_sem, table_sem, out_sem = refs
    rec_rows, block_len = traces[0].shape
    shots, half = flags.shape
    window = 2 * half
    slots = ready.shape[0]
    pitch = recs + 1
    wide = window // LANES
    mid = wide // 2
    parts = range(mid)
    side = math.sqrt(0.5)
    per_block = block_len // LANES
    f32, bf16 = jnp.float32, jnp.bfloat16
    here = lax.axis_index("tm")

    codes_copy = pltpu.make_async_copy(codes_ref, codes, codes_sem)
    record_copies = [
        pltpu.make_async_copy(block, records.at[index], record_sem.at[index])
        for index, block in enumerate(traces)
    ]
    table_copies = [
        pltpu.make_async_copy(table, place, table_sem.at[index])
        for index, (table, place) in enumerate(zip(table_refs, loaded))
    ]
    codes_copy.start()
    for copy in record_copies:
        copy.start()
    for index in (5, 0, 3, 2, 4, 1):
        table_copies[index].start()

    for index, away in enumerate(aways):
        record_copies[index].wait()
        base = partner(here, away, peers) * per_block
        for tile in range(per_block):
            tiles[base + tile] = records[index, :, tile * LANES : (tile + 1) * LANES]
    codes_copy.wait()
    for tile in range(wide):
        tiles[peers * per_block + tile] = jnp.zeros((rec_rows, LANES), bf16)

    lane = lax.broadcasted_iota(jnp.int16, (recs, LANES), 1)

    def cut(shot, rows):
        tick = codes[0, shot // share, shot % share]
        first = lax.shift_right_logical(tick, LANES.bit_length() - 1)
        within = tick & (LANES - 1)
        piece = [tiles[first + tile, rows] for tile in range(wide + 1)]
        early = lane < within.astype(jnp.int16)
        piece = [jnp.where(early, piece[tile + 1], piece[tile]) for tile in range(wide)]
        turn = (LANES - within) & (LANES - 1)
        sums = [piece[tile] + piece[tile + mid] for tile in range(mid)]
        gaps = [piece[tile] - piece[tile + mid] for tile in range(mid)]
        near = (gaps[1] - gaps[3]) * bf16(side)
        far = (gaps[1] + gaps[3]) * bf16(side)
        pairs = [
            (sums[0] + sums[2], sums[1] + sums[3]),
            (sums[0] - sums[2], sums[1] - sums[3]),
            (gaps[0] + near, gaps[2] + far),
            (gaps[0] - near, gaps[2] - far),
        ]
        return [[pltpu.roll(tile, turn, 1) for tile in pair] for pair in pairs]

    def cut_block(block, rows, items=range(BLOCK)):
        for item in items:
            for part, pair in enumerate(cut(block * BLOCK + item, rows)):
                for side_of, tile in enumerate(pair):
                    folds[block % 2, part, side_of, item * recs : (item + 1) * recs] = tile

    def columns(tile):
        return slice(tile * LANES, (tile + 1) * LANES)

    def transform_block(block, part):
        panel = jnp.concatenate([folds[block % 2, part, side_of] for side_of in range(2)], axis=1)
        found = jnp.dot(panel, forward[part], preferred_element_type=f32)
        for item in range(BLOCK):
            row = (block * BLOCK + item) * pitch
            for side_of in range(2):
                spectra[2 * part + side_of, row : row + recs] = found[
                    item * recs : (item + 1) * recs, columns(side_of)
                ]

    def over(rec, keep):
        at = pl.ds(rec, shots, stride=pitch)
        stacked = jnp.concatenate(
            [
                jnp.concatenate([spectra[2 * part + side_of, at].astype(bf16) for part in parts], axis=1)
                for side_of in range(2)
            ],
            axis=0,
        )
        waves = jnp.dot(over_shots[...], stacked, preferred_element_type=f32)
        masked = waves.astype(bf16) * keep
        for part in parts:
            waved[part, rec] = masked[:, columns(part)]

    def under(rec, back):
        masked = jnp.concatenate([waved[part, rec] for part in parts], axis=1)
        again = jnp.dot(back, masked, preferred_element_type=f32)
        to = pl.ds(rec, slots, stride=pitch)
        for part in parts:
            mixed[2 * part, to] = again[:slots, columns(part)]
            mixed[2 * part + 1, to] = again[slots:, columns(part)]

    group = min(slots, 256 // recs)
    out_copies = []

    def restore(chunk, first):
        found = []
        for part in parts:
            panel = [
                jnp.concatenate(
                    [
                        mixed[2 * part + side_of, slot * pitch : slot * pitch + recs].astype(bf16)
                        for slot in range(first, first + group)
                    ],
                    axis=0,
                )
                for side_of in range(2)
            ]
            found.append(
                jnp.dot(
                    jnp.concatenate(panel, axis=1), inverse[part], preferred_element_type=f32
                )
            )
        plus, minus = found[0] + found[1], found[0] - found[1]
        even = [plus[:, :LANES], plus[:, LANES:], minus[:, :LANES], minus[:, LANES:]]
        total, gap = found[2] + found[3], found[2] - found[3]
        real_gap, imag_sum = gap[:, :LANES], total[:, LANES:]
        odd = [
            total[:, :LANES],
            (real_gap - imag_sum) * side,
            -gap[:, LANES:],
            (real_gap + imag_sum) * -side,
        ]
        rows = slice(chunk * recs, (chunk + 1) * recs)
        for tile in range(mid):
            for to, value in ((tile, even[tile] + odd[tile]), (tile + mid, even[tile] - odd[tile])):
                ready[first : first + group, rows, columns(to)] = value.astype(bf16).reshape(
                    group, recs, LANES
                )
        block = (pl.ds(first, group), pl.ds(chunk * recs, recs))
        copy = pltpu.make_async_copy(
            ready.at[block], out.at[block], out_sem.at[chunk, first // group]
        )
        copy.start()
        out_copies.append(copy)

    shot_lane = lax.broadcasted_iota(jnp.int32, (1, shots), 1)
    place_all = jnp.full((1, shots), -1, jnp.int32)
    for shot in range(shots):
        tick = codes[0, shot // share, shot % share]
        mine = (tick >= here * block_len) & (tick < (here + 1) * block_len)
        place = jnp.where(mine, codes[1, shot // share, shot % share], -1)
        place_all = jnp.where(shot_lane == shot, place, place_all)
    slot_row = lax.broadcasted_iota(jnp.int32, (slots, shots), 0)
    owned = (slot_row == place_all).astype(f32).astype(bf16)

    blocks = shots // BLOCK
    for chunk in range(rec_rows // recs):
        rows = slice(chunk * recs, (chunk + 1) * recs)
        cut_block(0, rows)
        if chunk == 0:
            table_copies[5].wait()
            back = jnp.concatenate(
                [jnp.dot(owned, back_rows[part], preferred_element_type=f32) for part in range(2)],
                axis=0,
            ).astype(bf16)
            table_copies[0].wait()
        for block in range(blocks):
            for part in parts:
                transform_block(block, part)
                if block + 1 < blocks:
                    cut_block(block + 1, rows, range(part * BLOCK // mid, (part + 1) * BLOCK // mid))
            if chunk == 0 and block == 0:
                for index in (2, 3, 4):
                    table_copies[index].wait()
                kept = jnp.dot(
                    flags[...].astype(f32).astype(bf16), order[...], preferred_element_type=f32
                ).astype(bf16)
                keep = jnp.concatenate([kept, kept], axis=0)
        for rec in range(recs):
            over(rec, keep)
        for rec in range(recs):
            under(rec, back)
        if chunk == 0:
            table_copies[1].wait()
        for first in range(0, slots, group):
            restore(chunk, first)
    for copy in out_copies:
        copy.wait()


def filter_gathers(codes, traces, aways, flags, tables):
    forward, inverse, over_shots, back_rows, order = tables
    peers = len(traces)
    rec_rows, block_len = traces[0].shape
    shots, half = flags.shape
    window = 2 * half
    slots = 2 * shots // peers
    total = peers * block_len
    recs = rec_rows if shots * rec_rows * window <= 4 << 20 else BLOCK
    hbm = pl.BlockSpec(memory_space=pltpu.HBM)
    flops = 2 * rec_rows * (
        shots * window * half
        + slots * window * half
        + 4 * shots * shots * half
        + 4 * slots * shots * half
    )
    bf16 = jnp.bfloat16
    shared = [forward, inverse, order, flags, over_shots, back_rows]
    return pl.pallas_call(
        functools.partial(gather_kernel, aways, recs),
        out_shape=jax.ShapeDtypeStruct((slots, rec_rows, window), bf16),
        in_specs=[hbm] * (1 + peers + len(shared)),
        out_specs=hbm,
        scratch_shapes=[
            pltpu.SMEM(codes.shape, jnp.int32),
            pltpu.VMEM((peers, rec_rows, block_len), bf16),
            *[pltpu.VMEM(table.shape, table.dtype) for table in shared],
            pltpu.VMEM(((total + window) // LANES, rec_rows, LANES), bf16),
            pltpu.VMEM((2, half // LANES, 2, BLOCK * recs, LANES), bf16),
            pltpu.VMEM((window // LANES, shots * (recs + 1), LANES), jnp.float32),
            pltpu.VMEM((half // LANES, recs, 2 * shots, LANES), bf16),
            pltpu.VMEM((window // LANES, slots * (recs + 1), LANES), jnp.float32),
            pltpu.VMEM((slots, rec_rows, window), bf16),
            pltpu.SemaphoreType.DMA,
            pltpu.SemaphoreType.DMA((peers,)),
            pltpu.SemaphoreType.DMA((len(shared),)),
            pltpu.SemaphoreType.DMA((rec_rows // recs, slots)),
        ],
        compiler_params=pltpu.CompilerParams(vmem_limit_bytes=60 << 20),
        cost_estimate=pl.CostEstimate(
            flops=flops,
            bytes_accessed=2 * rec_rows * (total + slots * window),
            transcendentals=0,
        ),
    )(codes, *traces, *shared)


def on_device(station_traces, shot_onset_ticks, span_place_index, spectral_keep_flags):
    shots, half = spectral_keep_flags.shape
    tables = make_tables(2 * half, shots)
    peers = lax.axis_size("tm")
    lines = lax.axis_size("line")
    aways = list(range(peers))
    traces = [station_traces] + [
        lax.ppermute(
            station_traces,
            "tm",
            [(partner(index, away, peers), index) for index in range(peers)],
        )
        for away in aways[1:]
    ]
    shape = (2, lines, shots // lines)
    which = lax.broadcasted_iota(jnp.int32, shape, 0)
    line = lax.broadcasted_iota(jnp.int32, shape, 1)
    both = jnp.where(which == 0, shot_onset_ticks, span_place_index)
    codes = lax.psum(jnp.where(line == lax.axis_index("line"), both, 0), "line")
    return filter_gathers(codes, traces, aways, spectral_keep_flags, tables)


def solution(mesh):
    in_specs = (P("line", "tm"), P("line"), P("line"), P())
    out_specs = P("tm", "line", None)
    return jax.shard_map(
        on_device, mesh=mesh, in_specs=in_specs, out_specs=out_specs, check_vma=False
    )
```

```python
import functools
import math

import jax
import jax.numpy as jnp
import ml_dtypes
import numpy as np
from jax import lax
from jax.experimental import pallas as pl
from jax.experimental.pallas import tpu as pltpu
from jax.sharding import PartitionSpec as P

LANES = 128
BLOCK = 16


def make_tables(window, shots):
    half = window // 2
    quarter, eighth = window // 4, window // 8
    bf16 = ml_dtypes.bfloat16

    def waves(rows, columns, period):
        phase = (rows[:, None] * columns[None, :] % period) * (2.0 * math.pi / period)
        return np.cos(phase), np.sin(phase)

    classes = [np.arange(first, half, 4) for first in (0, 2)]
    classes += [
        np.concatenate([np.arange(first, half, 8) for first in pair]) for pair in ((1, 7), (3, 5))
    ]
    freqs = np.concatenate(classes)
    forward, inverse = [], []
    for part, found in enumerate(classes):
        gain = np.where(found == 0, 0.5, 1.0)[:, None] * (2.0 / (window * shots))
        if part < 2:
            cosine, sine = waves(np.arange(quarter), found, window)
            forward.append(np.concatenate([cosine, -sine], axis=1))
            inverse.append(np.concatenate([gain * cosine.T, -gain * sine.T], axis=0))
            continue
        cosine, sine = waves(np.arange(eighth), found, window)
        turn = np.where(found % 8 < 4, 1.0, -1.0)
        way = -turn if part == 2 else turn
        forward.append(np.block([[cosine, -sine], [way * sine, way * cosine]]))
        inverse.append(
            np.block(
                [
                    [gain * cosine.T, turn[:, None] * gain * sine.T],
                    [-gain * sine.T, turn[:, None] * gain * cosine.T],
                ]
            )
        )
    forward, inverse = np.stack(forward).astype(bf16), np.stack(inverse).astype(bf16)
    turn_cos, turn_sin = waves(np.arange(shots), np.arange(shots), shots)
    over_shots = np.block([[turn_cos, turn_sin], [-turn_sin, turn_cos]]).astype(bf16)
    back_rows = np.stack(
        [
            np.concatenate([turn_cos, -turn_sin], axis=1),
            np.concatenate([turn_sin, turn_cos], axis=1),
        ]
    ).astype(bf16)
    order = np.zeros((half, half), bf16)
    order[freqs, np.arange(half)] = 1
    return forward, inverse, over_shots, back_rows, order


def partner(index, away, count):
    if count & (count - 1) == 0:
        return index ^ away
    return (index + away) % count


def gather_kernel(aways, recs, *refs):
    codes_ref, *refs = refs
    peers = len(aways)
    traces, refs = refs[:peers], refs[peers:]
    table_refs, out, codes, records, loaded, refs = (
        refs[:6], refs[6], refs[7], refs[8], refs[9:15], refs[15:]
    )
    share = codes.shape[2]
    forward, inverse, order, flags, over_shots, back_rows = loaded
    tiles, folds, spectra, waved, mixed, ready, codes_sem, record_sem, table_sem, out_sem = refs
    rec_rows, block_len = traces[0].shape
    shots, half = flags.shape
    window = 2 * half
    slots = ready.shape[0]
    pitch = recs + 1
    wide = window // LANES
    mid = wide // 2
    parts = range(mid)
    side = math.sqrt(0.5)
    per_block = block_len // LANES
    f32, bf16 = jnp.float32, jnp.bfloat16
    here = lax.axis_index("tm")

    codes_copy = pltpu.make_async_copy(codes_ref, codes, codes_sem)
    record_copies = [
        pltpu.make_async_copy(block, records.at[index], record_sem.at[index])
        for index, block in enumerate(traces)
    ]
    table_copies = [
        pltpu.make_async_copy(table, place, table_sem.at[index])
        for index, (table, place) in enumerate(zip(table_refs, loaded))
    ]
    codes_copy.start()
    for copy in record_copies:
        copy.start()
    for index in (5, 0, 3, 2, 4, 1):
        table_copies[index].start()

    for index, away in enumerate(aways):
        record_copies[index].wait()
        base = partner(here, away, peers) * per_block
        for tile in range(per_block):
            tiles[base + tile] = records[index, :, tile * LANES : (tile + 1) * LANES]
    codes_copy.wait()
    for tile in range(wide):
        tiles[peers * per_block + tile] = jnp.zeros((rec_rows, LANES), bf16)

    lane = lax.broadcasted_iota(jnp.int16, (recs, LANES), 1)

    def cut(shot, rows):
        tick = codes[0, shot // share, shot % share]
        first = lax.shift_right_logical(tick, LANES.bit_length() - 1)
        within = tick & (LANES - 1)
        piece = [tiles[first + tile, rows] for tile in range(wide + 1)]
        early = lane < within.astype(jnp.int16)
        piece = [jnp.where(early, piece[tile + 1], piece[tile]) for tile in range(wide)]
        turn = (LANES - within) & (LANES - 1)
        sums = [piece[tile] + piece[tile + mid] for tile in range(mid)]
        gaps = [piece[tile] - piece[tile + mid] for tile in range(mid)]
        near = (gaps[1] - gaps[3]) * bf16(side)
        far = (gaps[1] + gaps[3]) * bf16(side)
        pairs = [
            (sums[0] + sums[2], sums[1] + sums[3]),
            (sums[0] - sums[2], sums[1] - sums[3]),
            (gaps[0] + near, gaps[2] + far),
            (gaps[0] - near, gaps[2] - far),
        ]
        return [[pltpu.roll(tile, turn, 1) for tile in pair] for pair in pairs]

    def cut_block(block, rows, items=range(BLOCK)):
        for item in items:
            for part, pair in enumerate(cut(block * BLOCK + item, rows)):
                for side_of, tile in enumerate(pair):
                    folds[block % 2, part, side_of, item * recs : (item + 1) * recs] = tile

    def columns(tile):
        return slice(tile * LANES, (tile + 1) * LANES)

    def transform_block(block, part):
        panel = jnp.concatenate([folds[block % 2, part, side_of] for side_of in range(2)], axis=1)
        found = jnp.dot(panel, forward[part], preferred_element_type=f32)
        for item in range(BLOCK):
            row = (block * BLOCK + item) * pitch
            for side_of in range(2):
                spectra[2 * part + side_of, row : row + recs] = found[
                    item * recs : (item + 1) * recs, columns(side_of)
                ]

    def over(rec, keep):
        at = pl.ds(rec, shots, stride=pitch)
        stacked = jnp.concatenate(
            [
                jnp.concatenate([spectra[2 * part + side_of, at].astype(bf16) for part in parts], axis=1)
                for side_of in range(2)
            ],
            axis=0,
        )
        waves = jnp.dot(over_shots[...], stacked, preferred_element_type=f32)
        masked = waves.astype(bf16) * keep
        for part in parts:
            waved[part, rec] = masked[:, columns(part)]

    def under(rec, back):
        masked = jnp.concatenate([waved[part, rec] for part in parts], axis=1)
        again = jnp.dot(back, masked, preferred_element_type=f32)
        to = pl.ds(rec, slots, stride=pitch)
        for part in parts:
            mixed[2 * part, to] = again[:slots, columns(part)]
            mixed[2 * part + 1, to] = again[slots:, columns(part)]

    group = min(slots, 256 // recs)
    out_copies = []

    def restore(chunk, first):
        found = []
        for part in parts:
            panel = [
                jnp.concatenate(
                    [
                        mixed[2 * part + side_of, slot * pitch : slot * pitch + recs].astype(bf16)
                        for slot in range(first, first + group)
                    ],
                    axis=0,
                )
                for side_of in range(2)
            ]
            found.append(
                jnp.dot(
                    jnp.concatenate(panel, axis=1), inverse[part], preferred_element_type=f32
                )
            )
        plus, minus = found[0] + found[1], found[0] - found[1]
        even = [plus[:, :LANES], plus[:, LANES:], minus[:, :LANES], minus[:, LANES:]]
        total, gap = found[2] + found[3], found[2] - found[3]
        real_gap, imag_sum = gap[:, :LANES], total[:, LANES:]
        odd = [
            total[:, :LANES],
            (real_gap - imag_sum) * side,
            -gap[:, LANES:],
            (real_gap + imag_sum) * -side,
        ]
        rows = slice(chunk * recs, (chunk + 1) * recs)
        for tile in range(mid):
            for to, value in ((tile, even[tile] + odd[tile]), (tile + mid, even[tile] - odd[tile])):
                ready[first : first + group, rows, columns(to)] = value.astype(bf16).reshape(
                    group, recs, LANES
                )
        block = (pl.ds(first, group), pl.ds(chunk * recs, recs))
        copy = pltpu.make_async_copy(
            ready.at[block], out.at[block], out_sem.at[chunk, first // group]
        )
        copy.start()
        out_copies.append(copy)

    shot_lane = lax.broadcasted_iota(jnp.int32, (1, shots), 1)
    place_all = jnp.full((1, shots), -1, jnp.int32)
    for shot in range(shots):
        tick = codes[0, shot // share, shot % share]
        mine = (tick >= here * block_len) & (tick < (here + 1) * block_len)
        place = jnp.where(mine, codes[1, shot // share, shot % share], -1)
        place_all = jnp.where(shot_lane == shot, place, place_all)
    slot_row = lax.broadcasted_iota(jnp.int32, (slots, shots), 0)
    owned = (slot_row == place_all).astype(f32).astype(bf16)

    blocks = shots // BLOCK
    for chunk in range(rec_rows // recs):
        rows = slice(chunk * recs, (chunk + 1) * recs)
        cut_block(0, rows)
        if chunk == 0:
            table_copies[5].wait()
            back = jnp.concatenate(
                [jnp.dot(owned, back_rows[part], preferred_element_type=f32) for part in range(2)],
                axis=0,
            ).astype(bf16)
            table_copies[0].wait()
        for block in range(blocks):
            for part in parts:
                transform_block(block, part)
                if block + 1 < blocks:
                    cut_block(block + 1, rows, range(part * BLOCK // mid, (part + 1) * BLOCK // mid))
            if chunk == 0 and block == 0:
                for index in (2, 3, 4):
                    table_copies[index].wait()
                kept = jnp.dot(
                    flags[...].astype(f32).astype(bf16), order[...], preferred_element_type=f32
                ).astype(bf16)
                keep = jnp.concatenate([kept, kept], axis=0)
        lag = recs // 2
        for rec in range(recs + lag):
            if rec < recs:
                over(rec, keep)
            if rec >= lag:
                under(rec - lag, back)
        if chunk == 0:
            table_copies[1].wait()
        for first in range(0, slots, group):
            restore(chunk, first)
    for copy in out_copies:
        copy.wait()


def filter_gathers(codes, traces, aways, flags, tables):
    forward, inverse, over_shots, back_rows, order = tables
    peers = len(traces)
    rec_rows, block_len = traces[0].shape
    shots, half = flags.shape
    window = 2 * half
    slots = 2 * shots // peers
    total = peers * block_len
    recs = rec_rows if shots * rec_rows * window <= 4 << 20 else BLOCK
    hbm = pl.BlockSpec(memory_space=pltpu.HBM)
    flops = 2 * rec_rows * (
        shots * window * half
        + slots * window * half
        + 4 * shots * shots * half
        + 4 * slots * shots * half
    )
    bf16 = jnp.bfloat16
    shared = [forward, inverse, order, flags, over_shots, back_rows]
    return pl.pallas_call(
        functools.partial(gather_kernel, aways, recs),
        out_shape=jax.ShapeDtypeStruct((slots, rec_rows, window), bf16),
        in_specs=[hbm] * (1 + peers + len(shared)),
        out_specs=hbm,
        scratch_shapes=[
            pltpu.SMEM(codes.shape, jnp.int32),
            pltpu.VMEM((peers, rec_rows, block_len), bf16),
            *[pltpu.VMEM(table.shape, table.dtype) for table in shared],
            pltpu.VMEM(((total + window) // LANES, rec_rows, LANES), bf16),
            pltpu.VMEM((2, half // LANES, 2, BLOCK * recs, LANES), bf16),
            pltpu.VMEM((window // LANES, shots * (recs + 1), LANES), jnp.float32),
            pltpu.VMEM((half // LANES, recs, 2 * shots, LANES), bf16),
            pltpu.VMEM((window // LANES, slots * (recs + 1), LANES), jnp.float32),
            pltpu.VMEM((slots, rec_rows, window), bf16),
            pltpu.SemaphoreType.DMA,
            pltpu.SemaphoreType.DMA((peers,)),
            pltpu.SemaphoreType.DMA((len(shared),)),
            pltpu.SemaphoreType.DMA((rec_rows // recs, slots)),
        ],
        compiler_params=pltpu.CompilerParams(vmem_limit_bytes=60 << 20),
        cost_estimate=pl.CostEstimate(
            flops=flops,
            bytes_accessed=2 * rec_rows * (total + slots * window),
            transcendentals=0,
        ),
    )(codes, *traces, *shared)


def on_device(station_traces, shot_onset_ticks, span_place_index, spectral_keep_flags):
    shots, half = spectral_keep_flags.shape
    tables = make_tables(2 * half, shots)
    peers = lax.axis_size("tm")
    lines = lax.axis_size("line")
    aways = list(range(peers))
    traces = [station_traces] + [
        lax.ppermute(
            station_traces,
            "tm",
            [(partner(index, away, peers), index) for index in range(peers)],
        )
        for away in aways[1:]
    ]
    shape = (2, lines, shots // lines)
    which = lax.broadcasted_iota(jnp.int32, shape, 0)
    line = lax.broadcasted_iota(jnp.int32, shape, 1)
    both = jnp.where(which == 0, shot_onset_ticks, span_place_index)
    codes = lax.psum(jnp.where(line == lax.axis_index("line"), both, 0), "line")
    return filter_gathers(codes, traces, aways, spectral_keep_flags, tables)


def solution(mesh):
    in_specs = (P("line", "tm"), P("line"), P("line"), P())
    out_specs = P("tm", "line", None)
    return jax.shard_map(
        on_device, mesh=mesh, in_specs=in_specs, out_specs=out_specs, check_vma=False
    )
```

```python
import functools
import math

import jax
import jax.numpy as jnp
import ml_dtypes
import numpy as np
from jax import lax
from jax.experimental import pallas as pl
from jax.experimental.pallas import tpu as pltpu
from jax.sharding import PartitionSpec as P

LANES = 128
BLOCK = 16


def make_tables(window, shots):
    half = window // 2
    quarter, eighth = window // 4, window // 8
    bf16 = ml_dtypes.bfloat16

    def waves(rows, columns, period):
        phase = (rows[:, None] * columns[None, :] % period) * (2.0 * math.pi / period)
        return np.cos(phase), np.sin(phase)

    classes = [np.arange(first, half, 4) for first in (0, 2)]
    classes += [
        np.concatenate([np.arange(first, half, 8) for first in pair]) for pair in ((1, 7), (3, 5))
    ]
    freqs = np.concatenate(classes)
    forward, inverse = [], []
    for part, found in enumerate(classes):
        gain = np.where(found == 0, 0.5, 1.0)[:, None] * (2.0 / (window * shots))
        if part < 2:
            cosine, sine = waves(np.arange(quarter), found, window)
            forward.append(np.concatenate([cosine, -sine], axis=1))
            inverse.append(np.concatenate([gain * cosine.T, -gain * sine.T], axis=0))
            continue
        cosine, sine = waves(np.arange(eighth), found, window)
        turn = np.where(found % 8 < 4, 1.0, -1.0)
        way = -turn if part == 2 else turn
        forward.append(np.block([[cosine, -sine], [way * sine, way * cosine]]))
        inverse.append(
            np.block(
                [
                    [gain * cosine.T, turn[:, None] * gain * sine.T],
                    [-gain * sine.T, turn[:, None] * gain * cosine.T],
                ]
            )
        )
    forward, inverse = np.stack(forward).astype(bf16), np.stack(inverse).astype(bf16)
    turn_cos, turn_sin = waves(np.arange(shots), np.arange(shots), shots)
    over_shots = np.block([[turn_cos, turn_sin], [-turn_sin, turn_cos]]).astype(bf16)
    back_rows = np.stack(
        [
            np.concatenate([turn_cos, -turn_sin], axis=1),
            np.concatenate([turn_sin, turn_cos], axis=1),
        ]
    ).astype(bf16)
    order = np.zeros((half, half), bf16)
    order[freqs, np.arange(half)] = 1
    return forward, inverse, over_shots, back_rows, order


def partner(index, away, count):
    if count & (count - 1) == 0:
        return index ^ away
    return (index + away) % count


def gather_kernel(aways, recs, *refs):
    codes_ref, *refs = refs
    peers = len(aways)
    traces, refs = refs[:peers], refs[peers:]
    table_refs, out, codes, records, loaded, refs = (
        refs[:6], refs[6], refs[7], refs[8], refs[9:15], refs[15:]
    )
    share = codes.shape[2]
    forward, inverse, order, flags, over_shots, back_rows = loaded
    tiles, folds, spectra, waved, mixed, ready, codes_sem, record_sem, table_sem, out_sem = refs
    rec_rows, block_len = traces[0].shape
    shots, half = flags.shape
    window = 2 * half
    slots = ready.shape[0]
    pitch = recs + 1
    wide = window // LANES
    mid = wide // 2
    parts = range(mid)
    side = math.sqrt(0.5)
    per_block = block_len // LANES
    f32, bf16 = jnp.float32, jnp.bfloat16
    here = lax.axis_index("tm")

    codes_copy = pltpu.make_async_copy(codes_ref, codes, codes_sem)
    record_copies = [
        pltpu.make_async_copy(block, records.at[index], record_sem.at[index])
        for index, block in enumerate(traces)
    ]
    table_copies = [
        pltpu.make_async_copy(table, place, table_sem.at[index])
        for index, (table, place) in enumerate(zip(table_refs, loaded))
    ]
    codes_copy.start()
    table_copies[5].start()
    for copy in record_copies:
        copy.start()
    for index in (0, 3, 2, 4, 1):
        table_copies[index].start()

    codes_copy.wait()
    shot_lane = lax.broadcasted_iota(jnp.int32, (1, shots), 1)
    place_all = jnp.full((1, shots), -1, jnp.int32)
    for shot in range(shots):
        tick = codes[0, shot // share, shot % share]
        mine = (tick >= here * block_len) & (tick < (here + 1) * block_len)
        place = jnp.where(mine, codes[1, shot // share, shot % share], -1)
        place_all = jnp.where(shot_lane == shot, place, place_all)
    slot_row = lax.broadcasted_iota(jnp.int32, (slots, shots), 0)
    owned = (slot_row == place_all).astype(f32).astype(bf16)

    table_copies[5].wait()
    back = jnp.concatenate(
        [jnp.dot(owned, back_rows[part], preferred_element_type=f32) for part in range(2)], axis=0
    ).astype(bf16)

    for index, away in enumerate(aways):
        record_copies[index].wait()
        base = partner(here, away, peers) * per_block
        for tile in range(per_block):
            tiles[base + tile] = records[index, :, tile * LANES : (tile + 1) * LANES]
    for tile in range(wide):
        tiles[peers * per_block + tile] = jnp.zeros((rec_rows, LANES), bf16)

    lane = lax.broadcasted_iota(jnp.int16, (recs, LANES), 1)

    def cut(shot, rows):
        tick = codes[0, shot // share, shot % share]
        first = lax.shift_right_logical(tick, LANES.bit_length() - 1)
        within = tick & (LANES - 1)
        piece = [tiles[first + tile, rows] for tile in range(wide + 1)]
        early = lane < within.astype(jnp.int16)
        piece = [jnp.where(early, piece[tile + 1], piece[tile]) for tile in range(wide)]
        turn = (LANES - within) & (LANES - 1)
        sums = [piece[tile] + piece[tile + mid] for tile in range(mid)]
        gaps = [piece[tile] - piece[tile + mid] for tile in range(mid)]
        near = (gaps[1] - gaps[3]) * bf16(side)
        far = (gaps[1] + gaps[3]) * bf16(side)
        pairs = [
            (sums[0] + sums[2], sums[1] + sums[3]),
            (sums[0] - sums[2], sums[1] - sums[3]),
            (gaps[0] + near, gaps[2] + far),
            (gaps[0] - near, gaps[2] - far),
        ]
        return [[pltpu.roll(tile, turn, 1) for tile in pair] for pair in pairs]

    def cut_block(block, rows, items=range(BLOCK)):
        for item in items:
            for part, pair in enumerate(cut(block * BLOCK + item, rows)):
                for side_of, tile in enumerate(pair):
                    folds[block % 2, part, side_of, item * recs : (item + 1) * recs] = tile

    def columns(tile):
        return slice(tile * LANES, (tile + 1) * LANES)

    def transform_block(block, part):
        panel = jnp.concatenate([folds[block % 2, part, side_of] for side_of in range(2)], axis=1)
        found = jnp.dot(panel, forward[part], preferred_element_type=f32)
        for item in range(BLOCK):
            row = (block * BLOCK + item) * pitch
            for side_of in range(2):
                spectra[2 * part + side_of, row : row + recs] = found[
                    item * recs : (item + 1) * recs, columns(side_of)
                ]

    def over(rec, keep):
        at = pl.ds(rec, shots, stride=pitch)
        stacked = jnp.concatenate(
            [
                jnp.concatenate([spectra[2 * part + side_of, at].astype(bf16) for part in parts], axis=1)
                for side_of in range(2)
            ],
            axis=0,
        )
        waves = jnp.dot(over_shots[...], stacked, preferred_element_type=f32)
        masked = waves.astype(bf16) * keep
        for part in parts:
            waved[part, rec] = masked[:, columns(part)]

    def under(rec, back):
        masked = jnp.concatenate([waved[part, rec] for part in parts], axis=1)
        again = jnp.dot(back, masked, preferred_element_type=f32)
        to = pl.ds(rec, slots, stride=pitch)
        for part in parts:
            mixed[2 * part, to] = again[:slots, columns(part)]
            mixed[2 * part + 1, to] = again[slots:, columns(part)]

    group = BLOCK
    out_copies = []

    def restore(chunk, start, first):
        found = []
        for part in parts:
            panel = [
                jnp.concatenate(
                    [
                        mixed[2 * part + side_of, slot * pitch + start : slot * pitch + start + BLOCK]
                        for slot in range(first, first + group)
                    ],
                    axis=0,
                ).astype(bf16)
                for side_of in range(2)
            ]
            found.append(
                jnp.dot(
                    jnp.concatenate(panel, axis=1), inverse[part], preferred_element_type=f32
                )
            )
        plus, minus = found[0] + found[1], found[0] - found[1]
        even = [plus[:, :LANES], plus[:, LANES:], minus[:, :LANES], minus[:, LANES:]]
        total, gap = found[2] + found[3], found[2] - found[3]
        real_gap, imag_sum = gap[:, :LANES], total[:, LANES:]
        odd = [
            total[:, :LANES],
            (real_gap - imag_sum) * side,
            -gap[:, LANES:],
            (real_gap + imag_sum) * -side,
        ]
        base = chunk * recs + start
        rows = slice(base, base + BLOCK)
        for tile in range(mid):
            for to, value in ((tile, even[tile] + odd[tile]), (tile + mid, even[tile] - odd[tile])):
                ready[first : first + group, rows, columns(to)] = value.astype(bf16).reshape(
                    group, BLOCK, LANES
                )
        block = (pl.ds(first, group), pl.ds(base, BLOCK))
        copy = pltpu.make_async_copy(
            ready.at[block], out.at[block], out_sem.at[base // BLOCK, first // group]
        )
        copy.start()
        out_copies.append(copy)

    blocks = shots // BLOCK
    for chunk in range(rec_rows // recs):
        rows = slice(chunk * recs, (chunk + 1) * recs)
        cut_block(0, rows)
        if chunk == 0:
            table_copies[0].wait()
        for block in range(blocks):
            for part in parts:
                transform_block(block, part)
                if block + 1 < blocks:
                    cut_block(block + 1, rows, range(part * BLOCK // mid, (part + 1) * BLOCK // mid))
            if chunk == 0 and block == 0:
                for index in (2, 3, 4):
                    table_copies[index].wait()
                kept = jnp.dot(
                    flags[...].astype(f32).astype(bf16), order[...], preferred_element_type=f32
                ).astype(bf16)
                keep = jnp.concatenate([kept, kept], axis=0)
        if chunk == 0:
            table_copies[1].wait()
        lag = recs // 2
        wanted = [(start, first) for start in range(0, recs, BLOCK) for first in range(0, slots, group)]
        for rec in range(recs + lag):
            if rec < recs:
                over(rec, keep)
            done = rec - lag
            if done >= 0:
                under(done, back)
                if wanted[0][0] + BLOCK + 4 <= done and done % 5 == 0:
                    restore(chunk, *wanted.pop(0))
        for start, first in wanted:
            restore(chunk, start, first)
    for copy in out_copies:
        copy.wait()


def filter_gathers(codes, traces, aways, flags, tables):
    forward, inverse, over_shots, back_rows, order = tables
    peers = len(traces)
    rec_rows, block_len = traces[0].shape
    shots, half = flags.shape
    window = 2 * half
    slots = 2 * shots // peers
    total = peers * block_len
    recs = rec_rows if shots * rec_rows * window <= 4 << 20 else BLOCK
    hbm = pl.BlockSpec(memory_space=pltpu.HBM)
    flops = 2 * rec_rows * (
        shots * window * half
        + slots * window * half
        + 4 * shots * shots * half
        + 4 * slots * shots * half
    )
    bf16 = jnp.bfloat16
    shared = [forward, inverse, order, flags, over_shots, back_rows]
    return pl.pallas_call(
        functools.partial(gather_kernel, aways, recs),
        out_shape=jax.ShapeDtypeStruct((slots, rec_rows, window), bf16),
        in_specs=[hbm] * (1 + peers + len(shared)),
        out_specs=hbm,
        scratch_shapes=[
            pltpu.SMEM(codes.shape, jnp.int32),
            pltpu.VMEM((peers, rec_rows, block_len), bf16),
            *[pltpu.VMEM(table.shape, table.dtype) for table in shared],
            pltpu.VMEM(((total + window) // LANES, rec_rows, LANES), bf16),
            pltpu.VMEM((2, half // LANES, 2, BLOCK * recs, LANES), bf16),
            pltpu.VMEM((window // LANES, shots * (recs + 1), LANES), jnp.float32),
            pltpu.VMEM((half // LANES, recs, 2 * shots, LANES), bf16),
            pltpu.VMEM((window // LANES, slots * (recs + 1), LANES), jnp.float32),
            pltpu.VMEM((slots, rec_rows, window), bf16),
            pltpu.SemaphoreType.DMA,
            pltpu.SemaphoreType.DMA((peers,)),
            pltpu.SemaphoreType.DMA((len(shared),)),
            pltpu.SemaphoreType.DMA((rec_rows // BLOCK, slots // BLOCK)),
        ],
        compiler_params=pltpu.CompilerParams(vmem_limit_bytes=60 << 20),
        cost_estimate=pl.CostEstimate(
            flops=flops,
            bytes_accessed=2 * rec_rows * (total + slots * window),
            transcendentals=0,
        ),
    )(codes, *traces, *shared)


def on_device(station_traces, shot_onset_ticks, span_place_index, spectral_keep_flags):
    shots, half = spectral_keep_flags.shape
    tables = make_tables(2 * half, shots)
    peers = lax.axis_size("tm")
    lines = lax.axis_size("line")
    aways = list(range(peers))
    traces = [station_traces] + [
        lax.ppermute(
            station_traces,
            "tm",
            [(partner(index, away, peers), index) for index in range(peers)],
        )
        for away in aways[1:]
    ]
    shape = (2, lines, shots // lines)
    which = lax.broadcasted_iota(jnp.int32, shape, 0)
    line = lax.broadcasted_iota(jnp.int32, shape, 1)
    both = jnp.where(which == 0, shot_onset_ticks, span_place_index)
    codes = lax.psum(jnp.where(line == lax.axis_index("line"), both, 0), "line")
    return filter_gathers(codes, traces, aways, spectral_keep_flags, tables)


def solution(mesh):
    in_specs = (P("line", "tm"), P("line"), P("line"), P())
    out_specs = P("tm", "line", None)
    return jax.shard_map(
        on_device, mesh=mesh, in_specs=in_specs, out_specs=out_specs, check_vma=False
    )
```

```python
import functools
import math

import jax
import jax.numpy as jnp
import ml_dtypes
import numpy as np
from jax import lax
from jax.experimental import pallas as pl
from jax.experimental.pallas import tpu as pltpu
from jax.sharding import PartitionSpec as P

LANES = 128
BLOCK = 16


def make_tables(window, shots):
    half = window // 2
    quarter, eighth = window // 4, window // 8
    bf16 = ml_dtypes.bfloat16

    def waves(rows, columns, period):
        phase = (rows[:, None] * columns[None, :] % period) * (2.0 * math.pi / period)
        return np.cos(phase), np.sin(phase)

    classes = [np.arange(first, half, 4) for first in (0, 2)]
    classes += [
        np.concatenate([np.arange(first, half, 8) for first in pair]) for pair in ((1, 7), (3, 5))
    ]
    freqs = np.concatenate(classes)
    forward, inverse = [], []
    for part, found in enumerate(classes):
        gain = np.where(found == 0, 0.5, 1.0)[:, None] * (2.0 / (window * shots))
        if part < 2:
            cosine, sine = waves(np.arange(quarter), found, window)
            forward.append(np.concatenate([cosine, -sine], axis=1))
            inverse.append(np.concatenate([gain * cosine.T, -gain * sine.T], axis=0))
            continue
        cosine, sine = waves(np.arange(eighth), found, window)
        turn = np.where(found % 8 < 4, 1.0, -1.0)
        way = -turn if part == 2 else turn
        forward.append(np.block([[cosine, -sine], [way * sine, way * cosine]]))
        inverse.append(
            np.block(
                [
                    [gain * cosine.T, turn[:, None] * gain * sine.T],
                    [-gain * sine.T, turn[:, None] * gain * cosine.T],
                ]
            )
        )
    forward, inverse = np.stack(forward).astype(bf16), np.stack(inverse).astype(bf16)
    turn_cos, turn_sin = waves(np.arange(shots), np.arange(shots), shots)
    over_shots = np.block([[turn_cos, turn_sin], [-turn_sin, turn_cos]]).astype(bf16)
    back_rows = np.stack(
        [
            np.concatenate([turn_cos, -turn_sin], axis=1),
            np.concatenate([turn_sin, turn_cos], axis=1),
        ]
    ).astype(bf16)
    order = np.zeros((half, half), bf16)
    order[freqs, np.arange(half)] = 1
    return forward, inverse, over_shots, back_rows, order


def partner(index, away, count):
    if count & (count - 1) == 0:
        return index ^ away
    return (index + away) % count


def gather_kernel(aways, recs, *refs):
    codes_ref, *refs = refs
    peers = len(aways)
    traces, refs = refs[:peers], refs[peers:]
    table_refs, out, codes, records, loaded, refs = (
        refs[:6], refs[6], refs[7], refs[8], refs[9:15], refs[15:]
    )
    share = codes.shape[2]
    forward, inverse, order, flags, over_shots, back_rows = loaded
    tiles, folds, spectra, waved, mixed, ready, codes_sem, record_sem, table_sem, out_sem = refs
    rec_rows, block_len = traces[0].shape
    shots, half = flags.shape
    window = 2 * half
    slots = ready.shape[0]
    pitch = recs + 1
    wide = window // LANES
    mid = wide // 2
    parts = range(mid)
    side = math.sqrt(0.5)
    per_block = block_len // LANES
    f32, bf16 = jnp.float32, jnp.bfloat16
    here = lax.axis_index("tm")

    codes_copy = pltpu.make_async_copy(codes_ref, codes, codes_sem)
    record_copies = [
        pltpu.make_async_copy(block, records.at[index], record_sem.at[index])
        for index, block in enumerate(traces)
    ]
    table_copies = [
        pltpu.make_async_copy(table, place, table_sem.at[index])
        for index, (table, place) in enumerate(zip(table_refs, loaded))
    ]
    codes_copy.start()
    table_copies[5].start()
    for copy in record_copies:
        copy.start()
    for index in (0, 3, 2, 4, 1):
        table_copies[index].start()

    codes_copy.wait()
    shot_lane = lax.broadcasted_iota(jnp.int32, (1, shots), 1)
    place_all = jnp.full((1, shots), -1, jnp.int32)
    for shot in range(shots):
        tick = codes[0, shot // share, shot % share]
        mine = (tick >= here * block_len) & (tick < (here + 1) * block_len)
        place = jnp.where(mine, codes[1, shot // share, shot % share], -1)
        place_all = jnp.where(shot_lane == shot, place, place_all)
    slot_row = lax.broadcasted_iota(jnp.int32, (slots, shots), 0)
    owned = (slot_row == place_all).astype(f32).astype(bf16)

    table_copies[5].wait()
    back = jnp.concatenate(
        [jnp.dot(owned, back_rows[part], preferred_element_type=f32) for part in range(2)], axis=0
    ).astype(bf16)

    for index, away in enumerate(aways):
        record_copies[index].wait()
        base = partner(here, away, peers) * per_block
        for tile in range(per_block):
            tiles[base + tile] = records[index, :, tile * LANES : (tile + 1) * LANES]
    for tile in range(wide):
        tiles[peers * per_block + tile] = jnp.zeros((rec_rows, LANES), bf16)

    lane = lax.broadcasted_iota(jnp.int16, (recs, LANES), 1)

    def cut(shot, rows):
        tick = codes[0, shot // share, shot % share]
        first = lax.shift_right_logical(tick, LANES.bit_length() - 1)
        within = tick & (LANES - 1)
        piece = [tiles[first + tile, rows] for tile in range(wide + 1)]
        early = lane < within.astype(jnp.int16)
        piece = [jnp.where(early, piece[tile + 1], piece[tile]) for tile in range(wide)]
        turn = (LANES - within) & (LANES - 1)
        sums = [piece[tile] + piece[tile + mid] for tile in range(mid)]
        gaps = [piece[tile] - piece[tile + mid] for tile in range(mid)]
        near = (gaps[1] - gaps[3]) * bf16(side)
        far = (gaps[1] + gaps[3]) * bf16(side)
        pairs = [
            (sums[0] + sums[2], sums[1] + sums[3]),
            (sums[0] - sums[2], sums[1] - sums[3]),
            (gaps[0] + near, gaps[2] + far),
            (gaps[0] - near, gaps[2] - far),
        ]
        return [[pltpu.roll(tile, turn, 1) for tile in pair] for pair in pairs]

    def cut_block(block, rows, items=range(BLOCK)):
        for item in items:
            for part, pair in enumerate(cut(block * BLOCK + item, rows)):
                for side_of, tile in enumerate(pair):
                    folds[block % 2, part, side_of, item * recs : (item + 1) * recs] = tile

    def columns(tile):
        return slice(tile * LANES, (tile + 1) * LANES)

    def transform_block(block, part):
        panel = jnp.concatenate([folds[block % 2, part, side_of] for side_of in range(2)], axis=1)
        found = jnp.dot(panel, forward[part], preferred_element_type=f32)
        for item in range(BLOCK):
            row = (block * BLOCK + item) * pitch
            for side_of in range(2):
                spectra[2 * part + side_of, row : row + recs] = found[
                    item * recs : (item + 1) * recs, columns(side_of)
                ]

    def over(rec, keep):
        at = pl.ds(rec, shots, stride=pitch)
        stacked = jnp.concatenate(
            [
                jnp.concatenate([spectra[2 * part + side_of, at].astype(bf16) for part in parts], axis=1)
                for side_of in range(2)
            ],
            axis=0,
        )
        waves = jnp.dot(over_shots[...], stacked, preferred_element_type=f32)
        masked = waves.astype(bf16) * keep
        for part in parts:
            waved[part, rec] = masked[:, columns(part)]

    def under(rec, back):
        masked = jnp.concatenate([waved[part, rec] for part in parts], axis=1)
        again = jnp.dot(back, masked, preferred_element_type=f32)
        to = pl.ds(rec, slots, stride=pitch)
        for part in parts:
            mixed[2 * part, to] = again[:slots, columns(part)]
            mixed[2 * part + 1, to] = again[slots:, columns(part)]

    group = BLOCK
    out_copies = []

    def restore(chunk, start, first):
        found = []
        for part in parts:
            panel = [
                jnp.concatenate(
                    [
                        mixed[2 * part + side_of, slot * pitch + start : slot * pitch + start + BLOCK]
                        for slot in range(first, first + group)
                    ],
                    axis=0,
                ).astype(bf16)
                for side_of in range(2)
            ]
            found.append(
                jnp.dot(
                    jnp.concatenate(panel, axis=1), inverse[part], preferred_element_type=f32
                )
            )
        plus, minus = found[0] + found[1], found[0] - found[1]
        even = [plus[:, :LANES], plus[:, LANES:], minus[:, :LANES], minus[:, LANES:]]
        total, gap = found[2] + found[3], found[2] - found[3]
        real_gap, imag_sum = gap[:, :LANES], total[:, LANES:]
        odd = [
            total[:, :LANES],
            (real_gap - imag_sum) * side,
            -gap[:, LANES:],
            (real_gap + imag_sum) * -side,
        ]
        base = chunk * recs + start
        rows = slice(base, base + BLOCK)
        for tile in range(mid):
            for to, value in ((tile, even[tile] + odd[tile]), (tile + mid, even[tile] - odd[tile])):
                ready[first : first + group, rows, columns(to)] = value.astype(bf16).reshape(
                    group, BLOCK, LANES
                )
        block = (pl.ds(first, group), pl.ds(base, BLOCK))
        copy = pltpu.make_async_copy(
            ready.at[block], out.at[block], out_sem.at[base // BLOCK, first // group]
        )
        copy.start()
        out_copies.append(copy)

    blocks = shots // BLOCK
    for chunk in range(rec_rows // recs):
        rows = slice(chunk * recs, (chunk + 1) * recs)
        cut_block(0, rows)
        if chunk == 0:
            table_copies[0].wait()
        for block in range(blocks):
            for part in parts:
                transform_block(block, part)
                if block + 1 < blocks:
                    cut_block(block + 1, rows, range(part * BLOCK // mid, (part + 1) * BLOCK // mid))
            if chunk == 0 and block == 0:
                for index in (2, 3, 4):
                    table_copies[index].wait()
                kept = jnp.dot(
                    flags[...].astype(f32).astype(bf16), order[...], preferred_element_type=f32
                ).astype(bf16)
                keep = jnp.concatenate([kept, kept], axis=0)
        if chunk == 0:
            table_copies[1].wait()
        lag = recs // 2
        wanted = [(start, first) for start in range(0, recs, BLOCK) for first in range(0, slots, group)]
        for rec in range(recs + lag):
            if rec < recs:
                over(rec, keep)
            done = rec - lag
            if done >= 0:
                under(done, back)
                if wanted[0][0] + BLOCK + 4 <= done and done % 5 == 0:
                    restore(chunk, *wanted.pop(0))
        for start, first in wanted:
            restore(chunk, start, first)
    for copy in out_copies:
        copy.wait()


def filter_gathers(codes, traces, aways, flags, tables):
    forward, inverse, over_shots, back_rows, order = tables
    peers = len(traces)
    rec_rows, block_len = traces[0].shape
    shots, half = flags.shape
    window = 2 * half
    slots = 2 * shots // peers
    total = peers * block_len
    recs = rec_rows if shots * rec_rows * window <= 4 << 20 else BLOCK
    hbm = pl.BlockSpec(memory_space=pltpu.HBM)
    flops = 2 * rec_rows * (
        shots * window * half
        + slots * window * half
        + 4 * shots * shots * half
        + 4 * slots * shots * half
    )
    bf16 = jnp.bfloat16
    shared = [forward, inverse, order, flags, over_shots, back_rows]
    return pl.pallas_call(
        functools.partial(gather_kernel, aways, recs),
        out_shape=jax.ShapeDtypeStruct((slots, rec_rows, window), bf16),
        in_specs=[hbm] * (1 + peers + len(shared)),
        out_specs=hbm,
        scratch_shapes=[
            pltpu.SMEM(codes.shape, jnp.int32),
            pltpu.VMEM((peers, rec_rows, block_len), bf16),
            *[pltpu.VMEM(table.shape, table.dtype) for table in shared],
            pltpu.VMEM(((total + window) // LANES, rec_rows, LANES), bf16),
            pltpu.VMEM((2, half // LANES, 2, BLOCK * recs, LANES), bf16),
            pltpu.VMEM((window // LANES, shots * (recs + 1), LANES), jnp.float32),
            pltpu.VMEM((half // LANES, recs, 2 * shots, LANES), bf16),
            pltpu.VMEM((window // LANES, slots * (recs + 1), LANES), jnp.float32),
            pltpu.VMEM((slots, rec_rows, window), bf16),
            pltpu.SemaphoreType.DMA,
            pltpu.SemaphoreType.DMA((peers,)),
            pltpu.SemaphoreType.DMA((len(shared),)),
            pltpu.SemaphoreType.DMA((rec_rows // BLOCK, slots // BLOCK)),
        ],
        compiler_params=pltpu.CompilerParams(vmem_limit_bytes=60 << 20),
        cost_estimate=pl.CostEstimate(
            flops=flops,
            bytes_accessed=2 * rec_rows * (total + slots * window),
            transcendentals=0,
        ),
    )(codes, *traces, *shared)


def on_device(station_traces, shot_onset_ticks, span_place_index, spectral_keep_flags):
    shots, half = spectral_keep_flags.shape
    tables = make_tables(2 * half, shots)
    peers = lax.axis_size("tm")
    lines = lax.axis_size("line")
    aways = [0, *range(2, peers)[:1], 1, *range(3, peers)]
    traces = [station_traces] + [
        lax.ppermute(
            station_traces,
            "tm",
            [(partner(index, away, peers), index) for index in range(peers)],
        )
        for away in aways[1:]
    ]
    shape = (2, lines, shots // lines)
    which = lax.broadcasted_iota(jnp.int32, shape, 0)
    line = lax.broadcasted_iota(jnp.int32, shape, 1)
    both = jnp.where(which == 0, shot_onset_ticks, span_place_index)
    codes = lax.psum(jnp.where(line == lax.axis_index("line"), both, 0), "line")
    return filter_gathers(codes, traces, aways, spectral_keep_flags, tables)


def solution(mesh):
    in_specs = (P("line", "tm"), P("line"), P("line"), P())
    out_specs = P("tm", "line", None)
    return jax.shard_map(
        on_device, mesh=mesh, in_specs=in_specs, out_specs=out_specs, check_vma=False
    )
```

```python
import functools
import math

import jax
import jax.numpy as jnp
import ml_dtypes
import numpy as np
from jax import lax
from jax.experimental import pallas as pl
from jax.experimental.pallas import tpu as pltpu
from jax.sharding import PartitionSpec as P

LANES = 128
BLOCK = 16


def make_tables(window, shots):
    half = window // 2
    quarter, eighth = window // 4, window // 8
    bf16 = ml_dtypes.bfloat16

    def waves(rows, columns, period):
        phase = (rows[:, None] * columns[None, :] % period) * (2.0 * math.pi / period)
        return np.cos(phase), np.sin(phase)

    classes = [np.arange(first, half, 4) for first in (0, 2)]
    classes += [
        np.concatenate([np.arange(first, half, 8) for first in pair]) for pair in ((1, 7), (3, 5))
    ]
    freqs = np.concatenate(classes)
    forward, inverse = [], []
    for part, found in enumerate(classes):
        gain = np.where(found == 0, 0.5, 1.0)[:, None] * (2.0 / (window * shots))
        if part < 2:
            cosine, sine = waves(np.arange(quarter), found, window)
            forward.append(np.concatenate([cosine, -sine], axis=1))
            inverse.append(np.concatenate([gain * cosine.T, -gain * sine.T], axis=0))
            continue
        cosine, sine = waves(np.arange(eighth), found, window)
        turn = np.where(found % 8 < 4, 1.0, -1.0)
        way = -turn if part == 2 else turn
        forward.append(np.block([[cosine, -sine], [way * sine, way * cosine]]))
        inverse.append(
            np.block(
                [
                    [gain * cosine.T, turn[:, None] * gain * sine.T],
                    [-gain * sine.T, turn[:, None] * gain * cosine.T],
                ]
            )
        )
    forward, inverse = np.stack(forward).astype(bf16), np.stack(inverse).astype(bf16)
    turn_cos, turn_sin = waves(np.arange(shots), np.arange(shots), shots)
    over_shots = np.block([[turn_cos, turn_sin], [-turn_sin, turn_cos]]).astype(bf16)
    back_rows = np.stack(
        [
            np.concatenate([turn_cos, -turn_sin], axis=1),
            np.concatenate([turn_sin, turn_cos], axis=1),
        ]
    ).astype(bf16)
    order = np.zeros((half, half), bf16)
    order[freqs, np.arange(half)] = 1
    return forward, inverse, over_shots, back_rows, order


def partner(index, away, count):
    if count & (count - 1) == 0:
        return index ^ away
    return (index + away) % count


def gather_kernel(aways, recs, *refs):
    codes_ref, *refs = refs
    peers = len(aways)
    traces, refs = refs[:peers], refs[peers:]
    table_refs, out, codes, records, loaded, refs = (
        refs[:6], refs[6], refs[7], refs[8], refs[9:15], refs[15:]
    )
    share = codes.shape[2]
    forward, inverse, order, flags, over_shots, back_rows = loaded
    tiles, folds, spectra, waved, mixed, ready, codes_sem, record_sem, table_sem, out_sem = refs
    rec_rows, block_len = traces[0].shape
    shots, half = flags.shape
    window = 2 * half
    slots = ready.shape[0]
    pitch = recs + 1
    wide = window // LANES
    mid = wide // 2
    parts = range(mid)
    side = math.sqrt(0.5)
    per_block = block_len // LANES
    f32, bf16 = jnp.float32, jnp.bfloat16
    here = lax.axis_index("tm")

    codes_copy = pltpu.make_async_copy(codes_ref, codes, codes_sem)
    record_copies = [
        pltpu.make_async_copy(block, records.at[index], record_sem.at[index])
        for index, block in enumerate(traces)
    ]
    table_copies = [
        pltpu.make_async_copy(table, place, table_sem.at[index])
        for index, (table, place) in enumerate(zip(table_refs, loaded))
    ]
    codes_copy.start()
    table_copies[5].start()
    for copy in record_copies:
        copy.start()
    for index in (0, 3, 2, 4, 1):
        table_copies[index].start()

    codes_copy.wait()
    shot_lane = lax.broadcasted_iota(jnp.int32, (1, shots), 1)
    place_all = jnp.full((1, shots), -1, jnp.int32)
    for shot in range(shots):
        tick = codes[0, shot // share, shot % share]
        mine = (tick >= here * block_len) & (tick < (here + 1) * block_len)
        place = jnp.where(mine, codes[1, shot // share, shot % share], -1)
        place_all = jnp.where(shot_lane == shot, place, place_all)
    slot_row = lax.broadcasted_iota(jnp.int32, (slots, shots), 0)
    owned = (slot_row == place_all).astype(f32).astype(bf16)

    table_copies[5].wait()
    back = jnp.concatenate(
        [jnp.dot(owned, back_rows[part], preferred_element_type=f32) for part in range(2)], axis=0
    ).astype(bf16)

    for index, away in enumerate(aways):
        record_copies[index].wait()
        base = partner(here, away, peers) * per_block
        for tile in range(per_block):
            tiles[base + tile] = records[index, :, tile * LANES : (tile + 1) * LANES]
    for tile in range(wide):
        tiles[peers * per_block + tile] = jnp.zeros((rec_rows, LANES), bf16)

    lane = lax.broadcasted_iota(jnp.int16, (recs, LANES), 1)

    def cut(shot, rows):
        tick = codes[0, shot // share, shot % share]
        first = lax.shift_right_logical(tick, LANES.bit_length() - 1)
        within = tick & (LANES - 1)
        piece = [tiles[first + tile, rows] for tile in range(wide + 1)]
        early = lane < within.astype(jnp.int16)
        piece = [jnp.where(early, piece[tile + 1], piece[tile]) for tile in range(wide)]
        turn = (LANES - within) & (LANES - 1)
        sums = [piece[tile] + piece[tile + mid] for tile in range(mid)]
        gaps = [piece[tile] - piece[tile + mid] for tile in range(mid)]
        near = (gaps[1] - gaps[3]) * bf16(side)
        far = (gaps[1] + gaps[3]) * bf16(side)
        pairs = [
            (sums[0] + sums[2], sums[1] + sums[3]),
            (sums[0] - sums[2], sums[1] - sums[3]),
            (gaps[0] + near, gaps[2] + far),
            (gaps[0] - near, gaps[2] - far),
        ]
        return [[pltpu.roll(tile, turn, 1) for tile in pair] for pair in pairs]

    def cut_block(block, rows, items=range(BLOCK)):
        for item in items:
            for part, pair in enumerate(cut(block * BLOCK + item, rows)):
                for side_of, tile in enumerate(pair):
                    folds[block % 2, part, side_of, item * recs : (item + 1) * recs] = tile

    def columns(tile):
        return slice(tile * LANES, (tile + 1) * LANES)

    def transform_block(block, part, items):
        at = slice(items[0] * recs, (items[-1] + 1) * recs)
        panel = jnp.concatenate([folds[block % 2, part, side_of, at] for side_of in range(2)], axis=1)
        found = jnp.dot(panel, forward[part], preferred_element_type=f32)
        for place, item in enumerate(items):
            row = (block * BLOCK + item) * pitch
            for side_of in range(2):
                spectra[2 * part + side_of, row : row + recs] = found[
                    place * recs : (place + 1) * recs, columns(side_of)
                ]

    def over(rec, keep):
        at = pl.ds(rec, shots, stride=pitch)
        stacked = jnp.concatenate(
            [
                jnp.concatenate([spectra[2 * part + side_of, at].astype(bf16) for part in parts], axis=1)
                for side_of in range(2)
            ],
            axis=0,
        )
        waves = jnp.dot(over_shots[...], stacked, preferred_element_type=f32)
        masked = waves.astype(bf16) * keep
        for part in parts:
            waved[part, rec] = masked[:, columns(part)]

    def under(rec, back):
        masked = jnp.concatenate([waved[part, rec] for part in parts], axis=1)
        again = jnp.dot(back, masked, preferred_element_type=f32)
        to = pl.ds(rec, slots, stride=pitch)
        for part in parts:
            mixed[2 * part, to] = again[:slots, columns(part)]
            mixed[2 * part + 1, to] = again[slots:, columns(part)]

    group = BLOCK
    out_copies = []

    def restore(chunk, start, first):
        found = []
        for part in parts:
            panel = [
                jnp.concatenate(
                    [
                        mixed[2 * part + side_of, slot * pitch + start : slot * pitch + start + BLOCK]
                        for slot in range(first, first + group)
                    ],
                    axis=0,
                ).astype(bf16)
                for side_of in range(2)
            ]
            found.append(
                jnp.dot(
                    jnp.concatenate(panel, axis=1), inverse[part], preferred_element_type=f32
                )
            )
        plus, minus = found[0] + found[1], found[0] - found[1]
        even = [plus[:, :LANES], plus[:, LANES:], minus[:, :LANES], minus[:, LANES:]]
        total, gap = found[2] + found[3], found[2] - found[3]
        real_gap, imag_sum = gap[:, :LANES], total[:, LANES:]
        odd = [
            total[:, :LANES],
            (real_gap - imag_sum) * side,
            -gap[:, LANES:],
            (real_gap + imag_sum) * -side,
        ]
        base = chunk * recs + start
        rows = slice(base, base + BLOCK)
        for tile in range(mid):
            for to, value in ((tile, even[tile] + odd[tile]), (tile + mid, even[tile] - odd[tile])):
                ready[first : first + group, rows, columns(to)] = value.astype(bf16).reshape(
                    group, BLOCK, LANES
                )
        block = (pl.ds(first, group), pl.ds(base, BLOCK))
        copy = pltpu.make_async_copy(
            ready.at[block], out.at[block], out_sem.at[base // BLOCK, first // group]
        )
        copy.start()
        out_copies.append(copy)

    blocks = shots // BLOCK
    for chunk in range(rec_rows // recs):
        rows = slice(chunk * recs, (chunk + 1) * recs)
        cut_block(0, rows)
        if chunk == 0:
            table_copies[0].wait()
        for block in range(blocks):
            for turn, (part, start) in enumerate((p, q) for p in parts for q in (0, BLOCK // 2)):
                transform_block(block, part, range(start, start + BLOCK // 2))
                if block + 1 < blocks:
                    cut_block(block + 1, rows, range(2 * turn, 2 * turn + 2))
            if chunk == 0 and block == 0:
                for index in (2, 3, 4):
                    table_copies[index].wait()
                kept = jnp.dot(
                    flags[...].astype(f32).astype(bf16), order[...], preferred_element_type=f32
                ).astype(bf16)
                keep = jnp.concatenate([kept, kept], axis=0)
        if chunk == 0:
            table_copies[1].wait()
        lag = recs // 2
        wanted = [(start, first) for start in range(0, recs, BLOCK) for first in range(0, slots, group)]
        for rec in range(recs + lag):
            if rec < recs:
                over(rec, keep)
            done = rec - lag
            if done >= 0:
                under(done, back)
                if wanted[0][0] + BLOCK + 4 <= done and done % 5 == 0:
                    restore(chunk, *wanted.pop(0))
        for start, first in wanted:
            restore(chunk, start, first)
    for copy in out_copies:
        copy.wait()


def filter_gathers(codes, traces, aways, flags, tables):
    forward, inverse, over_shots, back_rows, order = tables
    peers = len(traces)
    rec_rows, block_len = traces[0].shape
    shots, half = flags.shape
    window = 2 * half
    slots = 2 * shots // peers
    total = peers * block_len
    recs = rec_rows if shots * rec_rows * window <= 4 << 20 else BLOCK
    hbm = pl.BlockSpec(memory_space=pltpu.HBM)
    flops = 2 * rec_rows * (
        shots * window * half
        + slots * window * half
        + 4 * shots * shots * half
        + 4 * slots * shots * half
    )
    bf16 = jnp.bfloat16
    shared = [forward, inverse, order, flags, over_shots, back_rows]
    return pl.pallas_call(
        functools.partial(gather_kernel, aways, recs),
        out_shape=jax.ShapeDtypeStruct((slots, rec_rows, window), bf16),
        in_specs=[hbm] * (1 + peers + len(shared)),
        out_specs=hbm,
        scratch_shapes=[
            pltpu.SMEM(codes.shape, jnp.int32),
            pltpu.VMEM((peers, rec_rows, block_len), bf16),
            *[pltpu.VMEM(table.shape, table.dtype) for table in shared],
            pltpu.VMEM(((total + window) // LANES, rec_rows, LANES), bf16),
            pltpu.VMEM((2, half // LANES, 2, BLOCK * recs, LANES), bf16),
            pltpu.VMEM((window // LANES, shots * (recs + 1), LANES), jnp.float32),
            pltpu.VMEM((half // LANES, recs, 2 * shots, LANES), bf16),
            pltpu.VMEM((window // LANES, slots * (recs + 1), LANES), jnp.float32),
            pltpu.VMEM((slots, rec_rows, window), bf16),
            pltpu.SemaphoreType.DMA,
            pltpu.SemaphoreType.DMA((peers,)),
            pltpu.SemaphoreType.DMA((len(shared),)),
            pltpu.SemaphoreType.DMA((rec_rows // BLOCK, slots // BLOCK)),
        ],
        compiler_params=pltpu.CompilerParams(vmem_limit_bytes=60 << 20),
        cost_estimate=pl.CostEstimate(
            flops=flops,
            bytes_accessed=2 * rec_rows * (total + slots * window),
            transcendentals=0,
        ),
    )(codes, *traces, *shared)


def on_device(station_traces, shot_onset_ticks, span_place_index, spectral_keep_flags):
    shots, half = spectral_keep_flags.shape
    tables = make_tables(2 * half, shots)
    peers = lax.axis_size("tm")
    lines = lax.axis_size("line")
    aways = list(range(peers))
    traces = [station_traces] + [
        lax.ppermute(
            station_traces,
            "tm",
            [(partner(index, away, peers), index) for index in range(peers)],
        )
        for away in aways[1:]
    ]
    shape = (2, lines, shots // lines)
    which = lax.broadcasted_iota(jnp.int32, shape, 0)
    line = lax.broadcasted_iota(jnp.int32, shape, 1)
    both = jnp.where(which == 0, shot_onset_ticks, span_place_index)
    codes = lax.psum(jnp.where(line == lax.axis_index("line"), both, 0), "line")
    return filter_gathers(codes, traces, aways, spectral_keep_flags, tables)


def solution(mesh):
    in_specs = (P("line", "tm"), P("line"), P("line"), P())
    out_specs = P("tm", "line", None)
    return jax.shard_map(
        on_device, mesh=mesh, in_specs=in_specs, out_specs=out_specs, check_vma=False
    )
```
